32 devices in a mesh: dp: 8 (over y, x, core), tensor: 4 (over z).
Axes of the slice: x: 2, y: 2, z: 4, core: 2. Of those that a mesh axis runs over, the one named last changes fastest.
Arguments:
- attn_out: bfloat16 [4096, 8192], P('dp', 'tensor'), may hold values from -6 to 6
- out_weight: bfloat16 [8192, 3584], P('tensor', 'dp'), may hold values from -0.0625 to 0.0625
- residual: bfloat16 [4096, 3584], P(('dp', 'tensor')), may hold values from -101 to 101
- norm_gain: float32 [3584], replicated, may hold values from 0.5 to 1.5
- expert_ids: int32 [4096, 8], P(('dp', 'tensor')), may hold values from 0 to 31, all different within a row; in each aligned block of 128 rows (0 to 127, 128 to 255, ...) at most 48 rows name the same one
- route_weight: float32 [4096, 8], P(('dp', 'tensor')), may hold values from 0.05 to 0.35
- w_gate: bfloat16 [32, 3584, 1024], P(('dp', 'tensor')), may hold values from -1 to 1
- w_up: bfloat16 [32, 3584, 1024], P(('dp', 'tensor')), may hold values from -1 to 1
- w_down: bfloat16 [32, 1024, 3584], P(('dp', 'tensor')), may hold values from -0.1875 to 0.1875
- history_x: float32 [16], replicated, may hold values from 8 to 40
- history_h: float32 [16], replicated, may hold values from 4 to 16
Outputs:
- layer_out: bfloat16 [4096, 3584], P(('dp', 'tensor'))
- new_history_x: float32 [16], replicated
- new_history_h: float32 [16], replicated
The draws below stay inside these ranges and needn't reach their ends.
Inputs may be any that keep to these rules, and one draw needn't show every extreme that they name: `expert_ids`: among the routes of one device's 128 tokens no expert is named more than 48 times, a bound that some block reaches.
All inputs are finite; a program needn't handle non-finite values.
Results may differ from the reference program's by a relative error of at most 0.02.
Values may be sent and summed in bfloat16 or wider, within the bound.
No kernel may reach another device: no remote copies, remote signals or barrier semaphores. Data moves between devices by JAX's collectives and lax.ppermute only.
A program may use at most 128 MiB of HBM per device.

```python
import math
import jax
import jax.numpy as jnp
import numpy as np
from jax import lax

D = 3584
HEADS = 64
HD = 128
FF = 1024
TOP = 8
HIST = 16
ROWS_DEV = 128
EXPERTS = 32
CAP = 48
TOKENS = 4096
N_TENSOR = 4


def draw_residual(key, part):
    first_key, second_key = jax.random.split(jax.random.fold_in(key, 11))
    ramp = jnp.arange(TOKENS, dtype=jnp.float32)[:, None] / max(TOKENS - 1, 1)
    spread = jnp.clip(jax.random.normal(second_key, (TOKENS, D), jnp.float32), -5.0, 5.0)
    base = jnp.clip(jax.random.normal(first_key, (TOKENS, D), jnp.float32), -5.0, 5.0)
    heavy = 0.15 + 0.45 * ramp
    return (base * jnp.exp(heavy * spread)).astype(jnp.bfloat16)


def rising_weight(key, growth, flat_law):
    ramp = jnp.arange(EXPERTS, dtype=jnp.float32)[:, None, None] / max(EXPERTS - 1, 1)
    factor = D ** (-0.5) * jnp.power(growth, 0.5 * ramp)
    if flat_law:
        values = jax.random.uniform(key, (EXPERTS, D, FF), jnp.float32, -1.7, 1.7)
    else:
        values = jnp.clip(jax.random.normal(key, (EXPERTS, D, FF), jnp.float32), -5.0, 5.0)
    return jnp.clip(values * factor, -1.0, 1.0).astype(jnp.bfloat16)


def draw_w_gate(key, part):
    return rising_weight(jax.random.fold_in(key, 21), 3.0, False)


def draw_w_up(key, part):
    return rising_weight(jax.random.fold_in(key, 37), 3.0, False)


def block_scale(key, shape, pieces, least, high):
    def one(dim, blocks):
        draws = jax.random.uniform(jax.random.fold_in(jax.random.fold_in(key, 6), dim), (blocks,), jnp.float32, least / len(pieces), high / len(pieces))
        return jnp.repeat(jnp.exp(draws), shape[dim] // blocks).reshape((-1,) + (1,) * (len(shape) - dim - 1))

    loudness = one(*pieces[0])
    for cut in pieces[1:]:
        loudness = loudness * one(*cut)
    return loudness


def shared_out(stream_key, own, number, rows, number_of, top, reach, skew):
    sequence = jax.random.permutation(stream_key, number_of)
    heavy_load, common = shares(number_of, rows * top, reach, skew, True), shares(number_of, rows * top, reach, skew, False)
    places = jnp.arange(number_of)

    def named(sizes, offset_by):
        used = int((sizes > 0).sum())
        fixed = max(1, used // 4)
        passed = fixed + (places - fixed + offset_by * (used - fixed)) % max(1, number_of - fixed)
        return jnp.zeros((number_of,), jnp.int32).at[sequence[jnp.where(places < fixed, places, passed)]].set(jnp.asarray(sizes, jnp.int32))

    sizes = jnp.where(number % 4 == 0, named(heavy_load, number // 4), named(common, number - number // 4 - 1))
    mixed = jax.random.permutation(jax.random.fold_in(own, 3), number_of)
    source_of, receiver = mixed[0:number_of // 2 * 2:2], mixed[1:number_of // 2 * 2:2]
    margin = jnp.minimum(sizes[source_of] - 1, reach - sizes[receiver]) // 2
    margin = jnp.where((source_of == sequence[0]) | (receiver == sequence[0]) | (sizes[receiver] == 0), 0, jnp.maximum(margin, 0))
    passed = jax.random.randint(jax.random.fold_in(own, 4), (number_of // 2,), 0, 1 << 20) % (margin + 1)
    sizes = sizes.at[source_of].add(-passed).at[receiver].add(passed)
    labels = jnp.searchsorted(jnp.cumsum(sizes), jnp.arange(rows * top), side="right").astype(jnp.int32)
    grid = labels.reshape(top, rows).T
    grid = grid[jax.random.permutation(jax.random.fold_in(own, 1), rows)]
    offset_by = jax.random.randint(jax.random.fold_in(own, 2), (rows, 1), 0, top)
    return jnp.take_along_axis(grid, (jnp.arange(top)[None, :] + offset_by) % top, axis=1)


def shares(number_of, total, reach, slope, full):
    weights = [(1 << 20) // math.isqrt(grade ** slope) + 1 for grade in range(1, number_of + 1)]
    largest = reach if full else min(reach, max(-(-total // number_of), total * weights[0] // sum(weights)))
    least = 1 if total - largest >= number_of - 1 else 0
    counts, rest = [largest] + [least] * (number_of - 1), total - largest - least * (number_of - 1)
    while rest > 0:
        candidates = [i for i in range(1, number_of) if counts[i] < largest] or [i for i in range(1, number_of) if counts[i] < reach]
        whole, left = sum([weights[i] for i in candidates]), rest
        for i in candidates:
            extra = min(reach - counts[i], max(1, left * weights[i] // whole), rest)
            counts[i] = counts[i] + extra
            rest = rest - extra
    return np.array(counts)


def scatter_about(stream_key, shape, deviation, most, cuts=(), kind=jnp.bfloat16):
    result = jax.random.normal(stream_key, shape, jnp.float32) * deviation
    if len(cuts) > 0:
        result = block_scale(stream_key, shape, cuts, -0.22, 0.18) * result
    return jnp.clip(result, min=-most, max=most).astype(kind)


def setup_inputs(seed: int = 0) -> dict:
    streams_of = jax.random.split(jax.random.key(seed), 12)
    attn_out = scatter_about(streams_of[0], (TOKENS, HEADS * HD), 1.0, 6.0, ((0, 8), (1, 4)))
    out_weight = scatter_about(streams_of[1], (HEADS * HD, D), (HEADS * HD) ** -0.5, 0.0625, ((0, 4), (1, 8)))
    residual = draw_residual(jax.random.fold_in(streams_of[11], 71), 0)
    norm_gain = jnp.clip(1.0 + 0.1 * jax.random.normal(streams_of[3], (D,), jnp.float32), 0.5, 1.5)
    expert_ids_keys = jax.random.split(jax.random.fold_in(streams_of[4], 1), TOKENS // ROWS_DEV)
    expert_ids_turns = jax.random.permutation(jax.random.fold_in(streams_of[4], 3), TOKENS // ROWS_DEV)
    expert_ids = jax.vmap(lambda own, number: shared_out(jax.random.fold_in(streams_of[4], 2), own, number, ROWS_DEV, EXPERTS, TOP, CAP, 2))(expert_ids_keys, expert_ids_turns).reshape((TOKENS, TOP))
    route_weight = jnp.clip(0.05 + 0.29999999 * jax.random.uniform(streams_of[5], (TOKENS, TOP), jnp.float32) ** block_scale(streams_of[5], (TOKENS, TOP), ((0, 32),), -0.2, 0.2), 0.05, 0.35)
    w_gate = draw_w_gate(jax.random.fold_in(streams_of[11], 71), 0)
    w_up = draw_w_up(jax.random.fold_in(streams_of[11], 71), 0)
    w_down = scatter_about(streams_of[8], (EXPERTS, FF, D), FF ** -0.5, 0.1875, ((0, 32),))
    history_x = jnp.clip(jnp.exp(jax.random.uniform(streams_of[9], (HIST,), jnp.float32, math.log(8.0), math.log(40.0))), 8.0, 40.0)
    history_h = jnp.clip(jnp.exp(jax.random.uniform(streams_of[10], (HIST,), jnp.float32, math.log(4.0), math.log(16.0))), 4.0, 16.0)
    return dict(attn_out=attn_out, out_weight=out_weight, residual=residual, norm_gain=norm_gain, expert_ids=expert_ids, route_weight=route_weight, w_gate=w_gate, w_up=w_up, w_down=w_down, history_x=history_x, history_h=history_h)


FP8_LIMIT = 448.0

def reference(attn_out, out_weight, residual, norm_gain, expert_ids, route_weight, w_gate, w_up, w_down, history_x, history_h):
    block_width = HEADS * HD // N_TENSOR
    projected = jnp.zeros((TOKENS, D), jnp.float32)
    for column_block in range(N_TENSOR):
        lower = column_block * block_width
        partial_sum = jnp.dot(attn_out[:, lower:lower + block_width], out_weight[lower:lower + block_width], preferred_element_type=jnp.float32)
        rounded = lax.optimization_barrier(partial_sum.astype(jnp.bfloat16))
        projected = projected + rounded.astype(jnp.float32)
    stream = residual.astype(jnp.float32) + projected
    normed = stream * lax.rsqrt(lax.optimization_barrier(jnp.mean(stream * stream, axis=-1, keepdims=True)) + 1e-06) * norm_gain
    amax_x = jnp.max(jnp.abs(normed))
    scale_x = FP8_LIMIT / jnp.max(history_x)
    inv_x = jnp.max(history_x) / FP8_LIMIT
    scale_h = FP8_LIMIT / jnp.max(history_h)
    inv_h = jnp.max(history_h) / FP8_LIMIT
    quantized = jnp.clip(normed * scale_x, -FP8_LIMIT, FP8_LIMIT).astype(jnp.bfloat16)
    sources = TOKENS // ROWS_DEV
    flat_ids = expert_ids.reshape(sources, ROWS_DEV * TOP)
    onehot = (flat_ids[:, :, None] == jnp.arange(EXPERTS, dtype=jnp.int32)[None, None, :]).astype(jnp.int32)
    before = jnp.cumsum(onehot, axis=1) - onehot
    slot_index = lax.optimization_barrier(jnp.sum(before * onehot, axis=-1))
    position = flat_ids * (sources * CAP) + jnp.arange(sources, dtype=jnp.int32)[:, None] * CAP + slot_index
    table = jnp.full((EXPERTS * sources * CAP,), -1, jnp.int32)
    table = table.at[position.reshape(-1)].set(jnp.arange(TOKENS * TOP, dtype=jnp.int32))
    table = table.reshape(EXPERTS, sources * CAP)
    flat_weight = route_weight.reshape(-1)

    def one_expert(carry, inputs):
        running, largest = carry
        gate_matrix, up_matrix, down_matrix, entries = inputs
        valid = entries >= 0
        safe_entry = jnp.where(valid, entries, 0)
        token_index = safe_entry // TOP
        picked = quantized[token_index]
        picked = jnp.where(valid[:, None], picked, jnp.zeros_like(picked))
        gate = jnp.dot(picked, gate_matrix, preferred_element_type=jnp.float32) * inv_x
        upper = jnp.dot(picked, up_matrix, preferred_element_type=jnp.float32) * inv_x
        hidden = jax.nn.silu(gate) * upper
        largest = jnp.maximum(largest, jnp.max(jnp.abs(hidden)))
        hidden_q = jnp.clip(hidden * scale_h, -FP8_LIMIT, FP8_LIMIT).astype(jnp.bfloat16)
        expert_out = (jnp.dot(hidden_q, down_matrix, preferred_element_type=jnp.float32) * inv_h).astype(jnp.bfloat16)
        weights = jnp.where(valid, flat_weight[safe_entry], jnp.zeros((), jnp.float32))
        running = running.at[token_index].add(expert_out.astype(jnp.float32) * weights[:, None])
        return ((running, largest), None)
    start_carry = (jnp.zeros((TOKENS, D), jnp.float32), jnp.zeros((), jnp.float32))
    (mixture, amax_h), _ = lax.scan(one_expert, start_carry, (w_gate, w_up, w_down, table))
    layer_out = (stream + mixture).astype(jnp.bfloat16)
    new_history_x = jnp.concatenate([amax_x[None], history_x[:-1]])
    new_history_h = jnp.concatenate([amax_h[None], history_h[:-1]])
    return (layer_out, new_history_x, new_history_h)
```

```python
import jax
import jax.numpy as jnp
from jax import lax
from jax.sharding import PartitionSpec as P

FP8_LIMIT = 448.0
AXES = ("dp", "tensor")
CHUNKS = 2


def project(attn_out, out_weight):
    head_terms = jnp.dot(
        attn_out,
        lax.all_gather(out_weight, "dp", axis=1, tiled=True),
        preferred_element_type=jnp.float32,
    )
    return lax.psum_scatter(
        head_terms.astype(jnp.bfloat16), "tensor", scatter_dimension=0, tiled=True
    ).astype(jnp.float32)


def peaks_over_all(peaks):
    for axis in AXES:
        count = lax.axis_size(axis)
        shift = 1
        while shift < count:
            pairs = [(i, (i + shift) % count) for i in range(count)]
            peaks = jnp.maximum(peaks, lax.ppermute(peaks, axis, pairs))
            shift *= 2
    return peaks


def slots_of(ids, experts, capacity):
    flat_ids = ids.reshape(-1)
    onehot = (flat_ids[:, None] == jnp.arange(experts, dtype=jnp.int32)[None, :]).astype(jnp.int32)
    before = jnp.cumsum(onehot, axis=0) - onehot
    return flat_ids * capacity + jnp.sum(before * onehot, axis=-1)


def exchange_plan(
    quantized, stream, expert_ids, route_weight, weights, inv_x, scale_h, inv_h, capacity, experts
):
    w_gate, w_up, w_down = weights
    local_rows, width = quantized.shape
    top_count = expert_ids.shape[1]
    position = slots_of(expert_ids, experts, capacity)
    matches = (
        position.reshape(local_rows, top_count)[:, :, None]
        == jnp.arange(experts * capacity, dtype=jnp.int32)[None, None, :]
    )
    placing = jnp.sum(matches.astype(jnp.int32), axis=1).astype(jnp.bfloat16)
    outgoing = lax.dot_general(
        placing, quantized, (((0,), (0,)), ((), ())), preferred_element_type=jnp.float32
    )
    outgoing = outgoing.astype(jnp.bfloat16).reshape(experts, capacity, width)
    token_block = lax.all_to_all(outgoing, AXES, split_axis=0, concat_axis=0, tiled=True)
    flat_rows = token_block.reshape(-1, width)
    gate = jnp.dot(flat_rows, w_gate, preferred_element_type=jnp.float32) * inv_x
    upper = jnp.dot(flat_rows, w_up, preferred_element_type=jnp.float32) * inv_x
    hidden = jax.nn.silu(gate) * upper
    hidden_q = jnp.clip(hidden * scale_h, -FP8_LIMIT, FP8_LIMIT).astype(jnp.bfloat16)
    expert_out = (jnp.dot(hidden_q, w_down, preferred_element_type=jnp.float32) * inv_h).astype(
        jnp.bfloat16
    )
    returned = lax.all_to_all(
        expert_out.reshape(experts, capacity, width), AXES, split_axis=0, concat_axis=0, tiled=True
    )
    picked = returned.reshape(-1, width)[position].reshape(local_rows, top_count, width)
    mixture = jnp.sum(picked.astype(jnp.float32) * route_weight[:, :, None], axis=1)
    return (stream + mixture).astype(jnp.bfloat16), jnp.max(jnp.abs(hidden))


def gather_plan(
    quantized, stream, expert_ids, route_weight, weights, inv_x, scale_h, inv_h, capacity, experts
):
    w_gate, w_up, w_down = weights
    local_rows, width = quantized.shape
    mine = lax.axis_index("dp") * lax.axis_size("tensor") + lax.axis_index("tensor")
    all_ids = lax.all_gather(expert_ids, AXES, axis=0, tiled=True)
    all_weights = lax.all_gather(route_weight, AXES, axis=0, tiled=True)
    hit = all_ids == mine
    named = jnp.any(hit, axis=1).reshape(experts, local_rows)
    weight = jnp.sum(jnp.where(hit, all_weights, 0.0), axis=1).reshape(experts, local_rows)
    earlier = jnp.triu(jnp.ones((local_rows, local_rows), jnp.bfloat16), 1)
    slot = jnp.dot(named.astype(jnp.bfloat16), earlier, preferred_element_type=jnp.float32)
    slot = slot.astype(jnp.int32)
    chosen = (
        slot[:, None, :] == jnp.arange(capacity, dtype=jnp.int32)[None, :, None]
    ) & named[:, None, :]
    slot_weight = jnp.sum(jnp.where(chosen, weight[:, None, :], 0.0), axis=2)
    chosen = chosen.astype(jnp.bfloat16)
    step = width // CHUNKS
    gate = up = 0.0
    for c in range(CHUNKS):
        part = slice(c * step, (c + 1) * step)
        tokens = lax.all_gather(quantized[:, part], AXES, axis=0, tiled=True)
        rows = lax.dot_general(
            chosen,
            tokens.reshape(experts, local_rows, step),
            (((2,), (1,)), ((0,), (0,))),
            preferred_element_type=jnp.float32,
        )
        rows = rows.astype(jnp.bfloat16).reshape(experts * capacity, step)
        gate += jnp.dot(rows, w_gate[part], preferred_element_type=jnp.float32)
        up += jnp.dot(rows, w_up[part], preferred_element_type=jnp.float32)
    hidden = jax.nn.silu(gate * inv_x) * (up * inv_x)
    peak_h = jnp.max(jnp.abs(hidden))
    hidden_q = jnp.clip(hidden * scale_h, -FP8_LIMIT, FP8_LIMIT).astype(jnp.bfloat16)
    factor = slot_weight.reshape(-1, 1) * inv_h
    pieces = []
    for c in range(CHUNKS):
        part = slice(c * step, (c + 1) * step)
        terms = jnp.dot(hidden_q, w_down[:, part], preferred_element_type=jnp.float32) * factor
        spread = lax.dot_general(
            chosen,
            terms.astype(jnp.bfloat16).reshape(experts, capacity, step),
            (((1,), (1,)), ((0,), (0,))),
            preferred_element_type=jnp.float32,
        )
        spread = spread.astype(jnp.bfloat16).reshape(experts * local_rows, step)
        mixed = lax.psum_scatter(spread, AXES, scatter_dimension=0, tiled=True)
        pieces.append((stream[:, part] + mixed.astype(jnp.float32)).astype(jnp.bfloat16))
    return jnp.concatenate(pieces, axis=1), peak_h


def body(
    attn_out,
    out_weight,
    residual,
    norm_gain,
    expert_ids,
    route_weight,
    w_gate,
    w_up,
    w_down,
    history_x,
    history_h,
):
    experts = lax.axis_size("dp") * lax.axis_size("tensor")
    local_rows = residual.shape[0]
    top_count = expert_ids.shape[1]
    capacity = max(2, 3 * local_rows * top_count // (2 * experts))
    stream = residual.astype(jnp.float32) + project(attn_out, out_weight)
    normed = (
        stream * lax.rsqrt(jnp.mean(stream * stream, axis=-1, keepdims=True) + 1e-06) * norm_gain
    )
    peak_x = jnp.max(jnp.abs(normed))
    top_x, top_h = jnp.max(history_x), jnp.max(history_h)
    quantized = jnp.clip(normed * (FP8_LIMIT / top_x), -FP8_LIMIT, FP8_LIMIT).astype(jnp.bfloat16)
    plan = gather_plan if local_rows < 4 * capacity else exchange_plan
    layer_out, peak_h = plan(
        quantized,
        stream,
        expert_ids,
        route_weight,
        (w_gate[0], w_up[0], w_down[0]),
        top_x / FP8_LIMIT,
        FP8_LIMIT / top_h,
        top_h / FP8_LIMIT,
        capacity,
        experts,
    )
    peaks = peaks_over_all(jnp.stack([peak_x, peak_h]))
    new_history_x = jnp.concatenate([peaks[:1], history_x[:-1]])
    new_history_h = jnp.concatenate([peaks[1:], history_h[:-1]])
    return (layer_out, new_history_x, new_history_h)


def solution(mesh):
    in_specs = (
        P("dp", "tensor"),
        P("tensor", "dp"),
        P(AXES, None),
        P(),
        P(AXES, None),
        P(AXES, None),
        P(AXES, None, None),
        P(AXES, None, None),
        P(AXES, None, None),
        P(),
        P(),
    )
    out_specs = (P(AXES, None), P(), P())
    return jax.shard_map(body, mesh=mesh, in_specs=in_specs, out_specs=out_specs, check_vma=False)
```

```python
import functools

import jax
import jax.numpy as jnp
from jax import lax
from jax.experimental import pallas as pl
from jax.experimental.pallas import tpu as pltpu
from jax.sharding import PartitionSpec as P

FP8_LIMIT = 448.0
AXES = ("dp", "tensor")
CHUNKS = 2
VMEM_LIMIT = 40 * 2**20


def project(attn_out, out_weight):
    head_terms = jnp.dot(
        attn_out,
        lax.all_gather(out_weight, "dp", axis=1, tiled=True),
        preferred_element_type=jnp.float32,
    )
    return lax.psum_scatter(
        head_terms.astype(jnp.bfloat16), "tensor", scatter_dimension=0, tiled=True
    ).astype(jnp.float32)


def peaks_over_all(peaks):
    for axis in AXES:
        count = lax.axis_size(axis)
        shift = 1
        while shift < count:
            pairs = [(i, (i + shift) % count) for i in range(count)]
            peaks = jnp.maximum(peaks, lax.ppermute(peaks, axis, pairs))
            shift *= 2
    return peaks


def slots_of(ids, experts, capacity):
    flat_ids = ids.reshape(-1)
    onehot = (flat_ids[:, None] == jnp.arange(experts, dtype=jnp.int32)[None, :]).astype(jnp.int32)
    before = jnp.cumsum(onehot, axis=0) - onehot
    return flat_ids * capacity + jnp.sum(before * onehot, axis=-1)


def exchange_plan(
    quantized, stream, expert_ids, route_weight, weights, inv_x, scale_h, inv_h, capacity, experts
):
    w_gate, w_up, w_down = (weight[0] for weight in weights)
    local_rows, width = quantized.shape
    top_count = expert_ids.shape[1]
    position = slots_of(expert_ids, experts, capacity)
    matches = (
        position.reshape(local_rows, top_count)[:, :, None]
        == jnp.arange(experts * capacity, dtype=jnp.int32)[None, None, :]
    )
    placing = jnp.sum(matches.astype(jnp.int32), axis=1).astype(jnp.bfloat16)
    outgoing = lax.dot_general(
        placing, quantized, (((0,), (0,)), ((), ())), preferred_element_type=jnp.float32
    )
    outgoing = outgoing.astype(jnp.bfloat16).reshape(experts, capacity, width)
    token_block = lax.all_to_all(outgoing, AXES, split_axis=0, concat_axis=0, tiled=True)
    flat_rows = token_block.reshape(-1, width)
    gate = jnp.dot(flat_rows, w_gate, preferred_element_type=jnp.float32) * inv_x
    upper = jnp.dot(flat_rows, w_up, preferred_element_type=jnp.float32) * inv_x
    hidden = jax.nn.silu(gate) * upper
    hidden_q = jnp.clip(hidden * scale_h, -FP8_LIMIT, FP8_LIMIT).astype(jnp.bfloat16)
    expert_out = (jnp.dot(hidden_q, w_down, preferred_element_type=jnp.float32) * inv_h).astype(
        jnp.bfloat16
    )
    returned = lax.all_to_all(
        expert_out.reshape(experts, capacity, width), AXES, split_axis=0, concat_axis=0, tiled=True
    )
    picked = returned.reshape(-1, width)[position].reshape(local_rows, top_count, width)
    mixture = jnp.sum(picked.astype(jnp.float32) * route_weight[:, :, None], axis=1)
    return (stream + mixture).astype(jnp.bfloat16), jnp.max(jnp.abs(hidden))


def swap(value, bits):
    count = lax.axis_size("dp")
    return lax.ppermute(value, "dp", [(i, i ^ bits) for i in range(count)])


def route_table(expert_ids, route_weight, experts):
    rows = expert_ids.shape[0]
    names = jnp.arange(experts, dtype=jnp.int32)[:, None, None]
    table = jnp.sum(jnp.where(expert_ids[None] == names, route_weight[None], 0.0), axis=2)
    count = lax.axis_size("tensor")
    here = lax.axis_index("tensor")
    parts = [table]
    for shift in range(1, count):
        pairs = [(i, (i + shift) % count) for i in range(count)]
        parts.append(lax.ppermute(table, "tensor", pairs))
    order = (here - jnp.arange(count)) % count
    table = jnp.stack(parts)[order]
    bit = 1
    while bit < lax.axis_size("dp"):
        table = jnp.concatenate([table, swap(table, bit)])
        bit *= 2
    mine = lax.axis_index("dp") * count + here
    table = lax.dynamic_index_in_dim(table, mine, axis=1, keepdims=False)
    return table.reshape(-1, count, rows)


def gate_up_kernel(counts, first, last, *refs):
    refs = list(refs)
    scale_ref, chosen_ref = refs.pop(0), refs.pop(0)
    pieces = [refs.pop(0) for _ in counts]
    gate_w, up_w = refs.pop(0), refs.pop(0)
    before = [] if first else [refs.pop(0), refs.pop(0)]
    rows = refs.pop()
    capacity = chosen_ref.shape[1]

    @pl.when(pl.program_id(0) == 0)
    def _():
        source = 0
        for piece, count in zip(pieces, counts):
            for i in range(count):
                picked = jnp.dot(chosen_ref[source], piece[i], preferred_element_type=jnp.float32)
                rows[source * capacity : (source + 1) * capacity] = picked.astype(rows.dtype)
                source += 1

    gate = jnp.dot(rows[...], gate_w[0], preferred_element_type=jnp.float32)
    up = jnp.dot(rows[...], up_w[0], preferred_element_type=jnp.float32)
    if not first:
        gate += before[0][...]
        up += before[1][...]
    if not last:
        refs[0][...] = gate
        refs[1][...] = up
        return
    inv_x, scale_h = scale_ref[0], scale_ref[1]
    gate, up = gate * inv_x, up * inv_x
    hidden = gate / (1.0 + jnp.exp(-gate)) * up
    refs[0][...] = jnp.clip(hidden * scale_h, -FP8_LIMIT, FP8_LIMIT).astype(jnp.bfloat16)
    peak = jnp.max(jnp.abs(hidden), axis=0, keepdims=True)
    refs[1][...] = jnp.broadcast_to(peak, refs[1].shape)


def gate_up(scales, chosen, pieces, w_gate, w_up, c, before, last):
    sources, capacity, tokens = chosen.shape
    step = pieces[0].shape[-1]
    hidden = w_gate.shape[2]
    tile = min(256, hidden)
    rows = sources * capacity
    whole = lambda shape: pl.BlockSpec(shape, lambda n: (0,) * len(shape))
    column = lambda height: pl.BlockSpec((height, tile), lambda n: (0, n))
    weight = pl.BlockSpec((1, step, tile), lambda n: (0, c, n))
    if last:
        out_shape = [
            jax.ShapeDtypeStruct((rows, hidden), jnp.bfloat16),
            jax.ShapeDtypeStruct((8, hidden), jnp.float32),
        ]
        out_specs = [column(rows), column(8)]
    else:
        out_shape = [jax.ShapeDtypeStruct((rows, hidden), jnp.float32)] * 2
        out_specs = [column(rows)] * 2
    return pl.pallas_call(
        functools.partial(gate_up_kernel, [p.shape[0] for p in pieces], not before, last),
        grid=(hidden // tile,),
        in_specs=[pl.BlockSpec(memory_space=pltpu.SMEM), whole(chosen.shape)]
        + [whole(p.shape) for p in pieces]
        + [weight] * 2
        + [column(rows)] * len(before),
        out_specs=out_specs,
        out_shape=out_shape,
        scratch_shapes=[pltpu.VMEM((rows, step), jnp.bfloat16)],
        compiler_params=pltpu.CompilerParams(vmem_limit_bytes=VMEM_LIMIT),
        cost_estimate=pl.CostEstimate(
            flops=2 * rows * step * (2 * hidden + tokens),
            bytes_accessed=2 * step * (2 * hidden + sources * tokens) + 16 * rows * hidden,
            transcendentals=rows * hidden if last else 0,
        ),
        name="gate_up",
    )(scales, chosen, *pieces, w_gate, w_up, *before)


def down_kernel(hidden_ref, down_w, factor_ref, spread_ref, own_ref, other_ref):
    sources, tokens, capacity = spread_ref.shape
    terms = jnp.dot(hidden_ref[...], down_w[0], preferred_element_type=jnp.float32)
    terms = (terms * factor_ref[...]).astype(jnp.bfloat16)
    half = sources // 2
    for source in range(sources):
        spread = jnp.dot(
            spread_ref[source],
            terms[source * capacity : (source + 1) * capacity],
            preferred_element_type=jnp.float32,
        ).astype(jnp.bfloat16)
        if source < half:
            own_ref[source] = spread
        else:
            other_ref[source - half] = spread


def down(hidden_q, w_down, factor, spread, c, step):
    rows, hidden = hidden_q.shape
    sources, tokens, capacity = spread.shape
    tile = 256 if step % 256 == 0 else 128
    tiles = step // tile
    whole = lambda shape: pl.BlockSpec(shape, lambda j: (0,) * len(shape))
    return pl.pallas_call(
        down_kernel,
        grid=(tiles,),
        in_specs=[
            whole(hidden_q.shape),
            pl.BlockSpec((1, hidden, tile), lambda j: (0, 0, c * tiles + j)),
            whole(factor.shape),
            whole(spread.shape),
        ],
        out_specs=[pl.BlockSpec((sources // 2, tokens, tile), lambda j: (0, 0, j))] * 2,
        out_shape=[jax.ShapeDtypeStruct((sources // 2, tokens, step), jnp.bfloat16)] * 2,
        compiler_params=pltpu.CompilerParams(vmem_limit_bytes=VMEM_LIMIT),
        cost_estimate=pl.CostEstimate(
            flops=2 * rows * step * (hidden + tokens),
            bytes_accessed=2 * step * (hidden + sources * tokens),
            transcendentals=0,
        ),
        name="down",
    )(hidden_q, w_down, factor, spread)


def add(*terms):
    return sum(t.astype(jnp.float32) for t in terms).astype(jnp.bfloat16)


def gather_plan(
    quantized, stream, expert_ids, route_weight, weights, inv_x, scale_h, inv_h, capacity, experts
):
    w_gate, w_up, w_down = weights
    local_rows, width = quantized.shape
    layers = lax.axis_size("tensor")
    half = layers // 2
    weight = route_table(expert_ids, route_weight, experts)
    named = weight > 0.0
    earlier = jnp.triu(jnp.ones((local_rows, local_rows), jnp.bfloat16), 1)
    slot = lax.dot_general(
        named.astype(jnp.bfloat16), earlier, (((2,), (0,)), ((), ())),
        preferred_element_type=jnp.float32,
    ).astype(jnp.int32)
    chosen = (
        slot[:, :, None, :] == jnp.arange(capacity, dtype=jnp.int32)[:, None]
    ) & named[:, :, None, :]
    factor = jnp.sum(jnp.where(chosen, weight[:, :, None, :], 0.0), axis=3) * inv_h
    chosen = chosen.astype(jnp.bfloat16).reshape(4, 2 * layers, capacity, local_rows)
    factor = factor.reshape(4, 2 * layers * capacity, 1)
    spread = chosen.transpose(0, 1, 3, 2)
    scales = jnp.stack([inv_x, scale_h])
    step = width // CHUNKS

    sums = [[] for _ in range(4)]
    for c in range(CHUNKS):
        part = slice(c * step, (c + 1) * step)
        own = lax.all_gather(quantized[:, part], "tensor", axis=0).reshape(layers, local_rows, step)
        along_x, along_y = swap(own, 2), swap(own, 4)
        diagonal = [swap(along_x[:half], 4), swap(along_y[half:], 2)]
        groups = [[own], [along_x], [along_y], diagonal]
        for r, group in enumerate(groups):
            pieces = group + [swap(piece, 1) for piece in group]
            sums[r] = gate_up(
                scales, chosen[r], pieces, w_gate, w_up, c, sums[r], c == CHUNKS - 1
            )
    peak_h = jnp.max(jnp.stack([jnp.max(s[1]) for s in sums]))

    outputs = []
    for c in range(CHUNKS):
        part = slice(c * step, (c + 1) * step)
        to = []
        for r in range(4):
            kept, given = down(sums[r][0], w_down, factor[r], spread[r], c, step)
            taken = swap(given, 1)
            to.append([add(kept[:half], taken[:half]), add(kept[half:], taken[half:])])
        over_x, over_y = swap(to[3][0], 2), swap(to[3][1], 4)
        low = add(to[0][0], swap(to[1][0], 2), swap(add(to[2][0], over_x), 4))
        high = add(to[0][1], swap(add(to[1][1], over_y), 2), swap(to[2][1], 4))
        mixed = jnp.concatenate([low, high]).reshape(layers * local_rows, step)
        mixed = lax.psum_scatter(mixed, "tensor", scatter_dimension=0, tiled=True)
        outputs.append((stream[:, part] + mixed.astype(jnp.float32)).astype(jnp.bfloat16))
    return jnp.concatenate(outputs, axis=1), peak_h


def body(
    attn_out,
    out_weight,
    residual,
    norm_gain,
    expert_ids,
    route_weight,
    w_gate,
    w_up,
    w_down,
    history_x,
    history_h,
):
    experts = lax.axis_size("dp") * lax.axis_size("tensor")
    local_rows = residual.shape[0]
    top_count = expert_ids.shape[1]
    capacity = max(2, 3 * local_rows * top_count // (2 * experts))
    stream = residual.astype(jnp.float32) + project(attn_out, out_weight)
    normed = (
        stream * lax.rsqrt(jnp.mean(stream * stream, axis=-1, keepdims=True) + 1e-06) * norm_gain
    )
    peak_x = jnp.max(jnp.abs(normed))
    top_x, top_h = jnp.max(history_x), jnp.max(history_h)
    quantized = jnp.clip(normed * (FP8_LIMIT / top_x), -FP8_LIMIT, FP8_LIMIT).astype(jnp.bfloat16)
    gathers = lax.axis_size("dp") == 8 and local_rows < 4 * capacity
    plan = gather_plan if gathers else exchange_plan
    layer_out, peak_h = plan(
        quantized,
        stream,
        expert_ids,
        route_weight,
        (w_gate, w_up, w_down),
        top_x / FP8_LIMIT,
        FP8_LIMIT / top_h,
        top_h / FP8_LIMIT,
        capacity,
        experts,
    )
    peaks = peaks_over_all(jnp.stack([peak_x, peak_h]))
    new_history_x = jnp.concatenate([peaks[:1], history_x[:-1]])
    new_history_h = jnp.concatenate([peaks[1:], history_h[:-1]])
    return (layer_out, new_history_x, new_history_h)


def solution(mesh):
    in_specs = (
        P("dp", "tensor"),
        P("tensor", "dp"),
        P(AXES, None),
        P(),
        P(AXES, None),
        P(AXES, None),
        P(AXES, None, None),
        P(AXES, None, None),
        P(AXES, None, None),
        P(),
        P(),
    )
    out_specs = (P(AXES, None), P(), P())
    return jax.shard_map(body, mesh=mesh, in_specs=in_specs, out_specs=out_specs, check_vma=False)
```

```python
import functools

import jax
import jax.numpy as jnp
from jax import lax
from jax.experimental import pallas as pl
from jax.experimental.pallas import tpu as pltpu
from jax.sharding import PartitionSpec as P

FP8_LIMIT = 448.0
AXES = ("dp", "tensor")
CHUNKS = 2
VMEM_LIMIT = 40 * 2**20


def project(attn_out, out_weight):
    head_terms = jnp.dot(
        attn_out,
        lax.all_gather(out_weight, "dp", axis=1, tiled=True),
        preferred_element_type=jnp.float32,
    )
    return lax.psum_scatter(
        head_terms.astype(jnp.bfloat16), "tensor", scatter_dimension=0, tiled=True
    ).astype(jnp.float32)


def peaks_over_all(peaks):
    for axis in AXES:
        count = lax.axis_size(axis)
        shift = 1
        while shift < count:
            pairs = [(i, (i + shift) % count) for i in range(count)]
            peaks = jnp.maximum(peaks, lax.ppermute(peaks, axis, pairs))
            shift *= 2
    return peaks


def slots_of(ids, experts, capacity):
    flat_ids = ids.reshape(-1)
    onehot = (flat_ids[:, None] == jnp.arange(experts, dtype=jnp.int32)[None, :]).astype(jnp.int32)
    before = jnp.cumsum(onehot, axis=0) - onehot
    return flat_ids * capacity + jnp.sum(before * onehot, axis=-1)


def exchange_plan(
    attn_out,
    out_weight,
    residual,
    norm_gain,
    expert_ids,
    route_weight,
    w_gate,
    w_up,
    w_down,
    top_x,
    top_h,
    capacity,
):
    experts = lax.axis_size("dp") * lax.axis_size("tensor")
    inv_x, inv_h, scale_h = top_x / FP8_LIMIT, top_h / FP8_LIMIT, FP8_LIMIT / top_h
    local_rows, width = residual.shape
    top_count = expert_ids.shape[1]
    stream = residual.astype(jnp.float32) + project(attn_out, out_weight)
    normed = (
        stream * lax.rsqrt(jnp.mean(stream * stream, axis=-1, keepdims=True) + 1e-06) * norm_gain
    )
    quantized = jnp.clip(normed * (FP8_LIMIT / top_x), -FP8_LIMIT, FP8_LIMIT).astype(jnp.bfloat16)
    position = slots_of(expert_ids, experts, capacity)
    matches = (
        position.reshape(local_rows, top_count)[:, :, None]
        == jnp.arange(experts * capacity, dtype=jnp.int32)[None, None, :]
    )
    placing = jnp.sum(matches.astype(jnp.int32), axis=1).astype(jnp.bfloat16)
    outgoing = lax.dot_general(
        placing, quantized, (((0,), (0,)), ((), ())), preferred_element_type=jnp.float32
    )
    outgoing = outgoing.astype(jnp.bfloat16).reshape(experts, capacity, width)
    token_block = lax.all_to_all(outgoing, AXES, split_axis=0, concat_axis=0, tiled=True)
    flat_rows = token_block.reshape(-1, width)
    gate = jnp.dot(flat_rows, w_gate[0], preferred_element_type=jnp.float32) * inv_x
    upper = jnp.dot(flat_rows, w_up[0], preferred_element_type=jnp.float32) * inv_x
    hidden = jax.nn.silu(gate) * upper
    hidden_q = jnp.clip(hidden * scale_h, -FP8_LIMIT, FP8_LIMIT).astype(jnp.bfloat16)
    expert_out = (jnp.dot(hidden_q, w_down[0], preferred_element_type=jnp.float32) * inv_h).astype(
        jnp.bfloat16
    )
    returned = lax.all_to_all(
        expert_out.reshape(experts, capacity, width), AXES, split_axis=0, concat_axis=0, tiled=True
    )
    picked = returned.reshape(-1, width)[position].reshape(local_rows, top_count, width)
    mixture = jnp.sum(picked.astype(jnp.float32) * route_weight[:, :, None], axis=1)
    peaks = jnp.max(jnp.abs(normed)), jnp.max(jnp.abs(hidden))
    return (stream + mixture).astype(jnp.bfloat16), *peaks


def swap(value, bits):
    count = lax.axis_size("dp")
    return lax.ppermute(value, "dp", [(i, i ^ bits) for i in range(count)])


def from_all(value):
    count = lax.axis_size("tensor")
    parts = [value]
    for shift in range(1, count):
        pairs = [(i, (i + shift) % count) for i in range(count)]
        parts.append(lax.ppermute(value, "tensor", pairs))
    order = (lax.axis_index("tensor") - jnp.arange(count)) % count
    values = jnp.stack(parts)[order][None]
    bit = 1
    while bit < lax.axis_size("dp"):
        values = jnp.concatenate([values, swap(values, bit)])
        bit *= 2
    return values


def expert_weights(expert_ids, route_weight, experts):
    names = jnp.arange(experts, dtype=jnp.int32)[:, None, None]
    table = jnp.sum(jnp.where(expert_ids[None] == names, route_weight[None], 0.0), axis=2)
    mine = lax.axis_index("dp") * lax.axis_size("tensor") + lax.axis_index("tensor")
    return lax.dynamic_index_in_dim(from_all(table), mine, axis=2, keepdims=False)


def chip_groups(value):
    half = value.shape[0] // 2
    along_x, along_y = swap(value, 2), swap(value, 4)
    diagonal = [swap(along_x[:half], 4), swap(along_y[half:], 2)]
    groups = [[value], [along_x], [along_y], diagonal]
    return [(group, [swap(piece, 1) for piece in group]) for group in groups]


def project_kernel(place_ref, attn_ref, *refs):
    out_ref, joined, stage = refs[-3:]
    pieces = refs[:-3]
    columns = pieces[0].shape[0]
    attn = attn_ref[...]
    blocks = [pieces[0], pieces[1], pieces[2], pieces[3], pieces[4], pieces[5], None, None]
    for k, block in enumerate(blocks):
        if block is None:
            low, high = pieces[2 * k - 6], pieces[2 * k - 5]
            joined[: low.shape[0]] = low[...]
            joined[low.shape[0] :] = high[...]
            block = joined
        terms = lax.dot_general(
            attn, block[...], (((1,), (1,)), ((), ())), preferred_element_type=jnp.float32
        )
        stage[place_ref[0] ^ k, :, :columns] = terms
    for j in range(stage.shape[0]):
        out_ref[:, j * columns : (j + 1) * columns] = stage[j, :, :columns].astype(out_ref.dtype)


def project_part(place, attn_out, groups):
    rows, depth = attn_out.shape
    pieces = [piece for pair in groups for group in pair for piece in group]
    columns = pieces[0].shape[0]
    return pl.pallas_call(
        project_kernel,
        in_specs=[pl.BlockSpec(memory_space=pltpu.SMEM)]
        + [pl.BlockSpec(memory_space=pltpu.VMEM)] * (1 + len(pieces)),
        out_specs=pl.BlockSpec(memory_space=pltpu.VMEM),
        out_shape=jax.ShapeDtypeStruct((rows, 8 * columns), jnp.bfloat16),
        scratch_shapes=[
            pltpu.VMEM((columns, depth), jnp.bfloat16),
            pltpu.VMEM((8, rows, -(-columns // 128) * 128), jnp.float32),
        ],
        compiler_params=pltpu.CompilerParams(vmem_limit_bytes=VMEM_LIMIT),
        cost_estimate=pl.CostEstimate(
            flops=16 * rows * depth * columns,
            bytes_accessed=2 * depth * (rows + 8 * columns),
            transcendentals=0,
        ),
        name="project",
    )(place, attn_out, *pieces)


def gate_up_kernel(counts, first, last, *refs):
    refs = list(refs)
    scale_ref, gain_ref, chosen_ref, root_ref = (refs.pop(0) for _ in range(4))
    pieces = [refs.pop(0) for _ in counts]
    gate_w, up_w = refs.pop(0), refs.pop(0)
    before = [] if first else [refs.pop(0), refs.pop(0)]
    rows = refs.pop()
    capacity = chosen_ref.shape[1]

    @pl.when(pl.program_id(0) == 0)
    def _():
        source = 0
        for piece, count in zip(pieces, counts):
            for i in range(count):
                span = slice(source * capacity, (source + 1) * capacity)
                picked = jnp.dot(chosen_ref[source], piece[i], preferred_element_type=jnp.float32)
                picked = picked * root_ref[span] * gain_ref[...]
                rows[span] = jnp.clip(picked, -FP8_LIMIT, FP8_LIMIT).astype(rows.dtype)
                source += 1

    flat = lambda weight: weight[0].reshape(rows.shape[1], weight.shape[-1])
    gate = jnp.dot(rows[...], flat(gate_w), preferred_element_type=jnp.float32)
    up = jnp.dot(rows[...], flat(up_w), preferred_element_type=jnp.float32)
    if not first:
        gate += before[0][...]
        up += before[1][...]
    if not last:
        refs[0][...] = gate
        refs[1][...] = up
        return
    inv_x, scale_h = scale_ref[0], scale_ref[1]
    gate, up = gate * inv_x, up * inv_x
    hidden = gate / (1.0 + jnp.exp(-gate)) * up
    refs[0][...] = jnp.clip(hidden * scale_h, -FP8_LIMIT, FP8_LIMIT).astype(jnp.bfloat16)
    peak = jnp.max(jnp.abs(hidden), axis=0, keepdims=True)
    refs[1][...] = jnp.broadcast_to(peak, refs[1].shape)


def gate_up(scales, gain, chosen, root, pieces, w_gate, w_up, c, before, last):
    sources, capacity, tokens = chosen.shape
    step = pieces[0].shape[-1]
    hidden = w_gate.shape[-1]
    tile = min(256, hidden)
    rows = sources * capacity
    whole = lambda shape: pl.BlockSpec(shape, lambda n: (0,) * len(shape))
    column = lambda height: pl.BlockSpec((height, tile), lambda n: (0, n))
    owners, columns = w_gate.shape[1], w_gate.shape[3]
    weight = pl.BlockSpec((1, owners, None, columns, tile), lambda n: (0, 0, c, 0, n))
    if last:
        out_shape = [
            jax.ShapeDtypeStruct((rows, hidden), jnp.bfloat16),
            jax.ShapeDtypeStruct((8, hidden), jnp.float32),
        ]
        out_specs = [column(rows), column(8)]
    else:
        out_shape = [jax.ShapeDtypeStruct((rows, hidden), jnp.float32)] * 2
        out_specs = [column(rows)] * 2
    return pl.pallas_call(
        functools.partial(gate_up_kernel, [p.shape[0] for p in pieces], not before, last),
        grid=(hidden // tile,),
        in_specs=[pl.BlockSpec(memory_space=pltpu.SMEM)]
        + [whole(gain.shape), whole(chosen.shape), whole(root.shape)]
        + [whole(p.shape) for p in pieces]
        + [weight] * 2
        + [column(rows)] * len(before),
        out_specs=out_specs,
        out_shape=out_shape,
        scratch_shapes=[pltpu.VMEM((rows, step), jnp.bfloat16)],
        compiler_params=pltpu.CompilerParams(vmem_limit_bytes=VMEM_LIMIT),
        cost_estimate=pl.CostEstimate(
            flops=2 * rows * step * (2 * hidden + tokens),
            bytes_accessed=2 * step * (2 * hidden + sources * tokens) + 16 * rows * hidden,
            transcendentals=rows * hidden if last else 0,
        ),
        name="gate_up",
    )(scales, gain, chosen, root, *pieces, w_gate, w_up, *before)


def down_kernel(hidden_ref, down_w, factor_ref, spread_ref, own_ref, other_ref):
    sources, tokens, capacity = spread_ref.shape
    terms = jnp.dot(hidden_ref[...], down_w[0], preferred_element_type=jnp.float32)
    terms = (terms * factor_ref[...]).astype(jnp.bfloat16)
    half = sources // 2
    for source in range(sources):
        spread = jnp.dot(
            spread_ref[source],
            terms[source * capacity : (source + 1) * capacity],
            preferred_element_type=jnp.float32,
        ).astype(jnp.bfloat16)
        if source < half:
            own_ref[source] = spread
        else:
            other_ref[source - half] = spread


def down(hidden_q, w_down, factor, spread, c, step):
    rows, hidden = hidden_q.shape
    sources, tokens, capacity = spread.shape
    tile = 256 if step % 256 == 0 else 128
    tiles = step // tile
    whole = lambda shape: pl.BlockSpec(shape, lambda j: (0,) * len(shape))
    return pl.pallas_call(
        down_kernel,
        grid=(tiles,),
        in_specs=[
            whole(hidden_q.shape),
            pl.BlockSpec((1, hidden, tile), lambda j: (0, 0, c * tiles + j)),
            whole(factor.shape),
            whole(spread.shape),
        ],
        out_specs=[pl.BlockSpec((sources // 2, tokens, tile), lambda j: (0, 0, j))] * 2,
        out_shape=[jax.ShapeDtypeStruct((sources // 2, tokens, step), jnp.bfloat16)] * 2,
        compiler_params=pltpu.CompilerParams(vmem_limit_bytes=VMEM_LIMIT),
        cost_estimate=pl.CostEstimate(
            flops=2 * rows * step * (hidden + tokens),
            bytes_accessed=2 * step * (hidden + sources * tokens),
            transcendentals=0,
        ),
        name="down",
    )(hidden_q, w_down, factor, spread)


def add(*terms):
    return sum(t.astype(jnp.float32) for t in terms).astype(jnp.bfloat16)


def gather_plan(
    attn_out,
    out_weight,
    residual,
    norm_gain,
    expert_ids,
    route_weight,
    w_gate,
    w_up,
    w_down,
    top_x,
    top_h,
    capacity,
):
    owners, layers = lax.axis_size("dp"), lax.axis_size("tensor")
    experts = owners * layers
    local_rows, width = residual.shape
    half, step = layers // 2, width // CHUNKS
    columns = step // owners

    weight = expert_weights(expert_ids, route_weight, experts)
    weight_rows = out_weight.T.reshape(CHUNKS, columns, -1)
    blocks = [chip_groups(weight_rows[c]) for c in range(CHUNKS)]
    attn_out, weight = lax.optimization_barrier((attn_out, weight))

    named = weight > 0.0
    earlier = jnp.triu(jnp.ones((local_rows, local_rows), jnp.bfloat16), 1)
    slot = lax.dot_general(
        named.astype(jnp.bfloat16),
        earlier,
        (((2,), (0,)), ((), ())),
        preferred_element_type=jnp.float32,
    ).astype(jnp.int32)
    chosen = (
        slot[:, :, None, :] == jnp.arange(capacity, dtype=jnp.int32)[:, None]
    ) & named[:, :, None, :]
    by_slot = lambda values: jnp.sum(
        jnp.where(chosen, values[:, :, None, :], 0.0), axis=3
    ).reshape(4, 2 * layers * capacity, 1)
    factor = by_slot(weight) * (top_h / FP8_LIMIT)
    choice = chosen.astype(jnp.bfloat16).reshape(4, 2 * layers, capacity, local_rows)
    spread = choice.transpose(0, 1, 3, 2)
    scales = jnp.stack([top_x / FP8_LIMIT, FP8_LIMIT / top_h])

    split = lambda value: value.reshape(-1, owners, CHUNKS, columns)
    parts = lambda value, c: split(value)[:, :, c].reshape(-1, step)
    place = lax.axis_index("dp")[None]
    stream, tokens = [], []
    for c in range(CHUNKS):
        terms = project_part(place, attn_out, blocks[c])
        total = lax.psum_scatter(terms, "tensor", scatter_dimension=0, tiled=True)
        stream.append(parts(residual, c).astype(jnp.float32) + total.astype(jnp.float32))
        own = lax.all_gather(stream[c].astype(jnp.bfloat16), "tensor", axis=0)
        tokens.append(chip_groups(own))
    squares = sum(jnp.sum(part * part, axis=1) for part in stream)
    root = lax.rsqrt(squares / width + 1e-06)
    gains = [parts(norm_gain, c) for c in range(CHUNKS)]
    peak_x = jnp.max(
        jnp.stack([jnp.max(jnp.abs(s * root[:, None] * g)) for s, g in zip(stream, gains)])
    )
    roots = by_slot(from_all(root))
    gains = [g * (FP8_LIMIT / top_x) for g in gains]

    gate_rows = w_gate.reshape(1, owners, CHUNKS, columns, -1)
    up_rows = w_up.reshape(1, owners, CHUNKS, columns, -1)
    sums = [[] for _ in range(4)]
    for c in range(CHUNKS):
        for r, (near, far) in enumerate(tokens[c]):
            sums[r] = gate_up(
                scales,
                gains[c],
                choice[r],
                roots[r],
                near + far,
                gate_rows,
                up_rows,
                c,
                sums[r],
                c == CHUNKS - 1,
            )
    peak_h = jnp.max(jnp.stack([jnp.max(s[1]) for s in sums]))

    mixture = []
    for c in range(CHUNKS):
        to = []
        for r in range(4):
            kept, given = down(sums[r][0], w_down, factor[r], spread[r], c, step)
            taken = swap(given, 1)
            to.append([add(kept[:half], taken[:half]), add(kept[half:], taken[half:])])
        over_x, over_y = swap(to[3][0], 2), swap(to[3][1], 4)
        low = add(to[0][0], swap(to[1][0], 2), swap(add(to[2][0], over_x), 4))
        high = add(to[0][1], swap(add(to[1][1], over_y), 2), swap(to[2][1], 4))
        mixed = jnp.concatenate([low, high]).reshape(layers * local_rows, step)
        mixture.append(lax.psum_scatter(mixed, "tensor", scatter_dimension=0, tiled=True))
    stream = jnp.stack([s.reshape(local_rows, owners, columns) for s in stream], axis=2)
    stream = stream.reshape(local_rows, width)
    layer_out = stream + jnp.concatenate(mixture, axis=1).astype(jnp.float32)
    return layer_out.astype(jnp.bfloat16), peak_x, peak_h


def body(
    attn_out,
    out_weight,
    residual,
    norm_gain,
    expert_ids,
    route_weight,
    w_gate,
    w_up,
    w_down,
    history_x,
    history_h,
):
    experts = lax.axis_size("dp") * lax.axis_size("tensor")
    local_rows, top_count = expert_ids.shape
    capacity = max(2, 3 * local_rows * top_count // (2 * experts))
    top_x, top_h = jnp.max(history_x), jnp.max(history_h)
    gathers = lax.axis_size("dp") == 8 and local_rows < 4 * capacity
    plan = gather_plan if gathers else exchange_plan
    layer_out, peak_x, peak_h = plan(
        attn_out,
        out_weight,
        residual,
        norm_gain,
        expert_ids,
        route_weight,
        w_gate,
        w_up,
        w_down,
        top_x,
        top_h,
        capacity,
    )
    peaks = peaks_over_all(jnp.stack([peak_x, peak_h]))
    new_history_x = jnp.concatenate([peaks[:1], history_x[:-1]])
    new_history_h = jnp.concatenate([peaks[1:], history_h[:-1]])
    return (layer_out, new_history_x, new_history_h)


def solution(mesh):
    in_specs = (
        P("dp", "tensor"),
        P("tensor", "dp"),
        P(AXES, None),
        P(),
        P(AXES, None),
        P(AXES, None),
        P(AXES, None, None),
        P(AXES, None, None),
        P(AXES, None, None),
        P(),
        P(),
    )
    out_specs = (P(AXES, None), P(), P())
    return jax.shard_map(body, mesh=mesh, in_specs=in_specs, out_specs=out_specs, check_vma=False)
```

```python
import functools

import jax
import jax.numpy as jnp
from jax import lax
from jax.experimental import pallas as pl
from jax.experimental.pallas import tpu as pltpu
from jax.sharding import PartitionSpec as P

FP8_LIMIT = 448.0
AXES = ("dp", "tensor")
CHUNKS = 2
VMEM_LIMIT = 48 * 2**20


def project(attn_out, out_weight):
    head_terms = jnp.dot(
        attn_out,
        lax.all_gather(out_weight, "dp", axis=1, tiled=True),
        preferred_element_type=jnp.float32,
    )
    return lax.psum_scatter(
        head_terms.astype(jnp.bfloat16), "tensor", scatter_dimension=0, tiled=True
    ).astype(jnp.float32)


def peaks_over_all(peaks):
    for axis in AXES:
        count = lax.axis_size(axis)
        shift = 1
        while shift < count:
            pairs = [(i, (i + shift) % count) for i in range(count)]
            peaks = jnp.maximum(peaks, lax.ppermute(peaks, axis, pairs))
            shift *= 2
    return peaks


def slots_of(ids, experts, capacity):
    flat_ids = ids.reshape(-1)
    onehot = (flat_ids[:, None] == jnp.arange(experts, dtype=jnp.int32)[None, :]).astype(jnp.int32)
    before = jnp.cumsum(onehot, axis=0) - onehot
    return flat_ids * capacity + jnp.sum(before * onehot, axis=-1)


def exchange_plan(
    attn_out,
    out_weight,
    residual,
    norm_gain,
    expert_ids,
    route_weight,
    w_gate,
    w_up,
    w_down,
    top_x,
    top_h,
    capacity,
):
    experts = lax.axis_size("dp") * lax.axis_size("tensor")
    inv_x, inv_h, scale_h = top_x / FP8_LIMIT, top_h / FP8_LIMIT, FP8_LIMIT / top_h
    local_rows, width = residual.shape
    top_count = expert_ids.shape[1]
    stream = residual.astype(jnp.float32) + project(attn_out, out_weight)
    normed = (
        stream * lax.rsqrt(jnp.mean(stream * stream, axis=-1, keepdims=True) + 1e-06) * norm_gain
    )
    quantized = jnp.clip(normed * (FP8_LIMIT / top_x), -FP8_LIMIT, FP8_LIMIT).astype(jnp.bfloat16)
    position = slots_of(expert_ids, experts, capacity)
    matches = (
        position.reshape(local_rows, top_count)[:, :, None]
        == jnp.arange(experts * capacity, dtype=jnp.int32)[None, None, :]
    )
    placing = jnp.sum(matches.astype(jnp.int32), axis=1).astype(jnp.bfloat16)
    outgoing = lax.dot_general(
        placing, quantized, (((0,), (0,)), ((), ())), preferred_element_type=jnp.float32
    )
    outgoing = outgoing.astype(jnp.bfloat16).reshape(experts, capacity, width)
    token_block = lax.all_to_all(outgoing, AXES, split_axis=0, concat_axis=0, tiled=True)
    flat_rows = token_block.reshape(-1, width)
    gate = jnp.dot(flat_rows, w_gate[0], preferred_element_type=jnp.float32) * inv_x
    upper = jnp.dot(flat_rows, w_up[0], preferred_element_type=jnp.float32) * inv_x
    hidden = jax.nn.silu(gate) * upper
    hidden_q = jnp.clip(hidden * scale_h, -FP8_LIMIT, FP8_LIMIT).astype(jnp.bfloat16)
    expert_out = (jnp.dot(hidden_q, w_down[0], preferred_element_type=jnp.float32) * inv_h).astype(
        jnp.bfloat16
    )
    returned = lax.all_to_all(
        expert_out.reshape(experts, capacity, width), AXES, split_axis=0, concat_axis=0, tiled=True
    )
    picked = returned.reshape(-1, width)[position].reshape(local_rows, top_count, width)
    mixture = jnp.sum(picked.astype(jnp.float32) * route_weight[:, :, None], axis=1)
    peaks = jnp.max(jnp.abs(normed)), jnp.max(jnp.abs(hidden))
    return (stream + mixture).astype(jnp.bfloat16), *peaks


def swap(value, bits):
    count = lax.axis_size("dp")
    return lax.ppermute(value, "dp", [(i, i ^ bits) for i in range(count)])


def from_all(value):
    count = lax.axis_size("tensor")
    parts = [value]
    for shift in range(1, count):
        pairs = [(i, (i + shift) % count) for i in range(count)]
        parts.append(lax.ppermute(value, "tensor", pairs))
    order = (lax.axis_index("tensor") - jnp.arange(count)) % count
    values = jnp.stack(parts)[order][None]
    bit = 1
    while bit < lax.axis_size("dp"):
        values = jnp.concatenate([values, swap(values, bit)])
        bit *= 2
    return values


def along_tensor(value):
    count, here = lax.axis_size("tensor"), lax.axis_index("tensor")
    blocks = jnp.zeros((count,) + value.shape, value.dtype)
    for shift in range(count):
        pairs = [(i, (i + shift) % count) for i in range(count)]
        block = lax.ppermute(value, "tensor", pairs) if shift else value
        blocks = lax.dynamic_update_index_in_dim(blocks, block, (here - shift) % count, 0)
    return blocks


def expert_weights(expert_ids, route_weight, experts):
    names = jnp.arange(experts, dtype=jnp.int32)[:, None, None]
    table = jnp.sum(jnp.where(expert_ids[None] == names, route_weight[None], 0.0), axis=2)
    mine = lax.axis_index("dp") * lax.axis_size("tensor") + lax.axis_index("tensor")
    return lax.dynamic_index_in_dim(from_all(table), mine, axis=2, keepdims=False)


def chip_groups(value):
    half = value.shape[0] // 2
    along_x, along_y = swap(value, 2), swap(value, 4)
    diagonal = [swap(along_x[:half], 4), swap(along_y[half:], 2)]
    groups = [[value], [along_x], [along_y], diagonal]
    return [(group, [swap(piece, 1) for piece in group]) for group in groups]


def project_kernel(place_ref, attn_ref, *refs):
    out_ref, joined, stage = refs[-3:]
    pieces = refs[:-3]
    columns = pieces[0].shape[0]
    attn = attn_ref[...]
    blocks = [pieces[0], pieces[1], pieces[2], pieces[3], pieces[4], pieces[5], None, None]
    for k, block in enumerate(blocks):
        if block is None:
            low, high = pieces[2 * k - 6], pieces[2 * k - 5]
            joined[: low.shape[0]] = low[...]
            joined[low.shape[0] :] = high[...]
            block = joined
        terms = lax.dot_general(
            attn, block[...], (((1,), (1,)), ((), ())), preferred_element_type=jnp.float32
        )
        stage[place_ref[0] ^ k, :, :columns] = terms
    for j in range(stage.shape[0]):
        out_ref[:, j * columns : (j + 1) * columns] = stage[j, :, :columns].astype(out_ref.dtype)


def project_part(place, attn_out, groups):
    rows, depth = attn_out.shape
    pieces = [piece for pair in groups for group in pair for piece in group]
    columns = pieces[0].shape[0]
    return pl.pallas_call(
        project_kernel,
        in_specs=[pl.BlockSpec(memory_space=pltpu.SMEM)]
        + [pl.BlockSpec(memory_space=pltpu.VMEM)] * (1 + len(pieces)),
        out_specs=pl.BlockSpec(memory_space=pltpu.VMEM),
        out_shape=jax.ShapeDtypeStruct((rows, 8 * columns), jnp.bfloat16),
        scratch_shapes=[
            pltpu.VMEM((columns, depth), jnp.bfloat16),
            pltpu.VMEM((8, rows, -(-columns // 128) * 128), jnp.float32),
        ],
        compiler_params=pltpu.CompilerParams(vmem_limit_bytes=VMEM_LIMIT),
        cost_estimate=pl.CostEstimate(
            flops=16 * rows * depth * columns,
            bytes_accessed=2 * depth * (rows + 8 * columns),
            transcendentals=0,
        ),
        name="project",
    )(place, attn_out, *pieces)


def gate_up_kernel(parts, scale_ref, gain_ref, chosen_ref, *refs):
    hidden_ref, peak_ref, rows = refs[-3:]
    weights, pieces = refs[-3 - 2 * parts : -3], refs[: -3 - 2 * parts]
    per_part = len(pieces) // parts
    capacity = chosen_ref.shape[1]
    step = rows.shape[2]

    @pl.when(pl.program_id(0) == 0)
    def _():
        source = 0
        for p in range(per_part):
            for i in range(pieces[p].shape[0]):
                span = slice(source * capacity, (source + 1) * capacity)
                picked = [
                    jnp.dot(
                        chosen_ref[source],
                        pieces[c * per_part + p][i],
                        preferred_element_type=jnp.float32,
                    )
                    for c in range(parts)
                ]
                squares = sum(jnp.sum(x * x, axis=1, keepdims=True) for x in picked)
                root = lax.rsqrt(squares / (parts * step) + 1e-06)
                for c, x in enumerate(picked):
                    x = jnp.clip(x * root * gain_ref[c], -FP8_LIMIT, FP8_LIMIT)
                    rows[c, span] = x.astype(rows.dtype)
                source += 1

    def product(side):
        return sum(
            jnp.dot(
                rows[c],
                weights[2 * c + side][0].reshape(step, -1),
                preferred_element_type=jnp.float32,
            )
            for c in range(parts)
        )

    gate, up = product(0) * scale_ref[0], product(1) * scale_ref[0]
    hidden = gate / (1.0 + jnp.exp(-gate)) * up
    scaled = jnp.clip(hidden * scale_ref[1], -FP8_LIMIT, FP8_LIMIT)
    hidden_ref[...] = scaled.astype(hidden_ref.dtype)
    peak = jnp.max(jnp.abs(hidden), axis=0, keepdims=True)
    peak_ref[...] = jnp.broadcast_to(peak, peak_ref.shape)


def gate_up(scales, gains, chosen, pieces, w_gate, w_up):
    sources, capacity, tokens = chosen.shape
    parts, _, step = gains.shape
    owners, columns, hidden = w_gate.shape[1], w_gate.shape[3], w_gate.shape[-1]
    tile = min(256, hidden)
    rows = sources * capacity
    once = pl.Buffered(buffer_count=1)
    whole = lambda a: pl.BlockSpec(a.shape, lambda n: (0,) * a.ndim, pipeline_mode=once)
    column = lambda height: pl.BlockSpec((height, tile), lambda n: (0, n))
    weight = lambda c: pl.BlockSpec((1, owners, None, columns, tile), lambda n: (0, 0, c, 0, n))
    return pl.pallas_call(
        functools.partial(gate_up_kernel, parts),
        grid=(hidden // tile,),
        in_specs=[pl.BlockSpec(memory_space=pltpu.SMEM), whole(gains), whole(chosen)]
        + [whole(p) for p in pieces]
        + [weight(c) for c in range(parts) for _ in range(2)],
        out_specs=[column(rows), column(8)],
        out_shape=[
            jax.ShapeDtypeStruct((rows, hidden), jnp.bfloat16),
            jax.ShapeDtypeStruct((8, hidden), jnp.float32),
        ],
        scratch_shapes=[pltpu.VMEM((parts, rows, step), jnp.bfloat16)],
        compiler_params=pltpu.CompilerParams(vmem_limit_bytes=VMEM_LIMIT),
        cost_estimate=pl.CostEstimate(
            flops=2 * rows * parts * step * (2 * hidden + tokens),
            bytes_accessed=2 * parts * step * (2 * hidden + sources * tokens),
            transcendentals=rows * hidden,
        ),
        name="gate_up",
    )(scales, gains, chosen, *pieces, *([w_gate, w_up] * parts))


def down_kernel(hidden_ref, down_w, factor_ref, spread_ref, own_ref, other_ref):
    sources, tokens, capacity = spread_ref.shape
    terms = jnp.dot(hidden_ref[...], down_w[0], preferred_element_type=jnp.float32)
    terms = (terms * factor_ref[...]).astype(jnp.bfloat16)
    half = sources // 2
    for source in range(sources):
        spread = jnp.dot(
            spread_ref[source],
            terms[source * capacity : (source + 1) * capacity],
            preferred_element_type=jnp.float32,
        ).astype(jnp.bfloat16)
        if source < half:
            own_ref[source] = spread
        else:
            other_ref[source - half] = spread


def down(hidden_q, w_down, factor, spread, c, step):
    rows, hidden = hidden_q.shape
    sources, tokens, capacity = spread.shape
    tile = step // 2 if step % 256 == 0 else step
    tiles = step // tile
    whole = lambda shape: pl.BlockSpec(shape, lambda j: (0,) * len(shape))
    return pl.pallas_call(
        down_kernel,
        grid=(tiles,),
        in_specs=[
            whole(hidden_q.shape),
            pl.BlockSpec((1, hidden, tile), lambda j: (0, 0, c * tiles + j)),
            whole(factor.shape),
            whole(spread.shape),
        ],
        out_specs=[pl.BlockSpec((sources // 2, tokens, tile), lambda j: (0, 0, j))] * 2,
        out_shape=[jax.ShapeDtypeStruct((sources // 2, tokens, step), jnp.bfloat16)] * 2,
        compiler_params=pltpu.CompilerParams(vmem_limit_bytes=VMEM_LIMIT),
        cost_estimate=pl.CostEstimate(
            flops=2 * rows * step * (hidden + tokens),
            bytes_accessed=2 * step * (hidden + sources * tokens),
            transcendentals=0,
        ),
        name="down",
    )(hidden_q, w_down, factor, spread)


def add(*terms):
    return sum(t.astype(jnp.float32) for t in terms).astype(jnp.bfloat16)


def gather_plan(
    attn_out,
    out_weight,
    residual,
    norm_gain,
    expert_ids,
    route_weight,
    w_gate,
    w_up,
    w_down,
    top_x,
    top_h,
    capacity,
):
    owners, layers = lax.axis_size("dp"), lax.axis_size("tensor")
    experts = owners * layers
    local_rows, width = residual.shape
    half, step = layers // 2, width // CHUNKS
    columns = step // owners

    weight_rows = out_weight.T.reshape(CHUNKS, columns, -1)
    blocks = [chip_groups(weight_rows[c]) for c in range(CHUNKS)]
    first = blocks[0][1][0][0]
    first, expert_ids = lax.optimization_barrier((first, expert_ids))
    blocks[0][1][0][0] = first
    weight = expert_weights(expert_ids, route_weight, experts)
    blocks[-1], weight = lax.optimization_barrier((blocks[-1], weight))

    named = weight > 0.0
    earlier = jnp.triu(jnp.ones((local_rows, local_rows), jnp.bfloat16), 1)
    slot = lax.dot_general(
        named.astype(jnp.bfloat16),
        earlier,
        (((2,), (0,)), ((), ())),
        preferred_element_type=jnp.float32,
    ).astype(jnp.int32)
    chosen = (
        slot[:, :, None, :] == jnp.arange(capacity, dtype=jnp.int32)[:, None]
    ) & named[:, :, None, :]
    factor = jnp.sum(jnp.where(chosen, weight[:, :, None, :], 0.0), axis=3)
    factor = factor.reshape(4, 2 * layers * capacity, 1) * (top_h / FP8_LIMIT)
    choice = chosen.astype(jnp.bfloat16).reshape(4, 2 * layers, capacity, local_rows)
    spread = choice.transpose(0, 1, 3, 2)
    scales = jnp.stack([top_x / FP8_LIMIT, FP8_LIMIT / top_h])

    split = lambda value: value.reshape(-1, owners, CHUNKS, columns)
    parts = lambda value, c: split(value)[:, :, c].reshape(-1, step)
    place = lax.axis_index("dp")[None]
    stream, tokens = [], []
    for c in range(CHUNKS):
        terms = project_part(place, attn_out, blocks[c])
        total = lax.psum_scatter(terms, "tensor", scatter_dimension=0, tiled=True)
        stream.append(parts(residual, c).astype(jnp.float32) + total.astype(jnp.float32))
        tokens.append(chip_groups(along_tensor(stream[c].astype(jnp.bfloat16))))
    squares = sum(jnp.sum(part * part, axis=1) for part in stream)
    root = lax.rsqrt(squares / width + 1e-06)
    gains = [parts(norm_gain, c) for c in range(CHUNKS)]
    peak_x = jnp.max(
        jnp.stack([jnp.max(jnp.abs(s * root[:, None] * g)) for s, g in zip(stream, gains)])
    )
    gains = jnp.stack(gains) * (FP8_LIMIT / top_x)

    gate_rows = w_gate.reshape(1, owners, CHUNKS, columns, -1)
    up_rows = w_up.reshape(1, owners, CHUNKS, columns, -1)
    hidden = []
    for r in range(4):
        pieces = [piece for part in tokens for side in part[r] for piece in side]
        hidden.append(gate_up(scales, gains, choice[r], pieces, gate_rows, up_rows))
    peak_h = jnp.max(jnp.stack([jnp.max(peaks) for _, peaks in hidden]))

    mixture = []
    for c in range(CHUNKS):
        to = []
        for r in range(4):
            kept, given = down(hidden[r][0], w_down, factor[r], spread[r], c, step)
            taken = swap(given, 1)
            to.append([add(kept[:half], taken[:half]), add(kept[half:], taken[half:])])
        over_x, over_y = swap(to[3][0], 2), swap(to[3][1], 4)
        low = add(to[0][0], swap(to[1][0], 2), swap(add(to[2][0], over_x), 4))
        high = add(to[0][1], swap(add(to[1][1], over_y), 2), swap(to[2][1], 4))
        mixed = jnp.concatenate([low, high]).reshape(layers * local_rows, step)
        mixture.append(lax.psum_scatter(mixed, "tensor", scatter_dimension=0, tiled=True))
    stream = jnp.stack([s.reshape(local_rows, owners, columns) for s in stream], axis=2)
    stream = stream.reshape(local_rows, width)
    layer_out = stream + jnp.concatenate(mixture, axis=1).astype(jnp.float32)
    return layer_out.astype(jnp.bfloat16), peak_x, peak_h


def body(
    attn_out,
    out_weight,
    residual,
    norm_gain,
    expert_ids,
    route_weight,
    w_gate,
    w_up,
    w_down,
    history_x,
    history_h,
):
    experts = lax.axis_size("dp") * lax.axis_size("tensor")
    local_rows, top_count = expert_ids.shape
    capacity = max(2, 3 * local_rows * top_count // (2 * experts))
    top_x, top_h = jnp.max(history_x), jnp.max(history_h)
    gathers = lax.axis_size("dp") == 8 and local_rows < 4 * capacity
    plan = gather_plan if gathers else exchange_plan
    layer_out, peak_x, peak_h = plan(
        attn_out,
        out_weight,
        residual,
        norm_gain,
        expert_ids,
        route_weight,
        w_gate,
        w_up,
        w_down,
        top_x,
        top_h,
        capacity,
    )
    peaks = peaks_over_all(jnp.stack([peak_x, peak_h]))
    new_history_x = jnp.concatenate([peaks[:1], history_x[:-1]])
    new_history_h = jnp.concatenate([peaks[1:], history_h[:-1]])
    return (layer_out, new_history_x, new_history_h)


def solution(mesh):
    in_specs = (
        P("dp", "tensor"),
        P("tensor", "dp"),
        P(AXES, None),
        P(),
        P(AXES, None),
        P(AXES, None),
        P(AXES, None, None),
        P(AXES, None, None),
        P(AXES, None, None),
        P(),
        P(),
    )
    out_specs = (P(AXES, None), P(), P())
    return jax.shard_map(body, mesh=mesh, in_specs=in_specs, out_specs=out_specs, check_vma=False)
```

```python
import functools

import jax
import jax.numpy as jnp
from jax import lax
from jax.experimental import pallas as pl
from jax.experimental.pallas import tpu as pltpu
from jax.sharding import PartitionSpec as P

FP8_LIMIT = 448.0
AXES = ("dp", "tensor")
CHUNKS = 2
VMEM_LIMIT = 48 * 2**20


def project(attn_out, out_weight):
    head_terms = jnp.dot(
        attn_out,
        lax.all_gather(out_weight, "dp", axis=1, tiled=True),
        preferred_element_type=jnp.float32,
    )
    return lax.psum_scatter(
        head_terms.astype(jnp.bfloat16), "tensor", scatter_dimension=0, tiled=True
    ).astype(jnp.float32)


def peaks_over_all(peaks):
    for axis in AXES:
        count = lax.axis_size(axis)
        shift = 1
        while shift < count:
            pairs = [(i, (i + shift) % count) for i in range(count)]
            peaks = jnp.maximum(peaks, lax.ppermute(peaks, axis, pairs))
            shift *= 2
    return peaks


def slots_of(ids, experts, capacity):
    flat_ids = ids.reshape(-1)
    onehot = (flat_ids[:, None] == jnp.arange(experts, dtype=jnp.int32)[None, :]).astype(jnp.int32)
    before = jnp.cumsum(onehot, axis=0) - onehot
    return flat_ids * capacity + jnp.sum(before * onehot, axis=-1)


def exchange_plan(
    attn_out,
    out_weight,
    residual,
    norm_gain,
    expert_ids,
    route_weight,
    w_gate,
    w_up,
    w_down,
    top_x,
    top_h,
    capacity,
):
    experts = lax.axis_size("dp") * lax.axis_size("tensor")
    inv_x, inv_h, scale_h = top_x / FP8_LIMIT, top_h / FP8_LIMIT, FP8_LIMIT / top_h
    local_rows, width = residual.shape
    top_count = expert_ids.shape[1]
    stream = residual.astype(jnp.float32) + project(attn_out, out_weight)
    normed = (
        stream * lax.rsqrt(jnp.mean(stream * stream, axis=-1, keepdims=True) + 1e-06) * norm_gain
    )
    quantized = jnp.clip(normed * (FP8_LIMIT / top_x), -FP8_LIMIT, FP8_LIMIT).astype(jnp.bfloat16)
    position = slots_of(expert_ids, experts, capacity)
    matches = (
        position.reshape(local_rows, top_count)[:, :, None]
        == jnp.arange(experts * capacity, dtype=jnp.int32)[None, None, :]
    )
    placing = jnp.sum(matches.astype(jnp.int32), axis=1).astype(jnp.bfloat16)
    outgoing = lax.dot_general(
        placing, quantized, (((0,), (0,)), ((), ())), preferred_element_type=jnp.float32
    )
    outgoing = outgoing.astype(jnp.bfloat16).reshape(experts, capacity, width)
    token_block = lax.all_to_all(outgoing, AXES, split_axis=0, concat_axis=0, tiled=True)
    flat_rows = token_block.reshape(-1, width)
    gate = jnp.dot(flat_rows, w_gate[0], preferred_element_type=jnp.float32) * inv_x
    upper = jnp.dot(flat_rows, w_up[0], preferred_element_type=jnp.float32) * inv_x
    hidden = jax.nn.silu(gate) * upper
    hidden_q = jnp.clip(hidden * scale_h, -FP8_LIMIT, FP8_LIMIT).astype(jnp.bfloat16)
    expert_out = (jnp.dot(hidden_q, w_down[0], preferred_element_type=jnp.float32) * inv_h).astype(
        jnp.bfloat16
    )
    returned = lax.all_to_all(
        expert_out.reshape(experts, capacity, width), AXES, split_axis=0, concat_axis=0, tiled=True
    )
    picked = returned.reshape(-1, width)[position].reshape(local_rows, top_count, width)
    mixture = jnp.sum(picked.astype(jnp.float32) * route_weight[:, :, None], axis=1)
    peaks = jnp.max(jnp.abs(normed)), jnp.max(jnp.abs(hidden))
    return (stream + mixture).astype(jnp.bfloat16), *peaks


def swap(value, bits):
    count = lax.axis_size("dp")
    return lax.ppermute(value, "dp", [(i, i ^ bits) for i in range(count)])


def from_all(value):
    count = lax.axis_size("tensor")
    parts = [value]
    for shift in range(1, count):
        pairs = [(i, (i + shift) % count) for i in range(count)]
        parts.append(lax.ppermute(value, "tensor", pairs))
    order = (lax.axis_index("tensor") - jnp.arange(count)) % count
    values = jnp.stack(parts)[order][None]
    bit = 1
    while bit < lax.axis_size("dp"):
        values = jnp.concatenate([values, swap(values, bit)])
        bit *= 2
    return values


def along_tensor(value):
    count, here = lax.axis_size("tensor"), lax.axis_index("tensor")
    blocks = jnp.zeros((count,) + value.shape, value.dtype)
    blocks = lax.dynamic_update_index_in_dim(blocks, value, here, 0)
    below, above = [value], [value]
    for hop in range(1, count):
        up = [(i, i + 1) for i in range(hop - 1, count - 1)]
        below.append(lax.ppermute(below[-1], "tensor", up))
        above.append(lax.ppermute(above[-1], "tensor", [(count - 1 - i, count - 1 - j) for i, j in up]))
    for hop in range(1, count):
        block = jnp.where(here >= hop, below[hop], above[count - hop])
        blocks = lax.dynamic_update_index_in_dim(blocks, block, (here - hop) % count, 0)
    return blocks


def expert_weights(expert_ids, route_weight, experts):
    names = jnp.arange(experts, dtype=jnp.int32)[:, None, None]
    table = jnp.sum(jnp.where(expert_ids[None] == names, route_weight[None], 0.0), axis=2)
    mine = lax.axis_index("dp") * lax.axis_size("tensor") + lax.axis_index("tensor")
    return lax.dynamic_index_in_dim(from_all(table), mine, axis=2, keepdims=False)


def neighbours(value):
    return swap(value, 2), swap(value, 4)


def diagonal(along_x, along_y):
    half = along_x.shape[0] // 2
    return [swap(along_x[:half], 4), swap(along_y[half:], 2)]


def both_cores(group):
    return group + [swap(piece, 1) for piece in group]


def tie(*values):
    return lax.optimization_barrier(values)


def project_kernel(place_ref, attn_ref, *refs):
    out_ref, joined, stage = refs[-3:]
    pieces = refs[:-3]
    columns = pieces[0].shape[0]
    attn = attn_ref[...]
    blocks = [pieces[0], pieces[1], pieces[2], pieces[3], pieces[4], pieces[5], None, None]
    for k, block in enumerate(blocks):
        if block is None:
            low, high = pieces[2 * k - 6], pieces[2 * k - 5]
            joined[: low.shape[0]] = low[...]
            joined[low.shape[0] :] = high[...]
            block = joined
        terms = lax.dot_general(
            attn, block[...], (((1,), (1,)), ((), ())), preferred_element_type=jnp.float32
        )
        stage[place_ref[0] ^ k, :, :columns] = terms
    for j in range(stage.shape[0]):
        out_ref[:, j * columns : (j + 1) * columns] = stage[j, :, :columns].astype(out_ref.dtype)


def project_part(place, attn_out, groups):
    rows, depth = attn_out.shape
    pieces = [piece for group in groups for piece in group]
    columns = pieces[0].shape[0]
    return pl.pallas_call(
        project_kernel,
        in_specs=[pl.BlockSpec(memory_space=pltpu.SMEM)]
        + [pl.BlockSpec(memory_space=pltpu.VMEM)] * (1 + len(pieces)),
        out_specs=pl.BlockSpec(memory_space=pltpu.VMEM),
        out_shape=jax.ShapeDtypeStruct((rows, 8 * columns), jnp.bfloat16),
        scratch_shapes=[
            pltpu.VMEM((columns, depth), jnp.bfloat16),
            pltpu.VMEM((8, rows, -(-columns // 128) * 128), jnp.float32),
        ],
        compiler_params=pltpu.CompilerParams(vmem_limit_bytes=VMEM_LIMIT),
        cost_estimate=pl.CostEstimate(
            flops=16 * rows * depth * columns,
            bytes_accessed=2 * depth * (rows + 8 * columns),
            transcendentals=0,
        ),
        name="project",
    )(place, attn_out, *pieces)


def gate_up_kernel(parts, scale_ref, gain_ref, chosen_ref, *refs):
    hidden_ref, peak_ref, rows = refs[-3:]
    weights, pieces = refs[-3 - 2 * parts : -3], refs[: -3 - 2 * parts]
    per_part = len(pieces) // parts
    capacity = chosen_ref.shape[1]
    step = rows.shape[2]

    @pl.when(pl.program_id(0) == 0)
    def _():
        source = 0
        for p in range(per_part):
            for i in range(pieces[p].shape[0]):
                span = slice(source * capacity, (source + 1) * capacity)
                picked = [
                    jnp.dot(
                        chosen_ref[source],
                        pieces[c * per_part + p][i],
                        preferred_element_type=jnp.float32,
                    )
                    for c in range(parts)
                ]
                squares = sum(jnp.sum(x * x, axis=1, keepdims=True) for x in picked)
                root = lax.rsqrt(squares / (parts * step) + 1e-06)
                for c, x in enumerate(picked):
                    x = jnp.clip(x * root * gain_ref[c], -FP8_LIMIT, FP8_LIMIT)
                    rows[c, span] = x.astype(rows.dtype)
                source += 1

    def product(side):
        return sum(
            jnp.dot(
                rows[c],
                weights[2 * c + side][0].reshape(step, -1),
                preferred_element_type=jnp.float32,
            )
            for c in range(parts)
        )

    gate, up = product(0) * scale_ref[0], product(1) * scale_ref[0]
    hidden = gate / (1.0 + jnp.exp(-gate)) * up
    scaled = jnp.clip(hidden * scale_ref[1], -FP8_LIMIT, FP8_LIMIT)
    hidden_ref[...] = scaled.astype(hidden_ref.dtype)
    peak = jnp.broadcast_to(jnp.max(jnp.abs(hidden)), peak_ref.shape)
    first = pl.program_id(0) == 0
    peak_ref[...] = jnp.where(first, peak, jnp.maximum(peak_ref[...], peak))


def gate_up(scales, gains, chosen, pieces, w_gate, w_up):
    sources, capacity, tokens = chosen.shape
    parts, _, step = gains.shape
    owners, columns, hidden = w_gate.shape[1], w_gate.shape[3], w_gate.shape[-1]
    tile = min(256, hidden)
    rows = sources * capacity
    once = pl.Buffered(buffer_count=1)
    whole = lambda a: pl.BlockSpec(a.shape, lambda n: (0,) * a.ndim, pipeline_mode=once)
    column = lambda height: pl.BlockSpec((height, tile), lambda n: (0, n))
    weight = lambda c: pl.BlockSpec((1, owners, None, columns, tile), lambda n: (0, 0, c, 0, n))
    return pl.pallas_call(
        functools.partial(gate_up_kernel, parts),
        grid=(hidden // tile,),
        in_specs=[pl.BlockSpec(memory_space=pltpu.SMEM), whole(gains), whole(chosen)]
        + [whole(p) for p in pieces]
        + [weight(c) for c in range(parts) for _ in range(2)],
        out_specs=[column(rows), pl.BlockSpec((8, 128), lambda n: (0, 0))],
        out_shape=[
            jax.ShapeDtypeStruct((rows, hidden), jnp.bfloat16),
            jax.ShapeDtypeStruct((8, 128), jnp.float32),
        ],
        scratch_shapes=[pltpu.VMEM((parts, rows, step), jnp.bfloat16)],
        compiler_params=pltpu.CompilerParams(vmem_limit_bytes=VMEM_LIMIT),
        cost_estimate=pl.CostEstimate(
            flops=2 * rows * parts * step * (2 * hidden + tokens),
            bytes_accessed=2 * parts * step * (2 * hidden + sources * tokens),
            transcendentals=rows * hidden,
        ),
        name="gate_up",
    )(scales, gains, chosen, *pieces, *([w_gate, w_up] * parts))


def down_kernel(hidden_ref, down_w, factor_ref, spread_ref, own_ref, other_ref):
    sources, tokens, capacity = spread_ref.shape
    terms = jnp.dot(hidden_ref[...], down_w[0], preferred_element_type=jnp.float32)
    terms = (terms * factor_ref[...]).astype(jnp.bfloat16)
    half = sources // 2
    for source in range(sources):
        spread = jnp.dot(
            spread_ref[source],
            terms[source * capacity : (source + 1) * capacity],
            preferred_element_type=jnp.float32,
        ).astype(jnp.bfloat16)
        if source < half:
            own_ref[source] = spread
        else:
            other_ref[source - half] = spread


def down(hidden_q, w_down, factor, spread, c, step):
    rows, hidden = hidden_q.shape
    sources, tokens, capacity = spread.shape
    tile = step // 2 if step % 256 == 0 else step
    tiles = step // tile
    whole = lambda shape: pl.BlockSpec(shape, lambda j: (0,) * len(shape))
    return pl.pallas_call(
        down_kernel,
        grid=(tiles,),
        in_specs=[
            whole(hidden_q.shape),
            pl.BlockSpec((1, hidden, tile), lambda j: (0, 0, c * tiles + j)),
            whole(factor.shape),
            whole(spread.shape),
        ],
        out_specs=[pl.BlockSpec((sources // 2, tokens, tile), lambda j: (0, 0, j))] * 2,
        out_shape=[jax.ShapeDtypeStruct((sources // 2, tokens, step), jnp.bfloat16)] * 2,
        compiler_params=pltpu.CompilerParams(vmem_limit_bytes=VMEM_LIMIT),
        cost_estimate=pl.CostEstimate(
            flops=2 * rows * step * (hidden + tokens),
            bytes_accessed=2 * step * (hidden + sources * tokens),
            transcendentals=0,
        ),
        name="down",
    )(hidden_q, w_down, factor, spread)


def natural_kernel(columns, *refs):
    *parts, out_ref = refs
    for j in range(parts[0].shape[1] // columns):
        for c, part in enumerate(parts):
            place = (j * len(parts) + c) * columns
            out_ref[:, place : place + columns] = part[:, j * columns : (j + 1) * columns]


def natural(parts, columns):
    rows, step = parts[0].shape
    return pl.pallas_call(
        functools.partial(natural_kernel, columns),
        out_shape=jax.ShapeDtypeStruct((rows, step * len(parts)), parts[0].dtype),
        compiler_params=pltpu.CompilerParams(vmem_limit_bytes=VMEM_LIMIT),
        name="natural",
    )(*parts)


def add(*terms):
    return sum(t.astype(jnp.float32) for t in terms).astype(jnp.bfloat16)


def gather_plan(
    attn_out,
    out_weight,
    residual,
    norm_gain,
    expert_ids,
    route_weight,
    w_gate,
    w_up,
    w_down,
    top_x,
    top_h,
    capacity,
):
    owners, layers = lax.axis_size("dp"), lax.axis_size("tensor")
    experts = owners * layers
    local_rows, width = residual.shape
    half, step = layers // 2, width // CHUNKS
    columns = step // owners

    split = lambda value: value.reshape(-1, owners, CHUNKS, columns)
    parts = lambda value, c: split(value)[:, :, c].reshape(-1, step)
    place = lax.axis_index("dp")[None]

    weight_rows = list(out_weight.T.reshape(CHUNKS, columns, -1))
    stream, sent = [], []
    for c in range(CHUNKS):
        along_x, along_y = neighbours(weight_rows[c])
        if c + 1 < CHUNKS:
            along_x, along_y, weight_rows[c + 1] = tie(along_x, along_y, weight_rows[c + 1])
        groups = [[weight_rows[c]], [along_x], [along_y], diagonal(along_x, along_y)]
        terms = project_part(place, attn_out, [both_cores(group) for group in groups])
        if c == 0:
            terms, expert_ids = tie(terms, expert_ids)
            weight = expert_weights(expert_ids, route_weight, experts)
        else:
            terms, sent[-1], weight = tie(terms, sent[-1], weight)
        total = lax.psum_scatter(terms, "tensor", scatter_dimension=0, tiled=True)
        stream.append(parts(residual, c).astype(jnp.float32) + total.astype(jnp.float32))
        sent.append(stream[c].astype(jnp.bfloat16))

    named = weight > 0.0
    earlier = jnp.triu(jnp.ones((local_rows, local_rows), jnp.bfloat16), 1)
    slot = lax.dot_general(
        named.astype(jnp.bfloat16),
        earlier,
        (((2,), (0,)), ((), ())),
        preferred_element_type=jnp.float32,
    ).astype(jnp.int32)
    chosen = (
        slot[:, :, None, :] == jnp.arange(capacity, dtype=jnp.int32)[:, None]
    ) & named[:, :, None, :]
    factor = jnp.sum(jnp.where(chosen, weight[:, :, None, :], 0.0), axis=3)
    factor = factor.reshape(4, 2 * layers * capacity, 1) * (top_h / FP8_LIMIT)
    choice = chosen.astype(jnp.bfloat16).reshape(4, 2 * layers, capacity, local_rows)
    spread = choice.transpose(0, 1, 3, 2)
    scales = jnp.stack([top_x / FP8_LIMIT, FP8_LIMIT / top_h])

    squares = sum(jnp.sum(part * part, axis=1) for part in stream)
    root = lax.rsqrt(squares / width + 1e-06)
    gains = [parts(norm_gain, c) for c in range(CHUNKS)]
    peak_x = jnp.max(
        jnp.stack([jnp.max(jnp.abs(s * root[:, None] * g)) for s, g in zip(stream, gains)])
    )
    gains = jnp.stack(gains) * (FP8_LIMIT / top_x)

    gate_rows = w_gate.reshape(1, owners, CHUNKS, columns, -1)
    up_rows = w_up.reshape(1, owners, CHUNKS, columns, -1)

    def hidden_of(r, tokens):
        pieces = [piece for part in tokens for piece in part]
        return gate_up(scales, gains, choice[r], pieces, gate_rows, up_rows)

    groups = [[] for _ in range(4)]
    own = along_tensor(sent[0])
    for c in range(CHUNKS):
        along_x, along_y = neighbours(own)
        groups[0].append(both_cores([own]))
        if c + 1 < CHUNKS:
            own = along_tensor(sent[c + 1])
            along_x, along_y, own = tie(along_x, along_y, own)
        else:
            hidden = [hidden_of(0, groups[0])]
            stream = natural(stream, columns)
            along_x, along_y, hidden[0], stream = tie(along_x, along_y, hidden[0], stream)
        groups[1].append(both_cores([along_x]))
        groups[2].append(both_cores([along_y]))
        across = diagonal(along_x, along_y)
        if c + 1 == CHUNKS:
            hidden += [hidden_of(1, groups[1]), hidden_of(2, groups[2])]
            across, hidden = tie(across, hidden)
        groups[3].append(both_cores(across))

    def outputs(r, c):
        kept, given = down(hidden[r][0], w_down, factor[r], spread[r], c, step)
        taken = swap(given, 1)
        return [(kept[:half], taken[:half]), (kept[half:], taken[half:])]

    summed = lambda r, c: [add(*terms) for terms in outputs(r, c)]
    to_x, to_y = summed(1, 0), summed(2, 0)
    groups[3], to_x, to_y = tie(groups[3], to_x, to_y)
    hidden.append(hidden_of(3, groups[3]))
    peak_h = jnp.max(jnp.stack([peaks for _, peaks in hidden]))
    mixture = []
    for c in range(CHUNKS):
        if c > 0:
            to_x, to_y = summed(1, c), summed(2, c)
        beyond, to_own = summed(3, c), outputs(0, c)
        over_x, over_y = swap(beyond[0], 2), swap(beyond[1], 4)
        low = add(*to_own[0], swap(to_x[0], 2), swap(add(to_y[0], over_x), 4))
        high = add(*to_own[1], swap(add(to_x[1], over_y), 2), swap(to_y[1], 4))
        mixed = jnp.concatenate([low, high]).reshape(layers * local_rows, step)
        mixture.append(lax.psum_scatter(mixed, "tensor", scatter_dimension=0, tiled=True))
    layer_out = stream + jnp.concatenate(mixture, axis=1).astype(jnp.float32)
    return layer_out.astype(jnp.bfloat16), peak_x, peak_h


def body(
    attn_out,
    out_weight,
    residual,
    norm_gain,
    expert_ids,
    route_weight,
    w_gate,
    w_up,
    w_down,
    history_x,
    history_h,
):
    experts = lax.axis_size("dp") * lax.axis_size("tensor")
    local_rows, top_count = expert_ids.shape
    capacity = max(2, 3 * local_rows * top_count // (2 * experts))
    top_x, top_h = jnp.max(history_x), jnp.max(history_h)
    gathers = lax.axis_size("dp") == 8 and local_rows < 4 * capacity
    plan = gather_plan if gathers else exchange_plan
    layer_out, peak_x, peak_h = plan(
        attn_out,
        out_weight,
        residual,
        norm_gain,
        expert_ids,
        route_weight,
        w_gate,
        w_up,
        w_down,
        top_x,
        top_h,
        capacity,
    )
    peaks = peaks_over_all(jnp.stack([peak_x, peak_h]))
    new_history_x = jnp.concatenate([peaks[:1], history_x[:-1]])
    new_history_h = jnp.concatenate([peaks[1:], history_h[:-1]])
    return (layer_out, new_history_x, new_history_h)


def solution(mesh):
    in_specs = (
        P("dp", "tensor"),
        P("tensor", "dp"),
        P(AXES, None),
        P(),
        P(AXES, None),
        P(AXES, None),
        P(AXES, None, None),
        P(AXES, None, None),
        P(AXES, None, None),
        P(),
        P(),
    )
    out_specs = (P(AXES, None), P(), P())
    return jax.shard_map(body, mesh=mesh, in_specs=in_specs, out_specs=out_specs, check_vma=False)
```

```python
import functools

import jax
import jax.numpy as jnp
from jax import lax
from jax.experimental import pallas as pl
from jax.experimental.pallas import tpu as pltpu
from jax.sharding import PartitionSpec as P

FP8_LIMIT = 448.0
AXES = ("dp", "tensor")
CHUNKS = 2
VMEM_LIMIT = 48 * 2**20
COST_SHARE = 16


def project(attn_out, out_weight):
    head_terms = jnp.dot(
        attn_out,
        lax.all_gather(out_weight, "dp", axis=1, tiled=True),
        preferred_element_type=jnp.float32,
    )
    return lax.psum_scatter(
        head_terms.astype(jnp.bfloat16), "tensor", scatter_dimension=0, tiled=True
    ).astype(jnp.float32)


def peaks_over_all(peaks):
    for axis in AXES:
        count = lax.axis_size(axis)
        shift = 1
        while shift < count:
            pairs = [(i, (i + shift) % count) for i in range(count)]
            peaks = jnp.maximum(peaks, lax.ppermute(peaks, axis, pairs))
            shift *= 2
    return peaks


def slots_of(ids, experts, capacity):
    flat_ids = ids.reshape(-1)
    onehot = (flat_ids[:, None] == jnp.arange(experts, dtype=jnp.int32)[None, :]).astype(jnp.int32)
    before = jnp.cumsum(onehot, axis=0) - onehot
    return flat_ids * capacity + jnp.sum(before * onehot, axis=-1)


def exchange_plan(
    attn_out,
    out_weight,
    residual,
    norm_gain,
    expert_ids,
    route_weight,
    w_gate,
    w_up,
    w_down,
    top_x,
    top_h,
    capacity,
):
    experts = lax.axis_size("dp") * lax.axis_size("tensor")
    inv_x, inv_h, scale_h = top_x / FP8_LIMIT, top_h / FP8_LIMIT, FP8_LIMIT / top_h
    local_rows, width = residual.shape
    top_count = expert_ids.shape[1]
    stream = residual.astype(jnp.float32) + project(attn_out, out_weight)
    normed = (
        stream * lax.rsqrt(jnp.mean(stream * stream, axis=-1, keepdims=True) + 1e-06) * norm_gain
    )
    quantized = jnp.clip(normed * (FP8_LIMIT / top_x), -FP8_LIMIT, FP8_LIMIT).astype(jnp.bfloat16)
    position = slots_of(expert_ids, experts, capacity)
    matches = (
        position.reshape(local_rows, top_count)[:, :, None]
        == jnp.arange(experts * capacity, dtype=jnp.int32)[None, None, :]
    )
    placing = jnp.sum(matches.astype(jnp.int32), axis=1).astype(jnp.bfloat16)
    outgoing = lax.dot_general(
        placing, quantized, (((0,), (0,)), ((), ())), preferred_element_type=jnp.float32
    )
    outgoing = outgoing.astype(jnp.bfloat16).reshape(experts, capacity, width)
    token_block = lax.all_to_all(outgoing, AXES, split_axis=0, concat_axis=0, tiled=True)
    flat_rows = token_block.reshape(-1, width)
    gate = jnp.dot(flat_rows, w_gate[0], preferred_element_type=jnp.float32) * inv_x
    upper = jnp.dot(flat_rows, w_up[0], preferred_element_type=jnp.float32) * inv_x
    hidden = jax.nn.silu(gate) * upper
    hidden_q = jnp.clip(hidden * scale_h, -FP8_LIMIT, FP8_LIMIT).astype(jnp.bfloat16)
    expert_out = (jnp.dot(hidden_q, w_down[0], preferred_element_type=jnp.float32) * inv_h).astype(
        jnp.bfloat16
    )
    returned = lax.all_to_all(
        expert_out.reshape(experts, capacity, width), AXES, split_axis=0, concat_axis=0, tiled=True
    )
    picked = returned.reshape(-1, width)[position].reshape(local_rows, top_count, width)
    mixture = jnp.sum(picked.astype(jnp.float32) * route_weight[:, :, None], axis=1)
    peaks = jnp.max(jnp.abs(normed)), jnp.max(jnp.abs(hidden))
    return (stream + mixture).astype(jnp.bfloat16), *peaks


def cost(flops, bytes_accessed):
    return pl.CostEstimate(
        flops=flops // COST_SHARE, bytes_accessed=bytes_accessed // COST_SHARE, transcendentals=0
    )


def swap(value, bits):
    count = lax.axis_size("dp")
    return lax.ppermute(value, "dp", [(i, i ^ bits) for i in range(count)])


def along_tensor(value):
    count, here = lax.axis_size("tensor"), lax.axis_index("tensor")
    blocks = jnp.zeros((count,) + value.shape, value.dtype)
    blocks = lax.dynamic_update_index_in_dim(blocks, value, here, 0)
    below, above = [value], [value]
    for hop in range(1, count):
        up = [(i, i + 1) for i in range(hop - 1, count - 1)]
        below.append(lax.ppermute(below[-1], "tensor", up))
        above.append(lax.ppermute(above[-1], "tensor", [(count - 1 - i, count - 1 - j) for i, j in up]))
    for hop in range(1, count):
        block = jnp.where(here >= hop, below[hop], above[count - hop])
        blocks = lax.dynamic_update_index_in_dim(blocks, block, (here - hop) % count, 0)
    return blocks


def chip_table(expert_ids, route_weight, experts):
    names = jnp.arange(experts, dtype=jnp.int32)[:, None, None]
    table = jnp.sum(jnp.where(expert_ids[None] == names, route_weight[None], 0.0), axis=2)
    count = lax.axis_size("tensor")
    parts = [table]
    for shift in range(1, count):
        pairs = [(i, (i + shift) % count) for i in range(count)]
        parts.append(lax.ppermute(table, "tensor", pairs))
    order = (lax.axis_index("tensor") - jnp.arange(count)) % count
    table = jnp.stack(parts)[order][None]
    return jnp.concatenate([table, swap(table, 1)])


def expert_weights(table):
    for bit in (2, 4):
        table = jnp.concatenate([table, swap(table, bit)])
    mine = lax.axis_index("dp") * lax.axis_size("tensor") + lax.axis_index("tensor")
    return lax.dynamic_index_in_dim(table, mine, axis=2, keepdims=False)


def neighbours(value):
    return swap(value, 2), swap(value, 4)


def diagonal(along_x, along_y):
    half = along_x.shape[0] // 2
    return [swap(along_x[:half], 4), swap(along_y[half:], 2)]


def both_cores(group):
    return group + [swap(piece, 1) for piece in group]


def tie(*values):
    return lax.optimization_barrier(values)


def project_kernel(place_ref, attn_ref, *refs):
    out_ref, joined, stage = refs[-3:]
    pieces = refs[:-3]
    columns = pieces[0].shape[0]
    attn = attn_ref[...]
    blocks = [pieces[0], pieces[1], pieces[2], pieces[3], pieces[4], pieces[5], None, None]
    for k, block in enumerate(blocks):
        if block is None:
            low, high = pieces[2 * k - 6], pieces[2 * k - 5]
            joined[: low.shape[0]] = low[...]
            joined[low.shape[0] :] = high[...]
            block = joined
        terms = lax.dot_general(
            attn, block[...], (((1,), (1,)), ((), ())), preferred_element_type=jnp.float32
        )
        stage[place_ref[0] ^ k, :, :columns] = terms
    for j in range(stage.shape[0]):
        out_ref[:, j * columns : (j + 1) * columns] = stage[j, :, :columns].astype(out_ref.dtype)


def project_part(place, attn_out, groups):
    rows, depth = attn_out.shape
    pieces = [piece for group in groups for piece in group]
    columns = pieces[0].shape[0]
    return pl.pallas_call(
        project_kernel,
        in_specs=[pl.BlockSpec(memory_space=pltpu.SMEM)]
        + [pl.BlockSpec(memory_space=pltpu.VMEM)] * (1 + len(pieces)),
        out_specs=pl.BlockSpec(memory_space=pltpu.VMEM),
        out_shape=jax.ShapeDtypeStruct((rows, 8 * columns), jnp.bfloat16),
        scratch_shapes=[
            pltpu.VMEM((columns, depth), jnp.bfloat16),
            pltpu.VMEM((8, rows, -(-columns // 128) * 128), jnp.float32),
        ],
        compiler_params=pltpu.CompilerParams(vmem_limit_bytes=VMEM_LIMIT),
        cost_estimate=cost(16 * rows * depth * columns, 2 * depth * (rows + 8 * columns)),
        name="project",
    )(place, attn_out, *pieces)


def gate_up_kernel(parts, scale_ref, gain_ref, chosen_ref, *refs):
    hidden_ref, peak_ref, rows = refs[-3:]
    weights, pieces = refs[-3 - 2 * parts : -3], refs[: -3 - 2 * parts]
    per_part = len(pieces) // parts
    capacity = chosen_ref.shape[1]
    step = rows.shape[2]

    @pl.when(pl.program_id(0) == 0)
    def _():
        source = 0
        for p in range(per_part):
            for i in range(pieces[p].shape[0]):
                span = slice(source * capacity, (source + 1) * capacity)
                picked = [
                    jnp.dot(
                        chosen_ref[source],
                        pieces[c * per_part + p][i],
                        preferred_element_type=jnp.float32,
                    )
                    for c in range(parts)
                ]
                squares = sum(jnp.sum(x * x, axis=1, keepdims=True) for x in picked)
                root = lax.rsqrt(squares / (parts * step) + 1e-06)
                for c, x in enumerate(picked):
                    x = jnp.clip(x * root * gain_ref[c], -FP8_LIMIT, FP8_LIMIT)
                    rows[c, span] = x.astype(rows.dtype)
                source += 1

    def product(side):
        return sum(
            jnp.dot(
                rows[c],
                weights[2 * c + side][0].reshape(step, -1),
                preferred_element_type=jnp.float32,
            )
            for c in range(parts)
        )

    gate, up = product(0) * scale_ref[0], product(1) * scale_ref[0]
    hidden = gate / (1.0 + jnp.exp(-gate)) * up
    scaled = jnp.clip(hidden * scale_ref[1], -FP8_LIMIT, FP8_LIMIT)
    hidden_ref[...] = scaled.astype(hidden_ref.dtype)
    peak = jnp.broadcast_to(jnp.max(jnp.abs(hidden)), peak_ref.shape)
    first = pl.program_id(0) == 0
    peak_ref[...] = jnp.where(first, peak, jnp.maximum(peak_ref[...], peak))


def gate_up(scales, gains, chosen, pieces, w_gate, w_up):
    sources, capacity, tokens = chosen.shape
    parts, _, step = gains.shape
    owners, columns, hidden = w_gate.shape[1], w_gate.shape[3], w_gate.shape[-1]
    tile = min(256, hidden)
    rows = sources * capacity
    once = pl.Buffered(buffer_count=1)
    whole = lambda a: pl.BlockSpec(a.shape, lambda n: (0,) * a.ndim, pipeline_mode=once)
    column = lambda height: pl.BlockSpec((height, tile), lambda n: (0, n))
    weight = lambda c: pl.BlockSpec((1, owners, None, columns, tile), lambda n: (0, 0, c, 0, n))
    return pl.pallas_call(
        functools.partial(gate_up_kernel, parts),
        grid=(hidden // tile,),
        in_specs=[pl.BlockSpec(memory_space=pltpu.SMEM), whole(gains), whole(chosen)]
        + [whole(p) for p in pieces]
        + [weight(c) for c in range(parts) for _ in range(2)],
        out_specs=[column(rows), pl.BlockSpec((8, 128), lambda n: (0, 0))],
        out_shape=[
            jax.ShapeDtypeStruct((rows, hidden), jnp.bfloat16),
            jax.ShapeDtypeStruct((8, 128), jnp.float32),
        ],
        scratch_shapes=[pltpu.VMEM((parts, rows, step), jnp.bfloat16)],
        compiler_params=pltpu.CompilerParams(vmem_limit_bytes=VMEM_LIMIT),
        cost_estimate=cost(
            2 * rows * parts * step * (2 * hidden + tokens),
            2 * parts * step * (2 * hidden + sources * tokens),
        ),
        name="gate_up",
    )(scales, gains, chosen, *pieces, *([w_gate, w_up] * parts))


def down_kernel(hidden_ref, down_w, factor_ref, spread_ref, own_ref, other_ref):
    sources, tokens, capacity = spread_ref.shape
    terms = jnp.dot(hidden_ref[...], down_w[0], preferred_element_type=jnp.float32)
    terms = (terms * factor_ref[...]).astype(jnp.bfloat16)
    half = sources // 2
    for source in range(sources):
        spread = jnp.dot(
            spread_ref[source],
            terms[source * capacity : (source + 1) * capacity],
            preferred_element_type=jnp.float32,
        ).astype(jnp.bfloat16)
        if source < half:
            own_ref[source] = spread
        else:
            other_ref[source - half] = spread


def down(hidden_q, w_down, factor, spread, c, step):
    rows, hidden = hidden_q.shape
    sources, tokens, capacity = spread.shape
    tile = step // 2 if step % 256 == 0 else step
    tiles = step // tile
    whole = lambda shape: pl.BlockSpec(shape, lambda j: (0,) * len(shape))
    return pl.pallas_call(
        down_kernel,
        grid=(tiles,),
        in_specs=[
            whole(hidden_q.shape),
            pl.BlockSpec((1, hidden, tile), lambda j: (0, 0, c * tiles + j)),
            whole(factor.shape),
            whole(spread.shape),
        ],
        out_specs=[pl.BlockSpec((sources // 2, tokens, tile), lambda j: (0, 0, j))] * 2,
        out_shape=[jax.ShapeDtypeStruct((sources // 2, tokens, step), jnp.bfloat16)] * 2,
        compiler_params=pltpu.CompilerParams(vmem_limit_bytes=VMEM_LIMIT),
        cost_estimate=cost(
            2 * rows * step * (hidden + tokens), 2 * step * (hidden + sources * tokens)
        ),
        name="down",
    )(hidden_q, w_down, factor, spread)


def natural_kernel(columns, *refs):
    *parts, out_ref = refs
    for j in range(parts[0].shape[1] // columns):
        for c, part in enumerate(parts):
            place = (j * len(parts) + c) * columns
            out_ref[:, place : place + columns] = part[:, j * columns : (j + 1) * columns]


def natural(parts, columns):
    rows, step = parts[0].shape
    return pl.pallas_call(
        functools.partial(natural_kernel, columns),
        out_shape=jax.ShapeDtypeStruct((rows, step * len(parts)), parts[0].dtype),
        compiler_params=pltpu.CompilerParams(vmem_limit_bytes=VMEM_LIMIT),
        name="natural",
    )(*parts)


def add(*terms):
    return sum(t.astype(jnp.float32) for t in terms).astype(jnp.bfloat16)


def gather_plan(
    attn_out,
    out_weight,
    residual,
    norm_gain,
    expert_ids,
    route_weight,
    w_gate,
    w_up,
    w_down,
    top_x,
    top_h,
    capacity,
):
    owners, layers = lax.axis_size("dp"), lax.axis_size("tensor")
    experts = owners * layers
    local_rows, width = residual.shape
    half, step = layers // 2, width // CHUNKS
    columns = step // owners

    split = lambda value: value.reshape(-1, owners, CHUNKS, columns)
    parts = lambda value, c: split(value)[:, :, c].reshape(-1, step)
    place = lax.axis_index("dp")[None]

    weight_rows = list(out_weight.T.reshape(CHUNKS, columns, -1))
    table = chip_table(expert_ids, route_weight, experts)
    near = neighbours(weight_rows[0])
    stream, sent = [], []
    for c in range(CHUNKS):
        if c + 1 < CHUNKS:
            near, table, weight_rows[c + 1] = tie(near, table, weight_rows[c + 1])
        groups = [[weight_rows[c]], [near[0]], [near[1]], diagonal(*near)]
        if c + 1 < CHUNKS:
            near = neighbours(weight_rows[c + 1])
            groups[3], near = tie(groups[3], near)
        groups = [both_cores(group) for group in groups]
        if c > 0:
            groups, weight = tie(groups, weight)
        terms = project_part(place, attn_out, groups)
        if c == 0:
            terms, table = tie(terms, table)
            weight = expert_weights(table)
        else:
            terms, sent[-1] = tie(terms, sent[-1])
        total = lax.psum_scatter(terms, "tensor", scatter_dimension=0, tiled=True)
        stream.append(parts(residual, c).astype(jnp.float32) + total.astype(jnp.float32))
        sent.append(stream[c].astype(jnp.bfloat16))

    named = weight > 0.0
    earlier = jnp.triu(jnp.ones((local_rows, local_rows), jnp.bfloat16), 1)
    slot = lax.dot_general(
        named.astype(jnp.bfloat16),
        earlier,
        (((2,), (0,)), ((), ())),
        preferred_element_type=jnp.float32,
    ).astype(jnp.int32)
    chosen = (
        slot[:, :, None, :] == jnp.arange(capacity, dtype=jnp.int32)[:, None]
    ) & named[:, :, None, :]
    factor = jnp.sum(jnp.where(chosen, weight[:, :, None, :], 0.0), axis=3)
    factor = factor.reshape(4, 2 * layers * capacity, 1) * (top_h / FP8_LIMIT)
    choice = chosen.astype(jnp.bfloat16).reshape(4, 2 * layers, capacity, local_rows)
    spread = choice.transpose(0, 1, 3, 2)
    scales = jnp.stack([top_x / FP8_LIMIT, FP8_LIMIT / top_h])

    squares = sum(jnp.sum(part * part, axis=1) for part in stream)
    root = lax.rsqrt(squares / width + 1e-06)
    gains = [parts(norm_gain, c) for c in range(CHUNKS)]
    peak_x = jnp.max(
        jnp.stack([jnp.max(jnp.abs(s * root[:, None] * g)) for s, g in zip(stream, gains)])
    )
    gains = jnp.stack(gains) * (FP8_LIMIT / top_x)

    gate_rows = w_gate.reshape(1, owners, CHUNKS, columns, -1)
    up_rows = w_up.reshape(1, owners, CHUNKS, columns, -1)

    def hidden_of(r, tokens):
        pieces = [piece for part in tokens for piece in part]
        return gate_up(scales, gains, choice[r], pieces, gate_rows, up_rows)

    groups = [[] for _ in range(4)]
    own = along_tensor(sent[0])
    for c in range(CHUNKS):
        along_x, along_y = neighbours(own)
        groups[0].append(both_cores([own]))
        if c + 1 < CHUNKS:
            own = along_tensor(sent[c + 1])
            along_x, along_y, own = tie(along_x, along_y, own)
        else:
            hidden = [hidden_of(0, groups[0])]
            stream = natural(stream, columns)
            along_x, along_y, hidden[0], stream, groups[3] = tie(
                along_x, along_y, hidden[0], stream, groups[3]
            )
        groups[1].append(both_cores([along_x]))
        groups[2].append(both_cores([along_y]))
        across = diagonal(along_x, along_y)
        if c + 1 == CHUNKS:
            hidden += [hidden_of(1, groups[1]), hidden_of(2, groups[2])]
            across, hidden = tie(across, hidden)
        groups[3].append(both_cores(across))

    def outputs(r, c):
        return down(hidden[r][0], w_down, factor[r], spread[r], c, step)

    def halves(kept, given):
        taken = swap(given, 1)
        return [(kept[:half], taken[:half]), (kept[half:], taken[half:])]

    summed = lambda r, c: [add(*terms) for terms in halves(*outputs(r, c))]
    to_x, to_y = summed(1, 0), summed(2, 0)
    groups[3], to_x, to_y = tie(groups[3], to_x, to_y)
    hidden.append(hidden_of(3, groups[3]))
    peak_h = jnp.max(jnp.stack([peaks for _, peaks in hidden]))
    mixture = []
    for c in range(CHUNKS):
        early_x, early_y = swap(to_x[0], 2), swap(to_y[1], 4)
        kept, given = outputs(3, c)
        given, early_x, early_y = tie(given, early_x, early_y)
        beyond = [add(*terms) for terms in halves(kept, given)]
        if c > 0:
            beyond, mixed = tie(beyond, mixed)
            mixture.append(lax.psum_scatter(mixed, "tensor", scatter_dimension=0, tiled=True))
        over_x, over_y = swap(beyond[0], 2), swap(beyond[1], 4)
        late_x, late_y = to_x[1], to_y[0]
        if c + 1 < CHUNKS:
            to_x, to_y = summed(1, c + 1), summed(2, c + 1)
            over_x, over_y, to_x, to_y = tie(over_x, over_y, to_x, to_y)
        to_own = halves(*outputs(0, c))
        low = add(*to_own[0], early_x, swap(add(late_y, over_x), 4))
        high = add(*to_own[1], swap(add(late_x, over_y), 2), early_y)
        mixed = jnp.concatenate([low, high]).reshape(layers * local_rows, step)
    mixed, mixture = tie(mixed, mixture)
    mixture.append(lax.psum_scatter(mixed, "tensor", scatter_dimension=0, tiled=True))
    layer_out = stream + jnp.concatenate(mixture, axis=1).astype(jnp.float32)
    return layer_out.astype(jnp.bfloat16), peak_x, peak_h


def body(
    attn_out,
    out_weight,
    residual,
    norm_gain,
    expert_ids,
    route_weight,
    w_gate,
    w_up,
    w_down,
    history_x,
    history_h,
):
    experts = lax.axis_size("dp") * lax.axis_size("tensor")
    local_rows, top_count = expert_ids.shape
    capacity = max(2, 3 * local_rows * top_count // (2 * experts))
    top_x, top_h = jnp.max(history_x), jnp.max(history_h)
    gathers = lax.axis_size("dp") == 8 and local_rows < 4 * capacity
    plan = gather_plan if gathers else exchange_plan
    layer_out, peak_x, peak_h = plan(
        attn_out,
        out_weight,
        residual,
        norm_gain,
        expert_ids,
        route_weight,
        w_gate,
        w_up,
        w_down,
        top_x,
        top_h,
        capacity,
    )
    peaks = peaks_over_all(jnp.stack([peak_x, peak_h]))
    new_history_x = jnp.concatenate([peaks[:1], history_x[:-1]])
    new_history_h = jnp.concatenate([peaks[1:], history_h[:-1]])
    return (layer_out, new_history_x, new_history_h)


def solution(mesh):
    in_specs = (
        P("dp", "tensor"),
        P("tensor", "dp"),
        P(AXES, None),
        P(),
        P(AXES, None),
        P(AXES, None),
        P(AXES, None, None),
        P(AXES, None, None),
        P(AXES, None, None),
        P(),
        P(),
    )
    out_specs = (P(AXES, None), P(), P())
    return jax.shard_map(body, mesh=mesh, in_specs=in_specs, out_specs=out_specs, check_vma=False)
```

```python
import functools

import jax
import jax.numpy as jnp
from jax import lax
from jax.experimental import pallas as pl
from jax.experimental.pallas import tpu as pltpu
from jax.sharding import PartitionSpec as P

FP8_LIMIT = 448.0
AXES = ("dp", "tensor")
CHUNKS = 2
VMEM_LIMIT = 48 * 2**20
COST_SHARE = 16


def project(attn_out, out_weight):
    head_terms = jnp.dot(
        attn_out,
        lax.all_gather(out_weight, "dp", axis=1, tiled=True),
        preferred_element_type=jnp.float32,
    )
    return lax.psum_scatter(
        head_terms.astype(jnp.bfloat16), "tensor", scatter_dimension=0, tiled=True
    ).astype(jnp.float32)


def peaks_over_all(peaks):
    for axis in AXES:
        count = lax.axis_size(axis)
        shift = 1
        while shift < count:
            pairs = [(i, (i + shift) % count) for i in range(count)]
            peaks = jnp.maximum(peaks, lax.ppermute(peaks, axis, pairs))
            shift *= 2
    return peaks


def slots_of(ids, experts, capacity):
    flat_ids = ids.reshape(-1)
    onehot = (flat_ids[:, None] == jnp.arange(experts, dtype=jnp.int32)[None, :]).astype(jnp.int32)
    before = jnp.cumsum(onehot, axis=0) - onehot
    return flat_ids * capacity + jnp.sum(before * onehot, axis=-1)


def exchange_plan(
    attn_out,
    out_weight,
    residual,
    norm_gain,
    expert_ids,
    route_weight,
    w_gate,
    w_up,
    w_down,
    top_x,
    top_h,
    capacity,
):
    experts = lax.axis_size("dp") * lax.axis_size("tensor")
    inv_x, inv_h, scale_h = top_x / FP8_LIMIT, top_h / FP8_LIMIT, FP8_LIMIT / top_h
    local_rows, width = residual.shape
    top_count = expert_ids.shape[1]
    stream = residual.astype(jnp.float32) + project(attn_out, out_weight)
    normed = (
        stream * lax.rsqrt(jnp.mean(stream * stream, axis=-1, keepdims=True) + 1e-06) * norm_gain
    )
    quantized = jnp.clip(normed * (FP8_LIMIT / top_x), -FP8_LIMIT, FP8_LIMIT).astype(jnp.bfloat16)
    position = slots_of(expert_ids, experts, capacity)
    matches = (
        position.reshape(local_rows, top_count)[:, :, None]
        == jnp.arange(experts * capacity, dtype=jnp.int32)[None, None, :]
    )
    placing = jnp.sum(matches.astype(jnp.int32), axis=1).astype(jnp.bfloat16)
    outgoing = lax.dot_general(
        placing, quantized, (((0,), (0,)), ((), ())), preferred_element_type=jnp.float32
    )
    outgoing = outgoing.astype(jnp.bfloat16).reshape(experts, capacity, width)
    token_block = lax.all_to_all(outgoing, AXES, split_axis=0, concat_axis=0, tiled=True)
    flat_rows = token_block.reshape(-1, width)
    gate = jnp.dot(flat_rows, w_gate[0], preferred_element_type=jnp.float32) * inv_x
    upper = jnp.dot(flat_rows, w_up[0], preferred_element_type=jnp.float32) * inv_x
    hidden = jax.nn.silu(gate) * upper
    hidden_q = jnp.clip(hidden * scale_h, -FP8_LIMIT, FP8_LIMIT).astype(jnp.bfloat16)
    expert_out = (jnp.dot(hidden_q, w_down[0], preferred_element_type=jnp.float32) * inv_h).astype(
        jnp.bfloat16
    )
    returned = lax.all_to_all(
        expert_out.reshape(experts, capacity, width), AXES, split_axis=0, concat_axis=0, tiled=True
    )
    picked = returned.reshape(-1, width)[position].reshape(local_rows, top_count, width)
    mixture = jnp.sum(picked.astype(jnp.float32) * route_weight[:, :, None], axis=1)
    peaks = jnp.max(jnp.abs(normed)), jnp.max(jnp.abs(hidden))
    return (stream + mixture).astype(jnp.bfloat16), *peaks


def cost(flops, bytes_accessed):
    return pl.CostEstimate(
        flops=flops // COST_SHARE, bytes_accessed=bytes_accessed // COST_SHARE, transcendentals=0
    )


def swap(value, bits):
    count = lax.axis_size("dp")
    return lax.ppermute(value, "dp", [(i, i ^ bits) for i in range(count)])


def along_tensor(value, at_hop=None):
    count, here = lax.axis_size("tensor"), lax.axis_index("tensor")
    passed = [(value, value)]
    for hop in range(1, count):
        up = [(i, i + 1) for i in range(hop - 1, count - 1)]
        back = [(count - 1 - i, count - 1 - j) for i, j in up]
        below, above = passed[-1]
        arrived = lax.ppermute(below, "tensor", up), lax.ppermute(above, "tensor", back)
        passed.append(at_hop(hop, arrived) if at_hop else arrived)
    blocks = jnp.zeros((count,) + value.shape, value.dtype)
    blocks = lax.dynamic_update_index_in_dim(blocks, value, here, 0)
    for hop in range(1, count):
        block = jnp.where(here >= hop, passed[hop][0], passed[count - hop][1])
        blocks = lax.dynamic_update_index_in_dim(blocks, block, (here - hop) % count, 0)
    return blocks


def chip_table(expert_ids, route_weight, experts):
    names = jnp.arange(experts, dtype=jnp.int32)[:, None, None]
    table = jnp.sum(jnp.where(expert_ids[None] == names, route_weight[None], 0.0), axis=2)
    count = lax.axis_size("tensor")
    parts = [table]
    for shift in range(1, count):
        pairs = [(i, (i + shift) % count) for i in range(count)]
        parts.append(lax.ppermute(table, "tensor", pairs))
    order = (lax.axis_index("tensor") - jnp.arange(count)) % count
    table = jnp.stack(parts)[order][None]
    return jnp.concatenate([table, swap(table, 1)])


def expert_weights(table):
    for bit in (2, 4):
        table = jnp.concatenate([table, swap(table, bit)])
    mine = lax.axis_index("dp") * lax.axis_size("tensor") + lax.axis_index("tensor")
    return lax.dynamic_index_in_dim(table, mine, axis=2, keepdims=False)


def neighbours(value):
    return swap(value, 2), swap(value, 4)


def diagonal(along_x, along_y):
    half = along_x.shape[0] // 2
    return [swap(along_x[:half], 4), swap(along_y[half:], 2)]


def both_cores(group):
    return group + [swap(piece, 1) for piece in group]


def tie(*values):
    return lax.optimization_barrier(values)


def project_kernel(place_ref, attn_ref, *refs):
    out_ref, joined, stage = refs[-3:]
    pieces = refs[:-3]
    columns = pieces[0].shape[0]
    attn = attn_ref[...]
    blocks = [pieces[0], pieces[1], pieces[2], pieces[3], pieces[4], pieces[5], None, None]
    for k, block in enumerate(blocks):
        if block is None:
            low, high = pieces[2 * k - 6], pieces[2 * k - 5]
            joined[: low.shape[0]] = low[...]
            joined[low.shape[0] :] = high[...]
            block = joined
        terms = lax.dot_general(
            attn, block[...], (((1,), (1,)), ((), ())), preferred_element_type=jnp.float32
        )
        stage[place_ref[0] ^ k, :, :columns] = terms
    for j in range(stage.shape[0]):
        out_ref[:, j * columns : (j + 1) * columns] = stage[j, :, :columns].astype(out_ref.dtype)


def project_part(place, attn_out, groups):
    rows, depth = attn_out.shape
    pieces = [piece for group in groups for piece in group]
    columns = pieces[0].shape[0]
    return pl.pallas_call(
        project_kernel,
        in_specs=[pl.BlockSpec(memory_space=pltpu.SMEM)]
        + [pl.BlockSpec(memory_space=pltpu.VMEM)] * (1 + len(pieces)),
        out_specs=pl.BlockSpec(memory_space=pltpu.VMEM),
        out_shape=jax.ShapeDtypeStruct((rows, 8 * columns), jnp.bfloat16),
        scratch_shapes=[
            pltpu.VMEM((columns, depth), jnp.bfloat16),
            pltpu.VMEM((8, rows, -(-columns // 128) * 128), jnp.float32),
        ],
        compiler_params=pltpu.CompilerParams(vmem_limit_bytes=VMEM_LIMIT),
        cost_estimate=cost(16 * rows * depth * columns, 2 * depth * (rows + 8 * columns)),
        name="project",
    )(place, attn_out, *pieces)


def gate_up_kernel(parts, scale_ref, gain_ref, chosen_ref, *refs):
    hidden_ref, peak_ref, rows = refs[-3:]
    weights, pieces = refs[-3 - 2 * parts : -3], refs[: -3 - 2 * parts]
    per_part = len(pieces) // parts
    capacity = chosen_ref.shape[1]
    step = rows.shape[2]

    @pl.when(pl.program_id(0) == 0)
    def _():
        source = 0
        for p in range(per_part):
            for i in range(pieces[p].shape[0]):
                span = slice(source * capacity, (source + 1) * capacity)
                picked = [
                    jnp.dot(
                        chosen_ref[source],
                        pieces[c * per_part + p][i],
                        preferred_element_type=jnp.float32,
                    )
                    for c in range(parts)
                ]
                squares = sum(jnp.sum(x * x, axis=1, keepdims=True) for x in picked)
                root = lax.rsqrt(squares / (parts * step) + 1e-06)
                for c, x in enumerate(picked):
                    x = jnp.clip(x * root * gain_ref[c], -FP8_LIMIT, FP8_LIMIT)
                    rows[c, span] = x.astype(rows.dtype)
                source += 1

    def product(side):
        return sum(
            jnp.dot(
                rows[c],
                weights[2 * c + side][0].reshape(step, -1),
                preferred_element_type=jnp.float32,
            )
            for c in range(parts)
        )

    gate, up = product(0) * scale_ref[0], product(1) * scale_ref[0]
    hidden = gate / (1.0 + jnp.exp(-gate)) * up
    scaled = jnp.clip(hidden * scale_ref[1], -FP8_LIMIT, FP8_LIMIT)
    hidden_ref[...] = scaled.astype(hidden_ref.dtype)
    peak = jnp.broadcast_to(jnp.max(jnp.abs(hidden)), peak_ref.shape)
    first = pl.program_id(0) == 0
    peak_ref[...] = jnp.where(first, peak, jnp.maximum(peak_ref[...], peak))


def gate_up(scales, gains, chosen, pieces, w_gate, w_up):
    sources, capacity, tokens = chosen.shape
    parts, _, step = gains.shape
    owners, columns, hidden = w_gate.shape[1], w_gate.shape[3], w_gate.shape[-1]
    tile = min(256, hidden)
    rows = sources * capacity
    once = pl.Buffered(buffer_count=1)
    whole = lambda a: pl.BlockSpec(a.shape, lambda n: (0,) * a.ndim, pipeline_mode=once)
    column = lambda height: pl.BlockSpec((height, tile), lambda n: (0, n))
    weight = lambda c: pl.BlockSpec((1, owners, None, columns, tile), lambda n: (0, 0, c, 0, n))
    return pl.pallas_call(
        functools.partial(gate_up_kernel, parts),
        grid=(hidden // tile,),
        in_specs=[pl.BlockSpec(memory_space=pltpu.SMEM), whole(gains), whole(chosen)]
        + [whole(p) for p in pieces]
        + [weight(c) for c in range(parts) for _ in range(2)],
        out_specs=[column(rows), pl.BlockSpec((8, 128), lambda n: (0, 0))],
        out_shape=[
            jax.ShapeDtypeStruct((rows, hidden), jnp.bfloat16),
            jax.ShapeDtypeStruct((8, 128), jnp.float32),
        ],
        scratch_shapes=[pltpu.VMEM((parts, rows, step), jnp.bfloat16)],
        compiler_params=pltpu.CompilerParams(vmem_limit_bytes=VMEM_LIMIT),
        cost_estimate=cost(
            2 * rows * parts * step * (2 * hidden + tokens),
            2 * parts * step * (2 * hidden + sources * tokens),
        ),
        name="gate_up",
    )(scales, gains, chosen, *pieces, *([w_gate, w_up] * parts))


def down_kernel(hidden_ref, down_w, factor_ref, spread_ref, own_ref, other_ref):
    sources, tokens, capacity = spread_ref.shape
    terms = jnp.dot(hidden_ref[...], down_w[0], preferred_element_type=jnp.float32)
    terms = (terms * factor_ref[...]).astype(jnp.bfloat16)
    half = sources // 2
    for source in range(sources):
        spread = jnp.dot(
            spread_ref[source],
            terms[source * capacity : (source + 1) * capacity],
            preferred_element_type=jnp.float32,
        ).astype(jnp.bfloat16)
        if source < half:
            own_ref[source] = spread
        else:
            other_ref[source - half] = spread


def down(hidden_q, w_down, factor, spread, c, step):
    rows, hidden = hidden_q.shape
    sources, tokens, capacity = spread.shape
    tile = step // 2 if step % 256 == 0 else step
    tiles = step // tile
    whole = lambda shape: pl.BlockSpec(shape, lambda j: (0,) * len(shape))
    return pl.pallas_call(
        down_kernel,
        grid=(tiles,),
        in_specs=[
            whole(hidden_q.shape),
            pl.BlockSpec((1, hidden, tile), lambda j: (0, 0, c * tiles + j)),
            whole(factor.shape),
            whole(spread.shape),
        ],
        out_specs=[pl.BlockSpec((sources // 2, tokens, tile), lambda j: (0, 0, j))] * 2,
        out_shape=[jax.ShapeDtypeStruct((sources // 2, tokens, step), jnp.bfloat16)] * 2,
        compiler_params=pltpu.CompilerParams(vmem_limit_bytes=VMEM_LIMIT),
        cost_estimate=cost(
            2 * rows * step * (hidden + tokens), 2 * step * (hidden + sources * tokens)
        ),
        name="down",
    )(hidden_q, w_down, factor, spread)


def natural_kernel(columns, *refs):
    *parts, out_ref = refs
    for j in range(parts[0].shape[1] // columns):
        for c, part in enumerate(parts):
            place = (j * len(parts) + c) * columns
            out_ref[:, place : place + columns] = part[:, j * columns : (j + 1) * columns]


def natural(parts, columns):
    rows, step = parts[0].shape
    return pl.pallas_call(
        functools.partial(natural_kernel, columns),
        out_shape=jax.ShapeDtypeStruct((rows, step * len(parts)), parts[0].dtype),
        compiler_params=pltpu.CompilerParams(vmem_limit_bytes=VMEM_LIMIT),
        name="natural",
    )(*parts)


def add(*terms):
    return sum(t.astype(jnp.float32) for t in terms).astype(jnp.bfloat16)


def gather_plan(
    attn_out,
    out_weight,
    residual,
    norm_gain,
    expert_ids,
    route_weight,
    w_gate,
    w_up,
    w_down,
    top_x,
    top_h,
    capacity,
):
    owners, layers = lax.axis_size("dp"), lax.axis_size("tensor")
    experts = owners * layers
    local_rows, width = residual.shape
    half, step = layers // 2, width // CHUNKS
    columns = step // owners

    split = lambda value: value.reshape(-1, owners, CHUNKS, columns)
    parts = lambda value, c: split(value)[:, :, c].reshape(-1, step)
    place = lax.axis_index("dp")[None]

    def summed_over_tensor(terms, c):
        total = lax.psum_scatter(terms, "tensor", scatter_dimension=0, tiled=True)
        part = parts(residual, c).astype(jnp.float32) + total.astype(jnp.float32)
        return part, part.astype(jnp.bfloat16)

    weight_rows = list(out_weight.T.reshape(CHUNKS, columns, -1))
    near = neighbours(weight_rows[0])
    table = chip_table(expert_ids, route_weight, experts)
    near, table = tie(near, table)
    groups = [[weight_rows[0]], [near[0]], [near[1]], diagonal(*near)]
    terms = project_part(place, attn_out, [both_cores(group) for group in groups])
    terms, table, weight_rows[1] = tie(terms, table, weight_rows[1])
    weight = expert_weights(table)
    near = neighbours(weight_rows[1])
    groups = [[weight_rows[1]], [near[0]], [near[1]], diagonal(*near)]
    groups = [both_cores(group) for group in groups]
    first, sent = summed_over_tensor(terms, 0)
    sent, weight = tie(sent, weight)

    second = []

    def at_hop(hop, arrived):
        if hop == 1:
            arrived, tied = tie(arrived, groups)
            second.append(project_part(place, attn_out, tied))
        if hop == 2:
            arrived, terms = tie(arrived, second.pop())
            second.append(summed_over_tensor(terms, 1))
        return arrived

    own = along_tensor(sent, at_hop)
    stream = [first, second[0][0]]
    sent = second[0][1]

    named = weight > 0.0
    earlier = jnp.triu(jnp.ones((local_rows, local_rows), jnp.bfloat16), 1)
    slot = lax.dot_general(
        named.astype(jnp.bfloat16),
        earlier,
        (((2,), (0,)), ((), ())),
        preferred_element_type=jnp.float32,
    ).astype(jnp.int32)
    chosen = (
        slot[:, :, None, :] == jnp.arange(capacity, dtype=jnp.int32)[:, None]
    ) & named[:, :, None, :]
    factor = jnp.sum(jnp.where(chosen, weight[:, :, None, :], 0.0), axis=3)
    factor = factor.reshape(4, 2 * layers * capacity, 1) * (top_h / FP8_LIMIT)
    choice = chosen.astype(jnp.bfloat16).reshape(4, 2 * layers, capacity, local_rows)
    spread = choice.transpose(0, 1, 3, 2)
    scales = jnp.stack([top_x / FP8_LIMIT, FP8_LIMIT / top_h])

    squares = sum(jnp.sum(part * part, axis=1) for part in stream)
    root = lax.rsqrt(squares / width + 1e-06)
    gains = [parts(norm_gain, c) for c in range(CHUNKS)]
    peak_x = jnp.max(
        jnp.stack([jnp.max(jnp.abs(s * root[:, None] * g)) for s, g in zip(stream, gains)])
    )
    gains = jnp.stack(gains) * (FP8_LIMIT / top_x)

    gate_rows = w_gate.reshape(1, owners, CHUNKS, columns, -1)
    up_rows = w_up.reshape(1, owners, CHUNKS, columns, -1)

    def hidden_of(r, tokens, choice):
        pieces = [piece for part in tokens for piece in part]
        return gate_up(scales, gains, choice[r], pieces, gate_rows, up_rows)

    groups = [[] for _ in range(4)]
    for c in range(CHUNKS):
        along_x, along_y = neighbours(own)
        groups[0].append(both_cores([own]))
        if c + 1 < CHUNKS:
            along_x, along_y, sent = tie(along_x, along_y, sent)
            across = diagonal(along_x, along_y)

            def at_hop(hop, arrived):
                nonlocal across
                if hop == 2:
                    arrived, across = tie(arrived, across)
                return arrived

            own = along_tensor(sent, at_hop)
        else:
            hidden = [hidden_of(0, groups[0], choice)]
            stream = natural(stream, columns)
            along_x, along_y, hidden[0], stream, groups[3], choice, spread, factor = tie(
                along_x, along_y, hidden[0], stream, groups[3], choice, spread, factor
            )
        groups[1].append(both_cores([along_x]))
        groups[2].append(both_cores([along_y]))
        if c + 1 == CHUNKS:
            across = diagonal(along_x, along_y)
            hidden += [hidden_of(1, groups[1], choice), hidden_of(2, groups[2], choice)]
            across, hidden = tie(across, hidden)
        groups[3].append(both_cores(across))

    def outputs(r, c):
        return down(hidden[r][0], w_down, factor[r], spread[r], c, step)

    def halves(kept, given):
        taken = swap(given, 1)
        return [(kept[:half], taken[:half]), (kept[half:], taken[half:])]

    summed = lambda r, c: [add(*terms) for terms in halves(*outputs(r, c))]
    to_x, to_y = summed(1, 0), summed(2, 0)
    groups[3], to_x, to_y = tie(groups[3], to_x, to_y)
    hidden.append(hidden_of(3, groups[3], choice))
    peak_h = jnp.max(jnp.stack([peaks for _, peaks in hidden]))
    mixture = []
    for c in range(CHUNKS):
        early_x, early_y = swap(to_x[0], 2), swap(to_y[1], 4)
        kept, given = outputs(3, c)
        if c == 0:
            given, early_x, early_y = tie(given, early_x, early_y)
        beyond = [add(*terms) for terms in halves(kept, given)]
        if c > 0:
            beyond, mixed = tie(beyond, mixed)
            mixture.append(lax.psum_scatter(mixed, "tensor", scatter_dimension=0, tiled=True))
        over_x, over_y = swap(beyond[0], 2), swap(beyond[1], 4)
        late_x, late_y = to_x[1], to_y[0]
        if c + 1 < CHUNKS:
            over_x, over_y, hidden = tie(over_x, over_y, hidden)
            to_x, to_y = summed(1, c + 1), summed(2, c + 1)
        to_own = halves(*outputs(0, c))
        low = add(*to_own[0], early_x, swap(add(late_y, over_x), 4))
        high = add(*to_own[1], swap(add(late_x, over_y), 2), early_y)
        mixed = jnp.concatenate([low, high]).reshape(layers * local_rows, step)
    mixed, mixture = tie(mixed, mixture)
    mixture.append(lax.psum_scatter(mixed, "tensor", scatter_dimension=0, tiled=True))
    layer_out = stream + jnp.concatenate(mixture, axis=1).astype(jnp.float32)
    return layer_out.astype(jnp.bfloat16), peak_x, peak_h


def body(
    attn_out,
    out_weight,
    residual,
    norm_gain,
    expert_ids,
    route_weight,
    w_gate,
    w_up,
    w_down,
    history_x,
    history_h,
):
    experts = lax.axis_size("dp") * lax.axis_size("tensor")
    local_rows, top_count = expert_ids.shape
    capacity = max(2, 3 * local_rows * top_count // (2 * experts))
    top_x, top_h = jnp.max(history_x), jnp.max(history_h)
    gathers = lax.axis_size("dp") == 8 and local_rows < 4 * capacity
    plan = gather_plan if gathers else exchange_plan
    layer_out, peak_x, peak_h = plan(
        attn_out,
        out_weight,
        residual,
        norm_gain,
        expert_ids,
        route_weight,
        w_gate,
        w_up,
        w_down,
        top_x,
        top_h,
        capacity,
    )
    peaks = peaks_over_all(jnp.stack([peak_x, peak_h]))
    new_history_x = jnp.concatenate([peaks[:1], history_x[:-1]])
    new_history_h = jnp.concatenate([peaks[1:], history_h[:-1]])
    return (layer_out, new_history_x, new_history_h)


def solution(mesh):
    in_specs = (
        P("dp", "tensor"),
        P("tensor", "dp"),
        P(AXES, None),
        P(),
        P(AXES, None),
        P(AXES, None),
        P(AXES, None, None),
        P(AXES, None, None),
        P(AXES, None, None),
        P(),
        P(),
    )
    out_specs = (P(AXES, None), P(), P())
    return jax.shard_map(body, mesh=mesh, in_specs=in_specs, out_specs=out_specs, check_vma=False)
```

```python
import functools

import jax
import jax.numpy as jnp
from jax import lax
from jax.experimental import pallas as pl
from jax.experimental.pallas import tpu as pltpu
from jax.sharding import PartitionSpec as P

FP8_LIMIT = 448.0
AXES = ("dp", "tensor")
CHUNKS = 2
VMEM_LIMIT = 48 * 2**20
COST_SHARE = 16


def project(attn_out, out_weight):
    head_terms = jnp.dot(
        attn_out,
        lax.all_gather(out_weight, "dp", axis=1, tiled=True),
        preferred_element_type=jnp.float32,
    )
    return lax.psum_scatter(
        head_terms.astype(jnp.bfloat16), "tensor", scatter_dimension=0, tiled=True
    ).astype(jnp.float32)


def peaks_over_all(peaks):
    for axis in AXES:
        count = lax.axis_size(axis)
        shift = 1
        while shift < count:
            pairs = [(i, (i + shift) % count) for i in range(count)]
            peaks = jnp.maximum(peaks, lax.ppermute(peaks, axis, pairs))
            shift *= 2
    return peaks


def slots_of(ids, experts, capacity):
    flat_ids = ids.reshape(-1)
    onehot = (flat_ids[:, None] == jnp.arange(experts, dtype=jnp.int32)[None, :]).astype(jnp.int32)
    before = jnp.cumsum(onehot, axis=0) - onehot
    return flat_ids * capacity + jnp.sum(before * onehot, axis=-1)


def exchange_plan(
    attn_out,
    out_weight,
    residual,
    norm_gain,
    expert_ids,
    route_weight,
    w_gate,
    w_up,
    w_down,
    top_x,
    top_h,
    capacity,
):
    experts = lax.axis_size("dp") * lax.axis_size("tensor")
    inv_x, inv_h, scale_h = top_x / FP8_LIMIT, top_h / FP8_LIMIT, FP8_LIMIT / top_h
    local_rows, width = residual.shape
    top_count = expert_ids.shape[1]
    stream = residual.astype(jnp.float32) + project(attn_out, out_weight)
    normed = (
        stream * lax.rsqrt(jnp.mean(stream * stream, axis=-1, keepdims=True) + 1e-06) * norm_gain
    )
    quantized = jnp.clip(normed * (FP8_LIMIT / top_x), -FP8_LIMIT, FP8_LIMIT).astype(jnp.bfloat16)
    position = slots_of(expert_ids, experts, capacity)
    matches = (
        position.reshape(local_rows, top_count)[:, :, None]
        == jnp.arange(experts * capacity, dtype=jnp.int32)[None, None, :]
    )
    placing = jnp.sum(matches.astype(jnp.int32), axis=1).astype(jnp.bfloat16)
    outgoing = lax.dot_general(
        placing, quantized, (((0,), (0,)), ((), ())), preferred_element_type=jnp.float32
    )
    outgoing = outgoing.astype(jnp.bfloat16).reshape(experts, capacity, width)
    token_block = lax.all_to_all(outgoing, AXES, split_axis=0, concat_axis=0, tiled=True)
    flat_rows = token_block.reshape(-1, width)
    gate = jnp.dot(flat_rows, w_gate[0], preferred_element_type=jnp.float32) * inv_x
    upper = jnp.dot(flat_rows, w_up[0], preferred_element_type=jnp.float32) * inv_x
    hidden = jax.nn.silu(gate) * upper
    hidden_q = jnp.clip(hidden * scale_h, -FP8_LIMIT, FP8_LIMIT).astype(jnp.bfloat16)
    expert_out = (jnp.dot(hidden_q, w_down[0], preferred_element_type=jnp.float32) * inv_h).astype(
        jnp.bfloat16
    )
    returned = lax.all_to_all(
        expert_out.reshape(experts, capacity, width), AXES, split_axis=0, concat_axis=0, tiled=True
    )
    picked = returned.reshape(-1, width)[position].reshape(local_rows, top_count, width)
    mixture = jnp.sum(picked.astype(jnp.float32) * route_weight[:, :, None], axis=1)
    peaks = jnp.max(jnp.abs(normed)), jnp.max(jnp.abs(hidden))
    return (stream + mixture).astype(jnp.bfloat16), *peaks


def cost(flops, bytes_accessed):
    return pl.CostEstimate(
        flops=flops // COST_SHARE, bytes_accessed=bytes_accessed // COST_SHARE, transcendentals=0
    )


def swap(value, bits):
    count = lax.axis_size("dp")
    return lax.ppermute(value, "dp", [(i, i ^ bits) for i in range(count)])


def along_tensor(value, at_hop=None):
    count, here = lax.axis_size("tensor"), lax.axis_index("tensor")
    passed = [(value, value)]
    for hop in range(1, count):
        up = [(i, i + 1) for i in range(hop - 1, count - 1)]
        back = [(count - 1 - i, count - 1 - j) for i, j in up]
        below, above = passed[-1]
        arrived = lax.ppermute(below, "tensor", up), lax.ppermute(above, "tensor", back)
        passed.append(at_hop(hop, arrived) if at_hop else arrived)
    blocks = jnp.zeros((count,) + value.shape, value.dtype)
    blocks = lax.dynamic_update_index_in_dim(blocks, value, here, 0)
    for hop in range(1, count):
        block = jnp.where(here >= hop, passed[hop][0], passed[count - hop][1])
        blocks = lax.dynamic_update_index_in_dim(blocks, block, (here - hop) % count, 0)
    return blocks


def chip_table(expert_ids, route_weight, experts):
    names = jnp.arange(experts, dtype=jnp.int32)[:, None, None]
    table = jnp.sum(jnp.where(expert_ids[None] == names, route_weight[None], 0.0), axis=2)
    count = lax.axis_size("tensor")
    parts = [table]
    for shift in range(1, count):
        pairs = [(i, (i + shift) % count) for i in range(count)]
        parts.append(lax.ppermute(table, "tensor", pairs))
    order = (lax.axis_index("tensor") - jnp.arange(count)) % count
    table = jnp.stack(parts)[order][None]
    return jnp.concatenate([table, swap(table, 1)])


def expert_weights(table):
    for bit in (2, 4):
        table = jnp.concatenate([table, swap(table, bit)])
    mine = lax.axis_index("dp") * lax.axis_size("tensor") + lax.axis_index("tensor")
    return lax.dynamic_index_in_dim(table, mine, axis=2, keepdims=False)


def neighbours(value):
    return swap(value, 2), swap(value, 4)


def diagonal(along_x, along_y):
    half = along_x.shape[0] // 2
    return [swap(along_x[:half], 4), swap(along_y[half:], 2)]


def both_cores(group):
    return group + [swap(piece, 1) for piece in group]


def tie(*values):
    return lax.optimization_barrier(values)


def project_kernel(place_ref, attn_ref, *refs):
    out_ref, joined, stage = refs[-3:]
    pieces = refs[:-3]
    columns = pieces[0].shape[0]
    attn = attn_ref[...]
    blocks = [pieces[0], pieces[1], pieces[2], pieces[3], pieces[4], pieces[5], None, None]
    for k, block in enumerate(blocks):
        if block is None:
            low, high = pieces[2 * k - 6], pieces[2 * k - 5]
            joined[: low.shape[0]] = low[...]
            joined[low.shape[0] :] = high[...]
            block = joined
        terms = lax.dot_general(
            attn, block[...], (((1,), (1,)), ((), ())), preferred_element_type=jnp.float32
        )
        stage[place_ref[0] ^ k, :, :columns] = terms
    for j in range(stage.shape[0]):
        out_ref[:, j * columns : (j + 1) * columns] = stage[j, :, :columns].astype(out_ref.dtype)


def project_part(place, attn_out, groups):
    rows, depth = attn_out.shape
    pieces = [piece for group in groups for piece in group]
    columns = pieces[0].shape[0]
    return pl.pallas_call(
        project_kernel,
        in_specs=[pl.BlockSpec(memory_space=pltpu.SMEM)]
        + [pl.BlockSpec(memory_space=pltpu.VMEM)] * (1 + len(pieces)),
        out_specs=pl.BlockSpec(memory_space=pltpu.VMEM),
        out_shape=jax.ShapeDtypeStruct((rows, 8 * columns), jnp.bfloat16),
        scratch_shapes=[
            pltpu.VMEM((columns, depth), jnp.bfloat16),
            pltpu.VMEM((8, rows, -(-columns // 128) * 128), jnp.float32),
        ],
        compiler_params=pltpu.CompilerParams(vmem_limit_bytes=VMEM_LIMIT),
        cost_estimate=cost(16 * rows * depth * columns, 2 * depth * (rows + 8 * columns)),
        name="project",
    )(place, attn_out, *pieces)


def pick(chosen_ref, pieces):
    source = 0
    for piece in pieces:
        for i in range(piece.shape[0]):
            yield jnp.dot(chosen_ref[source], piece[i], preferred_element_type=jnp.float32)
            source += 1


def rows_kernel(chosen_ref, *refs):
    *pieces, rows_ref, squares_ref = refs
    capacity = chosen_ref.shape[1]
    for source, picked in enumerate(pick(chosen_ref, pieces)):
        span = slice(source * capacity, (source + 1) * capacity)
        rows_ref[span] = picked.astype(rows_ref.dtype)
        squares_ref[span] = jnp.sum(picked * picked, axis=1, keepdims=True)


def rows_of(chosen, pieces):
    sources, capacity, tokens = chosen.shape
    rows, step = sources * capacity, pieces[0].shape[-1]
    return pl.pallas_call(
        rows_kernel,
        out_shape=[
            jax.ShapeDtypeStruct((rows, step), jnp.bfloat16),
            jax.ShapeDtypeStruct((rows, 1), jnp.float32),
        ],
        compiler_params=pltpu.CompilerParams(vmem_limit_bytes=VMEM_LIMIT),
        cost_estimate=cost(2 * rows * step * tokens, 2 * step * sources * tokens),
        name="rows",
    )(chosen, *pieces)


def gate_up_kernel(scale_ref, gain_ref, chosen_ref, first_ref, squares_ref, *refs):
    hidden_ref, peak_ref, rows = refs[-3:]
    weights, pieces = refs[-7:-3], refs[:-7]
    capacity = chosen_ref.shape[1]
    step = rows.shape[2]

    @pl.when(pl.program_id(0) == 0)
    def _():
        for source, picked in enumerate(pick(chosen_ref, pieces)):
            span = slice(source * capacity, (source + 1) * capacity)
            squares = squares_ref[span] + jnp.sum(picked * picked, axis=1, keepdims=True)
            root = lax.rsqrt(squares / (2 * step) + 1e-06)
            for c, x in enumerate((first_ref[span].astype(jnp.float32), picked)):
                x = jnp.clip(x * root * gain_ref[c], -FP8_LIMIT, FP8_LIMIT)
                rows[c, span] = x.astype(rows.dtype)

    def product(side):
        return sum(
            jnp.dot(
                rows[c],
                weights[2 * c + side][0].reshape(step, -1),
                preferred_element_type=jnp.float32,
            )
            for c in range(2)
        )

    gate, up = product(0) * scale_ref[0], product(1) * scale_ref[0]
    hidden = gate / (1.0 + jnp.exp(-gate)) * up
    scaled = jnp.clip(hidden * scale_ref[1], -FP8_LIMIT, FP8_LIMIT)
    hidden_ref[...] = scaled.astype(hidden_ref.dtype)
    peak = jnp.broadcast_to(jnp.max(jnp.abs(hidden)), peak_ref.shape)
    first = pl.program_id(0) == 0
    peak_ref[...] = jnp.where(first, peak, jnp.maximum(peak_ref[...], peak))


def gate_up(scales, gains, chosen, first, pieces, w_gate, w_up):
    sources, capacity, tokens = chosen.shape
    parts, _, step = gains.shape
    owners, columns, hidden = w_gate.shape[1], w_gate.shape[3], w_gate.shape[-1]
    tile = min(256, hidden)
    rows = sources * capacity
    once = pl.Buffered(buffer_count=1)
    whole = lambda a: pl.BlockSpec(a.shape, lambda n: (0,) * a.ndim, pipeline_mode=once)
    weight = lambda c: pl.BlockSpec((1, owners, None, columns, tile), lambda n: (0, 0, c, 0, n))
    return pl.pallas_call(
        gate_up_kernel,
        grid=(hidden // tile,),
        in_specs=[pl.BlockSpec(memory_space=pltpu.SMEM), whole(gains), whole(chosen)]
        + [whole(a) for a in first]
        + [whole(p) for p in pieces]
        + [weight(c) for c in range(parts) for _ in range(2)],
        out_specs=[
            pl.BlockSpec((rows, tile), lambda n: (0, n)),
            pl.BlockSpec((8, 128), lambda n: (0, 0)),
        ],
        out_shape=[
            jax.ShapeDtypeStruct((rows, hidden), jnp.bfloat16),
            jax.ShapeDtypeStruct((8, 128), jnp.float32),
        ],
        scratch_shapes=[pltpu.VMEM((parts, rows, step), jnp.bfloat16)],
        compiler_params=pltpu.CompilerParams(vmem_limit_bytes=VMEM_LIMIT),
        cost_estimate=cost(
            2 * rows * parts * step * (2 * hidden + tokens),
            2 * parts * step * (2 * hidden + sources * tokens),
        ),
        name="gate_up",
    )(scales, gains, chosen, *first, *pieces, *([w_gate, w_up] * parts))


def down_kernel(hidden_ref, down_w, factor_ref, spread_ref, own_ref, other_ref):
    sources, tokens, capacity = spread_ref.shape
    terms = jnp.dot(hidden_ref[...], down_w[0], preferred_element_type=jnp.float32)
    terms = (terms * factor_ref[...]).astype(jnp.bfloat16)
    half = sources // 2
    for source in range(sources):
        spread = jnp.dot(
            spread_ref[source],
            terms[source * capacity : (source + 1) * capacity],
            preferred_element_type=jnp.float32,
        ).astype(jnp.bfloat16)
        if source < half:
            own_ref[source] = spread
        else:
            other_ref[source - half] = spread


def down(hidden_q, w_down, factor, spread, c, step):
    rows, hidden = hidden_q.shape
    sources, tokens, capacity = spread.shape
    tile = step // 2 if step % 256 == 0 else step
    tiles = step // tile
    whole = lambda shape: pl.BlockSpec(shape, lambda j: (0,) * len(shape))
    return pl.pallas_call(
        down_kernel,
        grid=(tiles,),
        in_specs=[
            whole(hidden_q.shape),
            pl.BlockSpec((1, hidden, tile), lambda j: (0, 0, c * tiles + j)),
            whole(factor.shape),
            whole(spread.shape),
        ],
        out_specs=[pl.BlockSpec((sources // 2, tokens, tile), lambda j: (0, 0, j))] * 2,
        out_shape=[jax.ShapeDtypeStruct((sources // 2, tokens, step), jnp.bfloat16)] * 2,
        compiler_params=pltpu.CompilerParams(vmem_limit_bytes=VMEM_LIMIT),
        cost_estimate=cost(
            2 * rows * step * (hidden + tokens), 2 * step * (hidden + sources * tokens)
        ),
        name="down",
    )(hidden_q, w_down, factor, spread)


def natural_kernel(columns, *refs):
    *parts, out_ref = refs
    for j in range(parts[0].shape[1] // columns):
        for c, part in enumerate(parts):
            place = (j * len(parts) + c) * columns
            out_ref[:, place : place + columns] = part[:, j * columns : (j + 1) * columns]


def natural(parts, columns):
    rows, step = parts[0].shape
    return pl.pallas_call(
        functools.partial(natural_kernel, columns),
        out_shape=jax.ShapeDtypeStruct((rows, step * len(parts)), parts[0].dtype),
        compiler_params=pltpu.CompilerParams(vmem_limit_bytes=VMEM_LIMIT),
        name="natural",
    )(*parts)


def add(*terms):
    return sum(t.astype(jnp.float32) for t in terms).astype(jnp.bfloat16)


def gather_plan(
    attn_out,
    out_weight,
    residual,
    norm_gain,
    expert_ids,
    route_weight,
    w_gate,
    w_up,
    w_down,
    top_x,
    top_h,
    capacity,
):
    owners, layers = lax.axis_size("dp"), lax.axis_size("tensor")
    experts = owners * layers
    local_rows, width = residual.shape
    half, step = layers // 2, width // CHUNKS
    columns = step // owners

    split = lambda value: value.reshape(-1, owners, CHUNKS, columns)
    parts = lambda value, c: split(value)[:, :, c].reshape(-1, step)
    place = lax.axis_index("dp")[None]

    def summed_over_tensor(terms, c):
        total = lax.psum_scatter(terms, "tensor", scatter_dimension=0, tiled=True)
        part = parts(residual, c).astype(jnp.float32) + total.astype(jnp.float32)
        return part, part.astype(jnp.bfloat16)

    weight_rows = list(out_weight.T.reshape(CHUNKS, columns, -1))
    near = neighbours(weight_rows[0])
    table = chip_table(expert_ids, route_weight, experts)
    near, table = tie(near, table)
    groups = [[weight_rows[0]], [near[0]], [near[1]], diagonal(*near)]
    terms = project_part(place, attn_out, [both_cores(group) for group in groups])
    terms, weight_rows[1] = tie(terms, weight_rows[1])
    near = neighbours(weight_rows[1])
    groups = [[weight_rows[1]], [near[0]], [near[1]], diagonal(*near)]
    groups = [both_cores(group) for group in groups]
    first, sent = summed_over_tensor(terms, 0)

    beside = {}

    def at_hop(hop, arrived):
        if hop == 1:
            arrived, tied, routes = tie(arrived, groups, table)
            beside["terms"] = project_part(place, attn_out, tied)
            beside["weight"] = expert_weights(routes)
        if hop == layers - 1:
            arrived, terms, weight = tie(arrived, beside["terms"], beside["weight"])
            beside["sum"], beside["weight"] = summed_over_tensor(terms, 1), weight
        return arrived

    own = along_tensor(sent, at_hop)
    weight = beside["weight"]
    stream = [first, beside["sum"][0]]
    sent = beside["sum"][1]

    named = weight > 0.0
    earlier = jnp.triu(jnp.ones((local_rows, local_rows), jnp.bfloat16), 1)
    slot = lax.dot_general(
        named.astype(jnp.bfloat16),
        earlier,
        (((2,), (0,)), ((), ())),
        preferred_element_type=jnp.float32,
    ).astype(jnp.int32)
    chosen = (
        slot[:, :, None, :] == jnp.arange(capacity, dtype=jnp.int32)[:, None]
    ) & named[:, :, None, :]
    factor = jnp.sum(jnp.where(chosen, weight[:, :, None, :], 0.0), axis=3)
    factor = factor.reshape(4, 2 * layers * capacity, 1) * (top_h / FP8_LIMIT)
    choice = chosen.astype(jnp.bfloat16).reshape(4, 2 * layers, capacity, local_rows)
    spread = choice.transpose(0, 1, 3, 2)
    scales = jnp.stack([top_x / FP8_LIMIT, FP8_LIMIT / top_h])

    squares = sum(jnp.sum(part * part, axis=1) for part in stream)
    root = lax.rsqrt(squares / width + 1e-06)
    gains = [parts(norm_gain, c) for c in range(CHUNKS)]
    peak_x = jnp.max(
        jnp.stack([jnp.max(jnp.abs(s * root[:, None] * g)) for s, g in zip(stream, gains)])
    )
    gains = jnp.stack(gains) * (FP8_LIMIT / top_x)

    gate_rows = w_gate.reshape(1, owners, CHUNKS, columns, -1)
    up_rows = w_up.reshape(1, owners, CHUNKS, columns, -1)

    def hidden_of(r, choice):
        rows, pieces = groups[r]
        return gate_up(scales, gains, choice[r], rows, pieces, gate_rows, up_rows)

    along_x, along_y = neighbours(own)
    first = [[own], [along_x], [along_y]]
    along_x, along_y, sent = tie(along_x, along_y, sent)
    across = diagonal(along_x, along_y)

    def at_middle_hop(hop, arrived):
        nonlocal across
        if hop == 2:
            arrived, across = tie(arrived, across)
        return arrived

    own = along_tensor(sent, at_middle_hop)
    first = [rows_of(choice[r], both_cores(p)) for r, p in enumerate(first + [across])]
    along_x, along_y = neighbours(own)
    groups = [(first[0], both_cores([own]))]
    hidden = [hidden_of(0, choice)]
    stream = natural(stream, columns)
    along_x, along_y, hidden[0], stream, first, choice, spread, factor = tie(
        along_x, along_y, hidden[0], stream, first, choice, spread, factor
    )
    across = diagonal(along_x, along_y)
    groups += [(first[1], both_cores([along_x])), (first[2], both_cores([along_y]))]
    hidden += [hidden_of(1, choice), hidden_of(2, choice)]
    across, hidden = tie(across, hidden)
    groups.append((first[3], both_cores(across)))

    def outputs(r, c):
        return down(hidden[r][0], w_down, factor[r], spread[r], c, step)

    def halves(kept, given):
        taken = swap(given, 1)
        return [(kept[:half], taken[:half]), (kept[half:], taken[half:])]

    summed = lambda r, c: [add(*terms) for terms in halves(*outputs(r, c))]
    to_x, to_y = summed(1, 0), summed(2, 0)
    groups[3], to_x, to_y = tie(groups[3], to_x, to_y)
    hidden.append(hidden_of(3, choice))
    peak_h = jnp.max(jnp.stack([peaks for _, peaks in hidden]))
    mixture = []
    for c in range(CHUNKS):
        early_x, early_y = swap(to_x[0], 2), swap(to_y[1], 4)
        kept, given = outputs(3, c)
        if c == 0:
            given, early_x, early_y = tie(given, early_x, early_y)
        beyond = [add(*terms) for terms in halves(kept, given)]
        if c > 0:
            beyond, early_x, early_y, mixed = tie(beyond, early_x, early_y, mixed)
            mixture.append(lax.psum_scatter(mixed, "tensor", scatter_dimension=0, tiled=True))
        over_x, over_y = swap(beyond[0], 2), swap(beyond[1], 4)
        to_own = outputs(0, c)
        if c + 1 < CHUNKS:
            coming = outputs(1, c + 1), outputs(2, c + 1)
            over_x, over_y, to_own, coming = tie(over_x, over_y, to_own, coming)
        late_x, late_y = add(to_x[1], over_y), add(to_y[0], over_x)
        if c + 1 < CHUNKS:
            late_x, late_y, hidden = tie(late_x, late_y, hidden)
            to_x, to_y = ([add(*terms) for terms in halves(*pair)] for pair in coming)
        to_own = halves(*to_own)
        low = add(*to_own[0], early_x, swap(late_y, 4))
        high = add(*to_own[1], swap(late_x, 2), early_y)
        mixed = jnp.concatenate([low, high]).reshape(layers * local_rows, step)
    mixed, mixture = tie(mixed, mixture)
    mixture.append(lax.psum_scatter(mixed, "tensor", scatter_dimension=0, tiled=True))
    layer_out = stream + jnp.concatenate(mixture, axis=1).astype(jnp.float32)
    return layer_out.astype(jnp.bfloat16), peak_x, peak_h


def body(
    attn_out,
    out_weight,
    residual,
    norm_gain,
    expert_ids,
    route_weight,
    w_gate,
    w_up,
    w_down,
    history_x,
    history_h,
):
    experts = lax.axis_size("dp") * lax.axis_size("tensor")
    local_rows, top_count = expert_ids.shape
    capacity = max(2, 3 * local_rows * top_count // (2 * experts))
    top_x, top_h = jnp.max(history_x), jnp.max(history_h)
    gathers = lax.axis_size("dp") == 8 and local_rows < 4 * capacity
    plan = gather_plan if gathers else exchange_plan
    layer_out, peak_x, peak_h = plan(
        attn_out,
        out_weight,
        residual,
        norm_gain,
        expert_ids,
        route_weight,
        w_gate,
        w_up,
        w_down,
        top_x,
        top_h,
        capacity,
    )
    peaks = peaks_over_all(jnp.stack([peak_x, peak_h]))
    new_history_x = jnp.concatenate([peaks[:1], history_x[:-1]])
    new_history_h = jnp.concatenate([peaks[1:], history_h[:-1]])
    return (layer_out, new_history_x, new_history_h)


def solution(mesh):
    in_specs = (
        P("dp", "tensor"),
        P("tensor", "dp"),
        P(AXES, None),
        P(),
        P(AXES, None),
        P(AXES, None),
        P(AXES, None, None),
        P(AXES, None, None),
        P(AXES, None, None),
        P(),
        P(),
    )
    out_specs = (P(AXES, None), P(), P())
    return jax.shard_map(body, mesh=mesh, in_specs=in_specs, out_specs=out_specs, check_vma=False)
```

```python
import functools

import jax
import jax.numpy as jnp
from jax import lax
from jax.experimental import pallas as pl
from jax.experimental.pallas import tpu as pltpu
from jax.sharding import PartitionSpec as P

FP8_LIMIT = 448.0
AXES = ("dp", "tensor")
CHUNKS = 2
VMEM_LIMIT = 58 * 2**20
COST_SHARE = 16


def project(attn_out, out_weight):
    head_terms = jnp.dot(
        attn_out,
        lax.all_gather(out_weight, "dp", axis=1, tiled=True),
        preferred_element_type=jnp.float32,
    )
    return lax.psum_scatter(
        head_terms.astype(jnp.bfloat16), "tensor", scatter_dimension=0, tiled=True
    ).astype(jnp.float32)


def peaks_over_all(peaks):
    for axis in AXES:
        count = lax.axis_size(axis)
        shift = 1
        while shift < count:
            pairs = [(i, (i + shift) % count) for i in range(count)]
            peaks = jnp.maximum(peaks, lax.ppermute(peaks, axis, pairs))
            shift *= 2
    return peaks


def slots_of(ids, experts, capacity):
    flat_ids = ids.reshape(-1)
    onehot = (flat_ids[:, None] == jnp.arange(experts, dtype=jnp.int32)[None, :]).astype(jnp.int32)
    before = jnp.cumsum(onehot, axis=0) - onehot
    return flat_ids * capacity + jnp.sum(before * onehot, axis=-1)


def exchange_plan(
    attn_out,
    out_weight,
    residual,
    norm_gain,
    expert_ids,
    route_weight,
    w_gate,
    w_up,
    w_down,
    top_x,
    top_h,
    capacity,
):
    experts = lax.axis_size("dp") * lax.axis_size("tensor")
    inv_x, inv_h, scale_h = top_x / FP8_LIMIT, top_h / FP8_LIMIT, FP8_LIMIT / top_h
    local_rows, width = residual.shape
    top_count = expert_ids.shape[1]
    stream = residual.astype(jnp.float32) + project(attn_out, out_weight)
    normed = (
        stream * lax.rsqrt(jnp.mean(stream * stream, axis=-1, keepdims=True) + 1e-06) * norm_gain
    )
    quantized = jnp.clip(normed * (FP8_LIMIT / top_x), -FP8_LIMIT, FP8_LIMIT).astype(jnp.bfloat16)
    position = slots_of(expert_ids, experts, capacity)
    matches = (
        position.reshape(local_rows, top_count)[:, :, None]
        == jnp.arange(experts * capacity, dtype=jnp.int32)[None, None, :]
    )
    placing = jnp.sum(matches.astype(jnp.int32), axis=1).astype(jnp.bfloat16)
    outgoing = lax.dot_general(
        placing, quantized, (((0,), (0,)), ((), ())), preferred_element_type=jnp.float32
    )
    outgoing = outgoing.astype(jnp.bfloat16).reshape(experts, capacity, width)
    token_block = lax.all_to_all(outgoing, AXES, split_axis=0, concat_axis=0, tiled=True)
    flat_rows = token_block.reshape(-1, width)
    gate = jnp.dot(flat_rows, w_gate[0], preferred_element_type=jnp.float32) * inv_x
    upper = jnp.dot(flat_rows, w_up[0], preferred_element_type=jnp.float32) * inv_x
    hidden = jax.nn.silu(gate) * upper
    hidden_q = jnp.clip(hidden * scale_h, -FP8_LIMIT, FP8_LIMIT).astype(jnp.bfloat16)
    expert_out = (jnp.dot(hidden_q, w_down[0], preferred_element_type=jnp.float32) * inv_h).astype(
        jnp.bfloat16
    )
    returned = lax.all_to_all(
        expert_out.reshape(experts, capacity, width), AXES, split_axis=0, concat_axis=0, tiled=True
    )
    picked = returned.reshape(-1, width)[position].reshape(local_rows, top_count, width)
    mixture = jnp.sum(picked.astype(jnp.float32) * route_weight[:, :, None], axis=1)
    peaks = jnp.max(jnp.abs(normed)), jnp.max(jnp.abs(hidden))
    return (stream + mixture).astype(jnp.bfloat16), *peaks


def cost(flops, bytes_accessed):
    return pl.CostEstimate(
        flops=flops // COST_SHARE, bytes_accessed=bytes_accessed // COST_SHARE, transcendentals=0
    )


def swap(value, bits):
    count = lax.axis_size("dp")
    return lax.ppermute(value, "dp", [(i, i ^ bits) for i in range(count)])


def along_tensor(value, at_hop=None):
    count, here = lax.axis_size("tensor"), lax.axis_index("tensor")
    passed = [(value, value)]
    for hop in range(1, count):
        up = [(i, i + 1) for i in range(hop - 1, count - 1)]
        back = [(count - 1 - i, count - 1 - j) for i, j in up]
        below, above = passed[-1]
        arrived = lax.ppermute(below, "tensor", up), lax.ppermute(above, "tensor", back)
        passed.append(at_hop(hop, arrived) if at_hop else arrived)
    blocks = jnp.zeros((count,) + value.shape, value.dtype)
    blocks = lax.dynamic_update_index_in_dim(blocks, value, here, 0)
    for hop in range(1, count):
        block = jnp.where(here >= hop, passed[hop][0], passed[count - hop][1])
        blocks = lax.dynamic_update_index_in_dim(blocks, block, (here - hop) % count, 0)
    return blocks


def chip_table(expert_ids, route_weight, experts):
    names = jnp.arange(experts, dtype=jnp.int32)[:, None, None]
    table = jnp.sum(jnp.where(expert_ids[None] == names, route_weight[None], 0.0), axis=2)
    count = lax.axis_size("tensor")
    parts = [table]
    for shift in range(1, count):
        pairs = [(i, (i + shift) % count) for i in range(count)]
        parts.append(lax.ppermute(table, "tensor", pairs))
    order = (lax.axis_index("tensor") - jnp.arange(count)) % count
    table = jnp.stack(parts)[order][None]
    return jnp.concatenate([table, swap(table, 1)])


def expert_weights(table):
    for bit in (2, 4):
        table = jnp.concatenate([table, swap(table, bit)])
    mine = lax.axis_index("dp") * lax.axis_size("tensor") + lax.axis_index("tensor")
    return lax.dynamic_index_in_dim(table, mine, axis=2, keepdims=False)


def neighbours(value):
    return swap(value, 2), swap(value, 4)


def diagonal(along_x, along_y):
    half = along_x.shape[0] // 2
    return [swap(along_x[:half], 4), swap(along_y[half:], 2)]


def both_cores(group):
    return group + [swap(piece, 1) for piece in group]


def tie(*values):
    return lax.optimization_barrier(values)


def project_kernel(place_ref, attn_ref, *refs):
    out_ref, joined, stage = refs[-3:]
    pieces = refs[:-3]
    columns = pieces[0].shape[0]
    attn = attn_ref[...]
    blocks = [pieces[0], pieces[1], pieces[2], pieces[3], pieces[4], pieces[5], None, None]
    for k, block in enumerate(blocks):
        if block is None:
            low, high = pieces[2 * k - 6], pieces[2 * k - 5]
            joined[: low.shape[0]] = low[...]
            joined[low.shape[0] :] = high[...]
            block = joined
        terms = lax.dot_general(
            attn, block[...], (((1,), (1,)), ((), ())), preferred_element_type=jnp.float32
        )
        stage[place_ref[0] ^ k, :, :columns] = terms
    for j in range(stage.shape[0]):
        out_ref[:, j * columns : (j + 1) * columns] = stage[j, :, :columns].astype(out_ref.dtype)


def project_part(place, attn_out, groups):
    rows, depth = attn_out.shape
    pieces = [piece for group in groups for piece in group]
    columns = pieces[0].shape[0]
    return pl.pallas_call(
        project_kernel,
        in_specs=[pl.BlockSpec(memory_space=pltpu.SMEM)]
        + [pl.BlockSpec(memory_space=pltpu.VMEM)] * (1 + len(pieces)),
        out_specs=pl.BlockSpec(memory_space=pltpu.VMEM),
        out_shape=jax.ShapeDtypeStruct((rows, 8 * columns), jnp.bfloat16),
        scratch_shapes=[
            pltpu.VMEM((columns, depth), jnp.bfloat16),
            pltpu.VMEM((8, rows, -(-columns // 128) * 128), jnp.float32),
        ],
        compiler_params=pltpu.CompilerParams(vmem_limit_bytes=VMEM_LIMIT),
        cost_estimate=cost(16 * rows * depth * columns, 2 * depth * (rows + 8 * columns)),
        name="project",
    )(place, attn_out, *pieces)


def pick(chosen_ref, pieces):
    source = 0
    for piece in pieces:
        for i in range(piece.shape[0]):
            yield jnp.dot(chosen_ref[source], piece[i], preferred_element_type=jnp.float32)
            source += 1


def rows_kernel(chosen_ref, *refs):
    *pieces, rows_ref, squares_ref = refs
    capacity = chosen_ref.shape[1]
    for source, picked in enumerate(pick(chosen_ref, pieces)):
        span = slice(source * capacity, (source + 1) * capacity)
        rows_ref[span] = picked.astype(rows_ref.dtype)
        squares_ref[span] = jnp.sum(picked * picked, axis=1, keepdims=True)


def rows_of(chosen, pieces):
    sources, capacity, tokens = chosen.shape
    rows, step = sources * capacity, pieces[0].shape[-1]
    return pl.pallas_call(
        rows_kernel,
        out_shape=[
            jax.ShapeDtypeStruct((rows, step), jnp.bfloat16),
            jax.ShapeDtypeStruct((rows, 1), jnp.float32),
        ],
        compiler_params=pltpu.CompilerParams(vmem_limit_bytes=VMEM_LIMIT),
        cost_estimate=cost(2 * rows * step * tokens, 2 * step * sources * tokens),
        name="rows",
    )(chosen, *pieces)


def gate_up_kernel(scale_ref, gain_ref, chosen_ref, first_ref, squares_ref, *refs):
    hidden_ref, peak_ref, rows = refs[-3:]
    weights, pieces = refs[-7:-3], refs[:-7]
    capacity = chosen_ref.shape[1]
    step = rows.shape[2]

    @pl.when(pl.program_id(0) == 0)
    def _():
        for source, picked in enumerate(pick(chosen_ref, pieces)):
            span = slice(source * capacity, (source + 1) * capacity)
            squares = squares_ref[span] + jnp.sum(picked * picked, axis=1, keepdims=True)
            root = lax.rsqrt(squares / (2 * step) + 1e-06)
            for c, x in enumerate((first_ref[span].astype(jnp.float32), picked)):
                x = jnp.clip(x * root * gain_ref[c], -FP8_LIMIT, FP8_LIMIT)
                rows[c, span] = x.astype(rows.dtype)

    def product(side):
        return sum(
            jnp.dot(
                rows[c],
                weights[2 * c + side][0].reshape(step, -1),
                preferred_element_type=jnp.float32,
            )
            for c in range(2)
        )

    gate, up = product(0) * scale_ref[0], product(1) * scale_ref[0]
    hidden = gate / (1.0 + jnp.exp(-gate)) * up
    scaled = jnp.clip(hidden * scale_ref[1], -FP8_LIMIT, FP8_LIMIT)
    hidden_ref[...] = scaled.astype(hidden_ref.dtype)
    peak = jnp.broadcast_to(jnp.max(jnp.abs(hidden)), peak_ref.shape)
    first = pl.program_id(0) == 0
    peak_ref[...] = jnp.where(first, peak, jnp.maximum(peak_ref[...], peak))


def gate_up(scales, gains, chosen, first, pieces, w_gate, w_up):
    sources, capacity, tokens = chosen.shape
    parts, _, step = gains.shape
    owners, columns, hidden = w_gate.shape[1], w_gate.shape[3], w_gate.shape[-1]
    tile = min(256, hidden)
    rows = sources * capacity
    once = pl.Buffered(buffer_count=1)
    whole = lambda a: pl.BlockSpec(a.shape, lambda n: (0,) * a.ndim, pipeline_mode=once)
    weight = lambda c: pl.BlockSpec((1, owners, None, columns, tile), lambda n: (0, 0, c, 0, n))
    return pl.pallas_call(
        gate_up_kernel,
        grid=(hidden // tile,),
        in_specs=[pl.BlockSpec(memory_space=pltpu.SMEM), whole(gains), whole(chosen)]
        + [whole(a) for a in first]
        + [whole(p) for p in pieces]
        + [weight(c) for c in range(parts) for _ in range(2)],
        out_specs=[
            pl.BlockSpec((rows, tile), lambda n: (0, n)),
            pl.BlockSpec((8, 128), lambda n: (0, 0)),
        ],
        out_shape=[
            jax.ShapeDtypeStruct((rows, hidden), jnp.bfloat16),
            jax.ShapeDtypeStruct((8, 128), jnp.float32),
        ],
        scratch_shapes=[pltpu.VMEM((parts, rows, step), jnp.bfloat16)],
        compiler_params=pltpu.CompilerParams(vmem_limit_bytes=VMEM_LIMIT),
        cost_estimate=cost(
            2 * rows * parts * step * (2 * hidden + tokens),
            2 * parts * step * (2 * hidden + sources * tokens),
        ),
        name="gate_up",
    )(scales, gains, chosen, *first, *pieces, *([w_gate, w_up] * parts))


def down_kernel(hidden_ref, down_w, factor_ref, spread_ref, own_ref, other_ref):
    sources, tokens, capacity = spread_ref.shape
    terms = jnp.dot(hidden_ref[...], down_w[0], preferred_element_type=jnp.float32)
    terms = (terms * factor_ref[...]).astype(jnp.bfloat16)
    half = sources // 2
    for source in range(sources):
        spread = jnp.dot(
            spread_ref[source],
            terms[source * capacity : (source + 1) * capacity],
            preferred_element_type=jnp.float32,
        ).astype(jnp.bfloat16)
        if source < half:
            own_ref[source] = spread
        else:
            other_ref[source - half] = spread


def down(hidden_q, w_down, factor, spread, start, width):
    rows, hidden = hidden_q.shape
    sources, tokens, capacity = spread.shape
    tile = next(t for t in (1024, 512, 256, 128) if start % t == 0 and width % t == 0)
    whole = lambda shape: pl.BlockSpec(shape, lambda j: (0,) * len(shape))
    return pl.pallas_call(
        down_kernel,
        grid=(width // tile,),
        in_specs=[
            whole(hidden_q.shape),
            pl.BlockSpec((1, hidden, tile), lambda j: (0, 0, start // tile + j)),
            whole(factor.shape),
            whole(spread.shape),
        ],
        out_specs=[pl.BlockSpec((sources // 2, tokens, tile), lambda j: (0, 0, j))] * 2,
        out_shape=[jax.ShapeDtypeStruct((sources // 2, tokens, width), jnp.bfloat16)] * 2,
        compiler_params=pltpu.CompilerParams(vmem_limit_bytes=VMEM_LIMIT),
        cost_estimate=cost(
            2 * rows * width * (hidden + tokens), 2 * width * (hidden + sources * tokens)
        ),
        name="down",
    )(hidden_q, w_down, factor, spread)


def natural_kernel(columns, *refs):
    *parts, out_ref = refs
    for j in range(parts[0].shape[1] // columns):
        for c, part in enumerate(parts):
            place = (j * len(parts) + c) * columns
            out_ref[:, place : place + columns] = part[:, j * columns : (j + 1) * columns]


def natural(parts, columns):
    rows, step = parts[0].shape
    return pl.pallas_call(
        functools.partial(natural_kernel, columns),
        out_shape=jax.ShapeDtypeStruct((rows, step * len(parts)), parts[0].dtype),
        compiler_params=pltpu.CompilerParams(vmem_limit_bytes=VMEM_LIMIT),
        name="natural",
    )(*parts)


def add(*terms):
    return sum(t.astype(jnp.float32) for t in terms).astype(jnp.bfloat16)


def gather_plan(
    attn_out,
    out_weight,
    residual,
    norm_gain,
    expert_ids,
    route_weight,
    w_gate,
    w_up,
    w_down,
    top_x,
    top_h,
    capacity,
):
    owners, layers = lax.axis_size("dp"), lax.axis_size("tensor")
    experts = owners * layers
    local_rows, width = residual.shape
    half, step = layers // 2, width // CHUNKS
    columns = step // owners

    split = lambda value: value.reshape(-1, owners, CHUNKS, columns)
    parts = lambda value, c: split(value)[:, :, c].reshape(-1, step)
    place = lax.axis_index("dp")[None]

    def summed_over_tensor(terms, c):
        total = lax.psum_scatter(terms, "tensor", scatter_dimension=0, tiled=True)
        part = parts(residual, c).astype(jnp.float32) + total.astype(jnp.float32)
        return part, part.astype(jnp.bfloat16)

    weight_rows = list(out_weight.T.reshape(CHUNKS, columns, -1))
    near = neighbours(weight_rows[0])
    table = chip_table(expert_ids, route_weight, experts)
    near, table = tie(near, table)
    groups = [[weight_rows[0]], [near[0]], [near[1]], diagonal(*near)]
    terms = project_part(place, attn_out, [both_cores(group) for group in groups])
    terms, weight_rows[1] = tie(terms, weight_rows[1])
    near = neighbours(weight_rows[1])
    groups = [[weight_rows[1]], [near[0]], [near[1]], diagonal(*near)]
    groups = [both_cores(group) for group in groups]
    first, sent = summed_over_tensor(terms, 0)

    beside = {}

    def at_hop(hop, arrived):
        if hop == 1:
            arrived, tied, routes = tie(arrived, groups, table)
            beside["terms"] = project_part(place, attn_out, tied)
            beside["weight"] = expert_weights(routes)
        if hop == layers - 1:
            arrived, terms, weight = tie(arrived, beside["terms"], beside["weight"])
            beside["sum"], beside["weight"] = summed_over_tensor(terms, 1), weight
        return arrived

    own = along_tensor(sent, at_hop)
    along_x, along_y = neighbours(own)
    own = both_cores([own])
    weight = beside["weight"]
    second, sent = beside["sum"]
    stream = [first, second]

    named = weight > 0.0
    earlier = jnp.triu(jnp.ones((local_rows, local_rows), jnp.bfloat16), 1)
    slot = lax.dot_general(
        named.astype(jnp.bfloat16),
        earlier,
        (((2,), (0,)), ((), ())),
        preferred_element_type=jnp.float32,
    ).astype(jnp.int32)
    chosen = (
        slot[:, :, None, :] == jnp.arange(capacity, dtype=jnp.int32)[:, None]
    ) & named[:, :, None, :]
    factor = jnp.sum(jnp.where(chosen, weight[:, :, None, :], 0.0), axis=3)
    factor = list(factor.reshape(4, 2 * layers * capacity, 1) * (top_h / FP8_LIMIT))
    choice = chosen.astype(jnp.bfloat16).reshape(4, 2 * layers, capacity, local_rows)
    spread = list(choice.transpose(0, 1, 3, 2))
    choice = list(choice)
    scales = jnp.stack([top_x / FP8_LIMIT, FP8_LIMIT / top_h])

    squares = sum(jnp.sum(part * part, axis=1) for part in stream)
    root = lax.rsqrt(squares / width + 1e-06)
    gains = [parts(norm_gain, c) for c in range(CHUNKS)]
    peak_x = jnp.max(
        jnp.stack([jnp.max(jnp.abs(s * root[:, None] * g)) for s, g in zip(stream, gains)])
    )
    gains = jnp.stack(gains) * (FP8_LIMIT / top_x)

    gate_rows = w_gate.reshape(1, owners, CHUNKS, columns, -1)
    up_rows = w_up.reshape(1, owners, CHUNKS, columns, -1)

    def hidden_of(r, choice):
        rows, pieces = groups[r]
        return gate_up(scales, gains, choice[r], rows, pieces, gate_rows, up_rows)

    own, sent = tie(own, sent)

    def at_middle_hop(hop, arrived):
        nonlocal along_x, along_y, across
        if hop == 1:
            arrived, along_x, along_y = tie(arrived, along_x, along_y)
            across = diagonal(along_x, along_y)
        if hop == layers - 1:
            arrived, across = tie(arrived, across)
        return arrived

    across = []
    later = along_tensor(sent, at_middle_hop)
    first = [own, both_cores([along_x]), both_cores([along_y])]
    own = later
    first = [rows_of(choice[r], p) for r, p in enumerate(first + [both_cores(across)])]
    along_x, along_y = neighbours(own)
    groups = [(first[0], both_cores([own]))]
    hidden = [hidden_of(0, choice)]
    stream = natural(stream, columns)
    along_x, along_y, hidden[0], stream, first, choice, spread, factor = tie(
        along_x, along_y, hidden[0], stream, first, choice, spread, factor
    )
    across = diagonal(along_x, along_y)
    groups += [(first[1], both_cores([along_x])), (first[2], both_cores([along_y]))]
    hidden += [hidden_of(1, choice), hidden_of(2, choice)]
    across, hidden = tie(across, hidden)
    groups.append((first[3], both_cores(across)))

    unit = 512 if width % 512 == 0 else 128
    cut = (width // unit + 1) // 2 * unit
    spans = [(0, cut), (cut, width - cut)]

    def outputs(r, c):
        return down(hidden[r][0], w_down, factor[r], spread[r], *spans[c])

    def halves(kept, given):
        taken = swap(given, 1)
        return [(kept[:half], taken[:half]), (kept[half:], taken[half:])]

    summed = lambda r, c: [add(*terms) for terms in halves(*outputs(r, c))]
    to_x, to_y = summed(1, 0), summed(2, 0)
    groups[3], to_x, to_y = tie(groups[3], to_x, to_y)
    hidden.append(hidden_of(3, choice))
    peak_h = jnp.max(jnp.stack([peaks for _, peaks in hidden]))
    mixture = []
    for c in range(CHUNKS):
        early_x, early_y = swap(to_x[0], 2), swap(to_y[1], 4)
        kept, given = outputs(3, c)
        if c == 0:
            given, early_x, early_y = tie(given, early_x, early_y)
        beyond = [add(*terms) for terms in halves(kept, given)]
        if c > 0:
            beyond, early_x, early_y, mixed = tie(beyond, early_x, early_y, mixed)
            mixture.append(lax.psum_scatter(mixed, "tensor", scatter_dimension=0, tiled=True))
        over_x, over_y = swap(beyond[0], 2), swap(beyond[1], 4)
        to_own = outputs(0, c)
        if c + 1 < CHUNKS:
            coming = outputs(1, c + 1), outputs(2, c + 1)
            over_x, over_y, to_own, coming = tie(over_x, over_y, to_own, coming)
        late_x, late_y = add(to_x[1], over_y), add(to_y[0], over_x)
        if c + 1 < CHUNKS:
            late_x, late_y, hidden = tie(late_x, late_y, hidden)
            to_x, to_y = ([add(*terms) for terms in halves(*pair)] for pair in coming)
        to_own = halves(*to_own)
        low = add(*to_own[0], early_x, swap(late_y, 4))
        high = add(*to_own[1], swap(late_x, 2), early_y)
        mixed = jnp.concatenate([low, high]).reshape(layers * local_rows, -1)
    mixed, mixture = tie(mixed, mixture)
    mixture.append(lax.psum_scatter(mixed, "tensor", scatter_dimension=0, tiled=True))
    layer_out = stream + jnp.concatenate(mixture, axis=1).astype(jnp.float32)
    return layer_out.astype(jnp.bfloat16), peak_x, peak_h


def body(
    attn_out,
    out_weight,
    residual,
    norm_gain,
    expert_ids,
    route_weight,
    w_gate,
    w_up,
    w_down,
    history_x,
    history_h,
):
    experts = lax.axis_size("dp") * lax.axis_size("tensor")
    local_rows, top_count = expert_ids.shape
    capacity = max(2, 3 * local_rows * top_count // (2 * experts))
    top_x, top_h = jnp.max(history_x), jnp.max(history_h)
    gathers = lax.axis_size("dp") == 8 and local_rows < 4 * capacity
    plan = gather_plan if gathers else exchange_plan
    layer_out, peak_x, peak_h = plan(
        attn_out,
        out_weight,
        residual,
        norm_gain,
        expert_ids,
        route_weight,
        w_gate,
        w_up,
        w_down,
        top_x,
        top_h,
        capacity,
    )
    peaks = peaks_over_all(jnp.stack([peak_x, peak_h]))
    new_history_x = jnp.concatenate([peaks[:1], history_x[:-1]])
    new_history_h = jnp.concatenate([peaks[1:], history_h[:-1]])
    return (layer_out, new_history_x, new_history_h)


def solution(mesh):
    in_specs = (
        P("dp", "tensor"),
        P("tensor", "dp"),
        P(AXES, None),
        P(),
        P(AXES, None),
        P(AXES, None),
        P(AXES, None, None),
        P(AXES, None, None),
        P(AXES, None, None),
        P(),
        P(),
    )
    out_specs = (P(AXES, None), P(), P())
    return jax.shard_map(body, mesh=mesh, in_specs=in_specs, out_specs=out_specs, check_vma=False)
```

```python
import functools

import jax
import jax.numpy as jnp
from jax import lax
from jax.experimental import pallas as pl
from jax.experimental.pallas import tpu as pltpu
from jax.sharding import PartitionSpec as P

FP8_LIMIT = 448.0
AXES = ("dp", "tensor")
CHUNKS = 2
VMEM_LIMIT = 48 * 2**20
COST_SHARE = 16


def project(attn_out, out_weight):
    head_terms = jnp.dot(
        attn_out,
        lax.all_gather(out_weight, "dp", axis=1, tiled=True),
        preferred_element_type=jnp.float32,
    )
    return lax.psum_scatter(
        head_terms.astype(jnp.bfloat16), "tensor", scatter_dimension=0, tiled=True
    ).astype(jnp.float32)


def peaks_over_all(peaks):
    for axis in AXES:
        count = lax.axis_size(axis)
        shift = 1
        while shift < count:
            pairs = [(i, (i + shift) % count) for i in range(count)]
            peaks = jnp.maximum(peaks, lax.ppermute(peaks, axis, pairs))
            shift *= 2
    return peaks


def slots_of(ids, experts, capacity):
    flat_ids = ids.reshape(-1)
    onehot = (flat_ids[:, None] == jnp.arange(experts, dtype=jnp.int32)[None, :]).astype(jnp.int32)
    before = jnp.cumsum(onehot, axis=0) - onehot
    return flat_ids * capacity + jnp.sum(before * onehot, axis=-1)


def exchange_plan(
    attn_out,
    out_weight,
    residual,
    norm_gain,
    expert_ids,
    route_weight,
    w_gate,
    w_up,
    w_down,
    top_x,
    top_h,
    capacity,
):
    experts = lax.axis_size("dp") * lax.axis_size("tensor")
    inv_x, inv_h, scale_h = top_x / FP8_LIMIT, top_h / FP8_LIMIT, FP8_LIMIT / top_h
    local_rows, width = residual.shape
    top_count = expert_ids.shape[1]
    stream = residual.astype(jnp.float32) + project(attn_out, out_weight)
    normed = (
        stream * lax.rsqrt(jnp.mean(stream * stream, axis=-1, keepdims=True) + 1e-06) * norm_gain
    )
    quantized = jnp.clip(normed * (FP8_LIMIT / top_x), -FP8_LIMIT, FP8_LIMIT).astype(jnp.bfloat16)
    position = slots_of(expert_ids, experts, capacity)
    matches = (
        position.reshape(local_rows, top_count)[:, :, None]
        == jnp.arange(experts * capacity, dtype=jnp.int32)[None, None, :]
    )
    placing = jnp.sum(matches.astype(jnp.int32), axis=1).astype(jnp.bfloat16)
    outgoing = lax.dot_general(
        placing, quantized, (((0,), (0,)), ((), ())), preferred_element_type=jnp.float32
    )
    outgoing = outgoing.astype(jnp.bfloat16).reshape(experts, capacity, width)
    token_block = lax.all_to_all(outgoing, AXES, split_axis=0, concat_axis=0, tiled=True)
    flat_rows = token_block.reshape(-1, width)
    gate = jnp.dot(flat_rows, w_gate[0], preferred_element_type=jnp.float32) * inv_x
    upper = jnp.dot(flat_rows, w_up[0], preferred_element_type=jnp.float32) * inv_x
    hidden = jax.nn.silu(gate) * upper
    hidden_q = jnp.clip(hidden * scale_h, -FP8_LIMIT, FP8_LIMIT).astype(jnp.bfloat16)
    expert_out = (jnp.dot(hidden_q, w_down[0], preferred_element_type=jnp.float32) * inv_h).astype(
        jnp.bfloat16
    )
    returned = lax.all_to_all(
        expert_out.reshape(experts, capacity, width), AXES, split_axis=0, concat_axis=0, tiled=True
    )
    picked = returned.reshape(-1, width)[position].reshape(local_rows, top_count, width)
    mixture = jnp.sum(picked.astype(jnp.float32) * route_weight[:, :, None], axis=1)
    peaks = jnp.max(jnp.abs(normed)), jnp.max(jnp.abs(hidden))
    return (stream + mixture).astype(jnp.bfloat16), *peaks


def cost(flops, bytes_accessed):
    return pl.CostEstimate(
        flops=flops // COST_SHARE, bytes_accessed=bytes_accessed // COST_SHARE, transcendentals=0
    )


def swap(value, bits):
    count = lax.axis_size("dp")
    return lax.ppermute(value, "dp", [(i, i ^ bits) for i in range(count)])


def along_tensor(value, at_hop=None):
    count, here = lax.axis_size("tensor"), lax.axis_index("tensor")
    passed = [(value, value)]
    for hop in range(1, count):
        up = [(i, i + 1) for i in range(hop - 1, count - 1)]
        back = [(count - 1 - i, count - 1 - j) for i, j in up]
        below, above = passed[-1]
        arrived = lax.ppermute(below, "tensor", up), lax.ppermute(above, "tensor", back)
        passed.append(at_hop(hop, arrived) if at_hop else arrived)
    blocks = jnp.zeros((count,) + value.shape, value.dtype)
    blocks = lax.dynamic_update_index_in_dim(blocks, value, here, 0)
    for hop in range(1, count):
        block = jnp.where(here >= hop, passed[hop][0], passed[count - hop][1])
        blocks = lax.dynamic_update_index_in_dim(blocks, block, (here - hop) % count, 0)
    return blocks


def chip_table(expert_ids, route_weight, experts):
    names = jnp.arange(experts, dtype=jnp.int32)[:, None, None]
    table = jnp.sum(jnp.where(expert_ids[None] == names, route_weight[None], 0.0), axis=2)
    count = lax.axis_size("tensor")
    parts = [table]
    for shift in range(1, count):
        pairs = [(i, (i + shift) % count) for i in range(count)]
        parts.append(lax.ppermute(table, "tensor", pairs))
    order = (lax.axis_index("tensor") - jnp.arange(count)) % count
    table = jnp.stack(parts)[order][None]
    return jnp.concatenate([table, swap(table, 1)])


def expert_weights(table):
    for bit in (2, 4):
        table = jnp.concatenate([table, swap(table, bit)])
    mine = lax.axis_index("dp") * lax.axis_size("tensor") + lax.axis_index("tensor")
    return lax.dynamic_index_in_dim(table, mine, axis=2, keepdims=False)


def neighbours(value):
    return swap(value, 2), swap(value, 4)


def diagonal(along_x, along_y):
    half = along_x.shape[0] // 2
    return [swap(along_x[:half], 4), swap(along_y[half:], 2)]


def both_cores(group):
    return group + [swap(piece, 1) for piece in group]


def tie(*values):
    return lax.optimization_barrier(values)


def project_kernel(place_ref, attn_ref, *refs):
    out_ref, joined, stage = refs[-3:]
    pieces = refs[:-3]
    columns = pieces[0].shape[0]
    attn = attn_ref[...]
    blocks = [pieces[0], pieces[1], pieces[2], pieces[3], pieces[4], pieces[5], None, None]
    for k, block in enumerate(blocks):
        if block is None:
            low, high = pieces[2 * k - 6], pieces[2 * k - 5]
            joined[: low.shape[0]] = low[...]
            joined[low.shape[0] :] = high[...]
            block = joined
        terms = lax.dot_general(
            attn, block[...], (((1,), (1,)), ((), ())), preferred_element_type=jnp.float32
        )
        stage[place_ref[0] ^ k, :, :columns] = terms
    for j in range(stage.shape[0]):
        out_ref[:, j * columns : (j + 1) * columns] = stage[j, :, :columns].astype(out_ref.dtype)


def project_part(place, attn_out, groups):
    rows, depth = attn_out.shape
    pieces = [piece for group in groups for piece in group]
    columns = pieces[0].shape[0]
    return pl.pallas_call(
        project_kernel,
        in_specs=[pl.BlockSpec(memory_space=pltpu.SMEM)]
        + [pl.BlockSpec(memory_space=pltpu.VMEM)] * (1 + len(pieces)),
        out_specs=pl.BlockSpec(memory_space=pltpu.VMEM),
        out_shape=jax.ShapeDtypeStruct((rows, 8 * columns), jnp.bfloat16),
        scratch_shapes=[
            pltpu.VMEM((columns, depth), jnp.bfloat16),
            pltpu.VMEM((8, rows, -(-columns // 128) * 128), jnp.float32),
        ],
        compiler_params=pltpu.CompilerParams(vmem_limit_bytes=VMEM_LIMIT),
        cost_estimate=cost(16 * rows * depth * columns, 2 * depth * (rows + 8 * columns)),
        name="project",
    )(place, attn_out, *pieces)


def pick(chosen_ref, pieces):
    source = 0
    for piece in pieces:
        for i in range(piece.shape[0]):
            yield jnp.dot(chosen_ref[source], piece[i], preferred_element_type=jnp.float32)
            source += 1


def rows_kernel(chosen_ref, *refs):
    *pieces, rows_ref, squares_ref = refs
    capacity = chosen_ref.shape[1]
    for source, picked in enumerate(pick(chosen_ref, pieces)):
        span = slice(source * capacity, (source + 1) * capacity)
        rows_ref[span] = picked.astype(rows_ref.dtype)
        squares_ref[span] = jnp.sum(picked * picked, axis=1, keepdims=True)


def rows_of(chosen, pieces):
    sources, capacity, tokens = chosen.shape
    rows, step = sources * capacity, pieces[0].shape[-1]
    return pl.pallas_call(
        rows_kernel,
        out_shape=[
            jax.ShapeDtypeStruct((rows, step), jnp.bfloat16),
            jax.ShapeDtypeStruct((rows, 1), jnp.float32),
        ],
        compiler_params=pltpu.CompilerParams(vmem_limit_bytes=VMEM_LIMIT),
        cost_estimate=cost(2 * rows * step * tokens, 2 * step * sources * tokens),
        name="rows",
    )(chosen, *pieces)


def gate_up_kernel(scale_ref, gain_ref, chosen_ref, first_ref, squares_ref, *refs):
    hidden_ref, peak_ref, rows = refs[-3:]
    weights, pieces = refs[-7:-3], refs[:-7]
    capacity = chosen_ref.shape[1]
    step = rows.shape[2]

    @pl.when(pl.program_id(0) == 0)
    def _():
        for source, picked in enumerate(pick(chosen_ref, pieces)):
            span = slice(source * capacity, (source + 1) * capacity)
            squares = squares_ref[span] + jnp.sum(picked * picked, axis=1, keepdims=True)
            root = lax.rsqrt(squares / (2 * step) + 1e-06)
            for c, x in enumerate((first_ref[span].astype(jnp.float32), picked)):
                x = jnp.clip(x * root * gain_ref[c], -FP8_LIMIT, FP8_LIMIT)
                rows[c, span] = x.astype(rows.dtype)

    def product(side):
        return sum(
            jnp.dot(
                rows[c],
                weights[2 * c + side][0].reshape(step, -1),
                preferred_element_type=jnp.float32,
            )
            for c in range(2)
        )

    gate, up = product(0) * scale_ref[0], product(1) * scale_ref[0]
    hidden = gate / (1.0 + jnp.exp(-gate)) * up
    scaled = jnp.clip(hidden * scale_ref[1], -FP8_LIMIT, FP8_LIMIT)
    hidden_ref[...] = scaled.astype(hidden_ref.dtype)
    peak = jnp.broadcast_to(jnp.max(jnp.abs(hidden)), peak_ref.shape)
    first = pl.program_id(0) == 0
    peak_ref[...] = jnp.where(first, peak, jnp.maximum(peak_ref[...], peak))


def gate_up(scales, gains, chosen, first, pieces, w_gate, w_up):
    sources, capacity, tokens = chosen.shape
    parts, _, step = gains.shape
    owners, columns, hidden = w_gate.shape[1], w_gate.shape[3], w_gate.shape[-1]
    tile = min(256, hidden)
    rows = sources * capacity
    once = pl.Buffered(buffer_count=1)
    whole = lambda a: pl.BlockSpec(a.shape, lambda n: (0,) * a.ndim, pipeline_mode=once)
    weight = lambda c: pl.BlockSpec((1, owners, None, columns, tile), lambda n: (0, 0, c, 0, n))
    return pl.pallas_call(
        gate_up_kernel,
        grid=(hidden // tile,),
        in_specs=[pl.BlockSpec(memory_space=pltpu.SMEM), whole(gains), whole(chosen)]
        + [whole(a) for a in first]
        + [whole(p) for p in pieces]
        + [weight(c) for c in range(parts) for _ in range(2)],
        out_specs=[
            pl.BlockSpec((rows, tile), lambda n: (0, n)),
            pl.BlockSpec((8, 128), lambda n: (0, 0)),
        ],
        out_shape=[
            jax.ShapeDtypeStruct((rows, hidden), jnp.bfloat16),
            jax.ShapeDtypeStruct((8, 128), jnp.float32),
        ],
        scratch_shapes=[pltpu.VMEM((parts, rows, step), jnp.bfloat16)],
        compiler_params=pltpu.CompilerParams(vmem_limit_bytes=VMEM_LIMIT),
        cost_estimate=cost(
            2 * rows * parts * step * (2 * hidden + tokens),
            2 * parts * step * (2 * hidden + sources * tokens),
        ),
        name="gate_up",
    )(scales, gains, chosen, *first, *pieces, *([w_gate, w_up] * parts))


def down_kernel(hidden_ref, down_w, factor_ref, spread_ref, own_ref, other_ref):
    sources, tokens, capacity = spread_ref.shape
    terms = jnp.dot(hidden_ref[...], down_w[0], preferred_element_type=jnp.float32)
    terms = (terms * factor_ref[...]).astype(jnp.bfloat16)
    half = sources // 2
    for source in range(sources):
        spread = jnp.dot(
            spread_ref[source],
            terms[source * capacity : (source + 1) * capacity],
            preferred_element_type=jnp.float32,
        ).astype(jnp.bfloat16)
        if source < half:
            own_ref[source] = spread
        else:
            other_ref[source - half] = spread


def down(hidden_q, w_down, factor, spread, start, width):
    rows, hidden = hidden_q.shape
    sources, tokens, capacity = spread.shape
    tile = width // 2 if width % 256 == 0 else width
    whole = lambda shape: pl.BlockSpec(shape, lambda j: (0,) * len(shape))
    return pl.pallas_call(
        down_kernel,
        grid=(width // tile,),
        in_specs=[
            whole(hidden_q.shape),
            pl.BlockSpec((1, hidden, tile), lambda j: (0, 0, start // tile + j)),
            whole(factor.shape),
            whole(spread.shape),
        ],
        out_specs=[pl.BlockSpec((sources // 2, tokens, tile), lambda j: (0, 0, j))] * 2,
        out_shape=[jax.ShapeDtypeStruct((sources // 2, tokens, width), jnp.bfloat16)] * 2,
        compiler_params=pltpu.CompilerParams(vmem_limit_bytes=VMEM_LIMIT),
        cost_estimate=cost(
            2 * rows * width * (hidden + tokens), 2 * width * (hidden + sources * tokens)
        ),
        name="down",
    )(hidden_q, w_down, factor, spread)


def natural_kernel(columns, *refs):
    *parts, out_ref = refs
    for j in range(parts[0].shape[1] // columns):
        for c, part in enumerate(parts):
            place = (j * len(parts) + c) * columns
            out_ref[:, place : place + columns] = part[:, j * columns : (j + 1) * columns]


def natural(parts, columns):
    rows, step = parts[0].shape
    return pl.pallas_call(
        functools.partial(natural_kernel, columns),
        out_shape=jax.ShapeDtypeStruct((rows, step * len(parts)), parts[0].dtype),
        compiler_params=pltpu.CompilerParams(vmem_limit_bytes=VMEM_LIMIT),
        name="natural",
    )(*parts)


def add(*terms):
    return sum(t.astype(jnp.float32) for t in terms).astype(jnp.bfloat16)


def gather_plan(
    attn_out,
    out_weight,
    residual,
    norm_gain,
    expert_ids,
    route_weight,
    w_gate,
    w_up,
    w_down,
    top_x,
    top_h,
    capacity,
):
    owners, layers = lax.axis_size("dp"), lax.axis_size("tensor")
    experts = owners * layers
    local_rows, width = residual.shape
    half, step = layers // 2, width // CHUNKS
    columns = step // owners

    split = lambda value: value.reshape(-1, owners, CHUNKS, columns)
    parts = lambda value, c: split(value)[:, :, c].reshape(-1, step)
    place = lax.axis_index("dp")[None]

    def summed_over_tensor(terms, c):
        total = lax.psum_scatter(terms, "tensor", scatter_dimension=0, tiled=True)
        part = parts(residual, c).astype(jnp.float32) + total.astype(jnp.float32)
        return part, part.astype(jnp.bfloat16)

    weight_rows = list(out_weight.T.reshape(CHUNKS, columns, -1))
    near = neighbours(weight_rows[0])
    table = chip_table(expert_ids, route_weight, experts)
    near, table = tie(near, table)
    groups = [[weight_rows[0]], [near[0]], [near[1]], diagonal(*near)]
    terms = project_part(place, attn_out, [both_cores(group) for group in groups])
    terms, weight_rows[1] = tie(terms, weight_rows[1])
    near = neighbours(weight_rows[1])
    groups = [[weight_rows[1]], [near[0]], [near[1]], diagonal(*near)]
    groups = [both_cores(group) for group in groups]
    first, sent = summed_over_tensor(terms, 0)

    beside = {}

    def at_hop(hop, arrived):
        if hop == 1:
            arrived, tied, routes = tie(arrived, groups, table)
            beside["terms"] = project_part(place, attn_out, tied)
            beside["weight"] = expert_weights(routes)
        if hop == layers - 1:
            arrived, terms, weight = tie(arrived, beside["terms"], beside["weight"])
            beside["sum"], beside["weight"] = summed_over_tensor(terms, 1), weight
        return arrived

    own = along_tensor(sent, at_hop)
    along_x, along_y = neighbours(own)
    own = both_cores([own])
    weight = beside["weight"]
    second, sent = beside["sum"]
    stream = [first, second]

    named = weight > 0.0
    earlier = jnp.triu(jnp.ones((local_rows, local_rows), jnp.bfloat16), 1)
    slot = lax.dot_general(
        named.astype(jnp.bfloat16),
        earlier,
        (((2,), (0,)), ((), ())),
        preferred_element_type=jnp.float32,
    ).astype(jnp.int32)
    chosen = (
        slot[:, :, None, :] == jnp.arange(capacity, dtype=jnp.int32)[:, None]
    ) & named[:, :, None, :]
    factor = jnp.sum(jnp.where(chosen, weight[:, :, None, :], 0.0), axis=3)
    factor = list(factor.reshape(4, 2 * layers * capacity, 1) * (top_h / FP8_LIMIT))
    choice = chosen.astype(jnp.bfloat16).reshape(4, 2 * layers, capacity, local_rows)
    spread = list(choice.transpose(0, 1, 3, 2))
    choice = list(choice)
    scales = jnp.stack([top_x / FP8_LIMIT, FP8_LIMIT / top_h])

    squares = sum(jnp.sum(part * part, axis=1) for part in stream)
    root = lax.rsqrt(squares / width + 1e-06)
    gains = [parts(norm_gain, c) for c in range(CHUNKS)]
    peak_x = jnp.max(
        jnp.stack([jnp.max(jnp.abs(s * root[:, None] * g)) for s, g in zip(stream, gains)])
    )
    gains = jnp.stack(gains) * (FP8_LIMIT / top_x)

    gate_rows = w_gate.reshape(1, owners, CHUNKS, columns, -1)
    up_rows = w_up.reshape(1, owners, CHUNKS, columns, -1)

    def hidden_of(r, choice):
        rows, pieces = groups[r]
        return gate_up(scales, gains, choice[r], rows, pieces, gate_rows, up_rows)

    own, sent = tie(own, sent)

    def at_middle_hop(hop, arrived):
        nonlocal along_x, along_y, across
        if hop == 1:
            arrived, along_x, along_y = tie(arrived, along_x, along_y)
            across = diagonal(along_x, along_y)
        if hop == layers - 1:
            arrived, across = tie(arrived, across)
        return arrived

    across = []
    later = along_tensor(sent, at_middle_hop)
    first = [own, both_cores([along_x]), both_cores([along_y])]
    own = later
    first = [rows_of(choice[r], p) for r, p in enumerate(first + [both_cores(across)])]
    along_x, along_y = neighbours(own)
    groups = [(first[0], both_cores([own]))]
    hidden = [hidden_of(0, choice)]
    stream = natural(stream, columns)
    along_x, along_y, hidden[0], stream, first, choice, spread, factor = tie(
        along_x, along_y, hidden[0], stream, first, choice, spread, factor
    )
    across = diagonal(along_x, along_y)
    groups += [(first[1], both_cores([along_x])), (first[2], both_cores([along_y]))]
    hidden += [hidden_of(1, choice), hidden_of(2, choice)]
    across, hidden = tie(across, hidden)
    groups.append((first[3], both_cores(across)))

    spans = [(c * step, step) for c in range(CHUNKS)]

    def outputs(r, c):
        return down(hidden[r][0], w_down, factor[r], spread[r], *spans[c])

    def halves(kept, given):
        taken = swap(given, 1)
        return [(kept[:half], taken[:half]), (kept[half:], taken[half:])]

    summed = lambda r, c: [add(*terms) for terms in halves(*outputs(r, c))]
    to_x, to_y = summed(1, 0), summed(2, 0)
    groups[3], to_x, to_y = tie(groups[3], to_x, to_y)
    hidden.append(hidden_of(3, choice))
    peak_h = jnp.max(jnp.stack([peaks for _, peaks in hidden]))
    mixture = []
    for c in range(CHUNKS):
        early_x, early_y = swap(to_x[0], 2), swap(to_y[1], 4)
        kept, given = outputs(3, c) if c == 0 else coming[2]
        if c == 0:
            given, early_x, early_y = tie(given, early_x, early_y)
        beyond = [add(*terms) for terms in halves(kept, given)]
        if c > 0:
            beyond, early_x, early_y, mixed = tie(beyond, early_x, early_y, mixed)
            mixture.append(lax.psum_scatter(mixed, "tensor", scatter_dimension=0, tiled=True))
        over_x, over_y = swap(beyond[0], 2), swap(beyond[1], 4)
        to_own = outputs(0, c)
        if c + 1 < CHUNKS:
            coming = [outputs(r, c + 1) for r in (1, 2, 3)]
            over_x, over_y, to_own, coming = tie(over_x, over_y, to_own, coming)
        late_x, late_y = add(to_x[1], over_y), add(to_y[0], over_x)
        if c + 1 < CHUNKS:
            late_x, late_y, hidden = tie(late_x, late_y, hidden)
            to_x, to_y = ([add(*terms) for terms in halves(*pair)] for pair in coming[:2])
        to_own = halves(*to_own)
        low = add(*to_own[0], early_x, swap(late_y, 4))
        high = add(*to_own[1], swap(late_x, 2), early_y)
        mixed = jnp.concatenate([low, high]).reshape(layers * local_rows, -1)
    mixed, mixture = tie(mixed, mixture)
    mixture.append(lax.psum_scatter(mixed, "tensor", scatter_dimension=0, tiled=True))
    layer_out = stream + jnp.concatenate(mixture, axis=1).astype(jnp.float32)
    return layer_out.astype(jnp.bfloat16), peak_x, peak_h


def body(
    attn_out,
    out_weight,
    residual,
    norm_gain,
    expert_ids,
    route_weight,
    w_gate,
    w_up,
    w_down,
    history_x,
    history_h,
):
    experts = lax.axis_size("dp") * lax.axis_size("tensor")
    local_rows, top_count = expert_ids.shape
    capacity = max(2, 3 * local_rows * top_count // (2 * experts))
    top_x, top_h = jnp.max(history_x), jnp.max(history_h)
    gathers = lax.axis_size("dp") == 8 and local_rows < 4 * capacity
    plan = gather_plan if gathers else exchange_plan
    layer_out, peak_x, peak_h = plan(
        attn_out,
        out_weight,
        residual,
        norm_gain,
        expert_ids,
        route_weight,
        w_gate,
        w_up,
        w_down,
        top_x,
        top_h,
        capacity,
    )
    peaks = peaks_over_all(jnp.stack([peak_x, peak_h]))
    new_history_x = jnp.concatenate([peaks[:1], history_x[:-1]])
    new_history_h = jnp.concatenate([peaks[1:], history_h[:-1]])
    return (layer_out, new_history_x, new_history_h)


def solution(mesh):
    in_specs = (
        P("dp", "tensor"),
        P("tensor", "dp"),
        P(AXES, None),
        P(),
        P(AXES, None),
        P(AXES, None),
        P(AXES, None, None),
        P(AXES, None, None),
        P(AXES, None, None),
        P(),
        P(),
    )
    out_specs = (P(AXES, None), P(), P())
    return jax.shard_map(body, mesh=mesh, in_specs=in_specs, out_specs=out_specs, check_vma=False)
```

```python
import functools

import jax
import jax.numpy as jnp
from jax import lax
from jax.experimental import pallas as pl
from jax.experimental.pallas import tpu as pltpu
from jax.sharding import PartitionSpec as P

FP8_LIMIT = 448.0
AXES = ("dp", "tensor")
CHUNKS = 2
VMEM_LIMIT = 48 * 2**20
COST_SHARE = 16


def project(attn_out, out_weight):
    head_terms = jnp.dot(
        attn_out,
        lax.all_gather(out_weight, "dp", axis=1, tiled=True),
        preferred_element_type=jnp.float32,
    )
    return lax.psum_scatter(
        head_terms.astype(jnp.bfloat16), "tensor", scatter_dimension=0, tiled=True
    ).astype(jnp.float32)


def peaks_over_all(peaks):
    for axis in AXES:
        count = lax.axis_size(axis)
        shift = 1
        while shift < count:
            pairs = [(i, (i + shift) % count) for i in range(count)]
            peaks = jnp.maximum(peaks, lax.ppermute(peaks, axis, pairs))
            shift *= 2
    return peaks


def slots_of(ids, experts, capacity):
    flat_ids = ids.reshape(-1)
    onehot = (flat_ids[:, None] == jnp.arange(experts, dtype=jnp.int32)[None, :]).astype(jnp.int32)
    before = jnp.cumsum(onehot, axis=0) - onehot
    return flat_ids * capacity + jnp.sum(before * onehot, axis=-1)


def exchange_plan(
    attn_out,
    out_weight,
    residual,
    norm_gain,
    expert_ids,
    route_weight,
    w_gate,
    w_up,
    w_down,
    top_x,
    top_h,
    capacity,
):
    experts = lax.axis_size("dp") * lax.axis_size("tensor")
    inv_x, inv_h, scale_h = top_x / FP8_LIMIT, top_h / FP8_LIMIT, FP8_LIMIT / top_h
    local_rows, width = residual.shape
    top_count = expert_ids.shape[1]
    stream = residual.astype(jnp.float32) + project(attn_out, out_weight)
    normed = (
        stream * lax.rsqrt(jnp.mean(stream * stream, axis=-1, keepdims=True) + 1e-06) * norm_gain
    )
    quantized = jnp.clip(normed * (FP8_LIMIT / top_x), -FP8_LIMIT, FP8_LIMIT).astype(jnp.bfloat16)
    position = slots_of(expert_ids, experts, capacity)
    matches = (
        position.reshape(local_rows, top_count)[:, :, None]
        == jnp.arange(experts * capacity, dtype=jnp.int32)[None, None, :]
    )
    placing = jnp.sum(matches.astype(jnp.int32), axis=1).astype(jnp.bfloat16)
    outgoing = lax.dot_general(
        placing, quantized, (((0,), (0,)), ((), ())), preferred_element_type=jnp.float32
    )
    outgoing = outgoing.astype(jnp.bfloat16).reshape(experts, capacity, width)
    token_block = lax.all_to_all(outgoing, AXES, split_axis=0, concat_axis=0, tiled=True)
    flat_rows = token_block.reshape(-1, width)
    gate = jnp.dot(flat_rows, w_gate[0], preferred_element_type=jnp.float32) * inv_x
    upper = jnp.dot(flat_rows, w_up[0], preferred_element_type=jnp.float32) * inv_x
    hidden = jax.nn.silu(gate) * upper
    hidden_q = jnp.clip(hidden * scale_h, -FP8_LIMIT, FP8_LIMIT).astype(jnp.bfloat16)
    expert_out = (jnp.dot(hidden_q, w_down[0], preferred_element_type=jnp.float32) * inv_h).astype(
        jnp.bfloat16
    )
    returned = lax.all_to_all(
        expert_out.reshape(experts, capacity, width), AXES, split_axis=0, concat_axis=0, tiled=True
    )
    picked = returned.reshape(-1, width)[position].reshape(local_rows, top_count, width)
    mixture = jnp.sum(picked.astype(jnp.float32) * route_weight[:, :, None], axis=1)
    peaks = jnp.max(jnp.abs(normed)), jnp.max(jnp.abs(hidden))
    return (stream + mixture).astype(jnp.bfloat16), *peaks


def cost(flops, bytes_accessed):
    return pl.CostEstimate(
        flops=flops // COST_SHARE, bytes_accessed=bytes_accessed // COST_SHARE, transcendentals=0
    )


def swap(value, bits):
    count = lax.axis_size("dp")
    return lax.ppermute(value, "dp", [(i, i ^ bits) for i in range(count)])


def along_tensor(value, at_hop=None):
    count, here = lax.axis_size("tensor"), lax.axis_index("tensor")
    passed = [(value, value)]
    for hop in range(1, count):
        up = [(i, i + 1) for i in range(hop - 1, count - 1)]
        back = [(count - 1 - i, count - 1 - j) for i, j in up]
        below, above = passed[-1]
        arrived = lax.ppermute(below, "tensor", up), lax.ppermute(above, "tensor", back)
        passed.append(at_hop(hop, arrived) if at_hop else arrived)
    blocks = jnp.zeros((count,) + value.shape, value.dtype)
    blocks = lax.dynamic_update_index_in_dim(blocks, value, here, 0)
    for hop in range(1, count):
        block = jnp.where(here >= hop, passed[hop][0], passed[count - hop][1])
        blocks = lax.dynamic_update_index_in_dim(blocks, block, (here - hop) % count, 0)
    return blocks


def chip_table(expert_ids, route_weight, experts):
    names = jnp.arange(experts, dtype=jnp.int32)[:, None, None]
    table = jnp.sum(jnp.where(expert_ids[None] == names, route_weight[None], 0.0), axis=2)
    count = lax.axis_size("tensor")
    parts = [table]
    for shift in range(1, count):
        pairs = [(i, (i + shift) % count) for i in range(count)]
        parts.append(lax.ppermute(table, "tensor", pairs))
    order = (lax.axis_index("tensor") - jnp.arange(count)) % count
    table = jnp.stack(parts)[order][None]
    return jnp.concatenate([table, swap(table, 1)])


def expert_weights(table):
    for bit in (2, 4):
        table = jnp.concatenate([table, swap(table, bit)])
    mine = lax.axis_index("dp") * lax.axis_size("tensor") + lax.axis_index("tensor")
    return lax.dynamic_index_in_dim(table, mine, axis=2, keepdims=False)


def neighbours(value):
    return swap(value, 2), swap(value, 4)


def diagonal(along_x, along_y):
    half = along_x.shape[0] // 2
    return [swap(along_x[:half], 4), swap(along_y[half:], 2)]


def both_cores(group):
    return group + [swap(piece, 1) for piece in group]


def tie(*values):
    return lax.optimization_barrier(values)


def project_kernel(place_ref, attn_ref, *refs):
    out_ref, joined, stage = refs[-3:]
    pieces = refs[:-3]
    columns = pieces[0].shape[0]
    attn = attn_ref[...]
    blocks = [pieces[0], pieces[1], pieces[2], pieces[3], pieces[4], pieces[5], None, None]
    for k, block in enumerate(blocks):
        if block is None:
            low, high = pieces[2 * k - 6], pieces[2 * k - 5]
            joined[: low.shape[0]] = low[...]
            joined[low.shape[0] :] = high[...]
            block = joined
        terms = lax.dot_general(
            attn, block[...], (((1,), (1,)), ((), ())), preferred_element_type=jnp.float32
        )
        stage[place_ref[0] ^ k, :, :columns] = terms
    for j in range(stage.shape[0]):
        out_ref[:, j * columns : (j + 1) * columns] = stage[j, :, :columns].astype(out_ref.dtype)


def project_part(place, attn_out, groups):
    rows, depth = attn_out.shape
    pieces = [piece for group in groups for piece in group]
    columns = pieces[0].shape[0]
    return pl.pallas_call(
        project_kernel,
        in_specs=[pl.BlockSpec(memory_space=pltpu.SMEM)]
        + [pl.BlockSpec(memory_space=pltpu.VMEM)] * (1 + len(pieces)),
        out_specs=pl.BlockSpec(memory_space=pltpu.VMEM),
        out_shape=jax.ShapeDtypeStruct((rows, 8 * columns), jnp.bfloat16),
        scratch_shapes=[
            pltpu.VMEM((columns, depth), jnp.bfloat16),
            pltpu.VMEM((8, rows, -(-columns // 128) * 128), jnp.float32),
        ],
        compiler_params=pltpu.CompilerParams(vmem_limit_bytes=VMEM_LIMIT),
        cost_estimate=cost(16 * rows * depth * columns, 2 * depth * (rows + 8 * columns)),
        name="project",
    )(place, attn_out, *pieces)


def pick(chosen_ref, pieces):
    source = 0
    for piece in pieces:
        for i in range(piece.shape[0]):
            yield jnp.dot(chosen_ref[source], piece[i], preferred_element_type=jnp.float32)
            source += 1


def rows_kernel(chosen_ref, *refs):
    *pieces, rows_ref, squares_ref = refs
    capacity = chosen_ref.shape[1]
    for source, picked in enumerate(pick(chosen_ref, pieces)):
        span = slice(source * capacity, (source + 1) * capacity)
        rows_ref[span] = picked.astype(rows_ref.dtype)
        squares_ref[span] = jnp.sum(picked * picked, axis=1, keepdims=True)


def rows_of(chosen, pieces):
    sources, capacity, tokens = chosen.shape
    rows, step = sources * capacity, pieces[0].shape[-1]
    return pl.pallas_call(
        rows_kernel,
        out_shape=[
            jax.ShapeDtypeStruct((rows, step), jnp.bfloat16),
            jax.ShapeDtypeStruct((rows, 1), jnp.float32),
        ],
        compiler_params=pltpu.CompilerParams(vmem_limit_bytes=VMEM_LIMIT),
        cost_estimate=cost(2 * rows * step * tokens, 2 * step * sources * tokens),
        name="rows",
    )(chosen, *pieces)


def gate_up_kernel(scale_ref, gain_ref, chosen_ref, first_ref, squares_ref, *refs):
    hidden_ref, peak_ref, rows = refs[-3:]
    weights, pieces = refs[-7:-3], refs[:-7]
    capacity = chosen_ref.shape[1]
    step = rows.shape[2]

    @pl.when(pl.program_id(0) == 0)
    def _():
        for source, picked in enumerate(pick(chosen_ref, pieces)):
            span = slice(source * capacity, (source + 1) * capacity)
            squares = squares_ref[span] + jnp.sum(picked * picked, axis=1, keepdims=True)
            root = lax.rsqrt(squares / (2 * step) + 1e-06)
            for c, x in enumerate((first_ref[span].astype(jnp.float32), picked)):
                x = jnp.clip(x * root * gain_ref[c], -FP8_LIMIT, FP8_LIMIT)
                rows[c, span] = x.astype(rows.dtype)

    def product(side):
        return sum(
            jnp.dot(
                rows[c],
                weights[2 * c + side][0].reshape(step, -1),
                preferred_element_type=jnp.float32,
            )
            for c in range(2)
        )

    gate, up = product(0) * scale_ref[0], product(1) * scale_ref[0]
    hidden = gate / (1.0 + jnp.exp(-gate)) * up
    scaled = jnp.clip(hidden * scale_ref[1], -FP8_LIMIT, FP8_LIMIT)
    hidden_ref[...] = scaled.astype(hidden_ref.dtype)
    peak = jnp.broadcast_to(jnp.max(jnp.abs(hidden)), peak_ref.shape)
    first = pl.program_id(0) == 0
    peak_ref[...] = jnp.where(first, peak, jnp.maximum(peak_ref[...], peak))


def gate_up(scales, gains, chosen, first, pieces, w_gate, w_up):
    sources, capacity, tokens = chosen.shape
    parts, _, step = gains.shape
    owners, columns, hidden = w_gate.shape[1], w_gate.shape[3], w_gate.shape[-1]
    tile = min(256, hidden)
    rows = sources * capacity
    once = pl.Buffered(buffer_count=1)
    whole = lambda a: pl.BlockSpec(a.shape, lambda n: (0,) * a.ndim, pipeline_mode=once)
    weight = lambda c: pl.BlockSpec((1, owners, None, columns, tile), lambda n: (0, 0, c, 0, n))
    return pl.pallas_call(
        gate_up_kernel,
        grid=(hidden // tile,),
        in_specs=[pl.BlockSpec(memory_space=pltpu.SMEM), whole(gains), whole(chosen)]
        + [whole(a) for a in first]
        + [whole(p) for p in pieces]
        + [weight(c) for c in range(parts) for _ in range(2)],
        out_specs=[
            pl.BlockSpec((rows, tile), lambda n: (0, n)),
            pl.BlockSpec((8, 128), lambda n: (0, 0)),
        ],
        out_shape=[
            jax.ShapeDtypeStruct((rows, hidden), jnp.bfloat16),
            jax.ShapeDtypeStruct((8, 128), jnp.float32),
        ],
        scratch_shapes=[pltpu.VMEM((parts, rows, step), jnp.bfloat16)],
        compiler_params=pltpu.CompilerParams(vmem_limit_bytes=VMEM_LIMIT),
        cost_estimate=cost(
            2 * rows * parts * step * (2 * hidden + tokens),
            2 * parts * step * (2 * hidden + sources * tokens),
        ),
        name="gate_up",
    )(scales, gains, chosen, *first, *pieces, *([w_gate, w_up] * parts))


def down_kernel(hidden_ref, down_w, factor_ref, spread_ref, own_ref, other_ref):
    sources, tokens, capacity = spread_ref.shape
    terms = jnp.dot(hidden_ref[...], down_w[0], preferred_element_type=jnp.float32)
    terms = (terms * factor_ref[...]).astype(jnp.bfloat16)
    half = sources // 2
    for source in range(sources):
        spread = jnp.dot(
            spread_ref[source],
            terms[source * capacity : (source + 1) * capacity],
            preferred_element_type=jnp.float32,
        ).astype(jnp.bfloat16)
        if source < half:
            own_ref[source] = spread
        else:
            other_ref[source - half] = spread


def down(hidden_q, w_down, factor, spread, start, width):
    rows, hidden = hidden_q.shape
    sources, tokens, capacity = spread.shape
    tile = next(t for t in (1024, 512, 256, 128) if start % t == 0 and width % t == 0)
    whole = lambda shape: pl.BlockSpec(shape, lambda j: (0,) * len(shape))
    return pl.pallas_call(
        down_kernel,
        grid=(width // tile,),
        in_specs=[
            whole(hidden_q.shape),
            pl.BlockSpec((1, hidden, tile), lambda j: (0, 0, start // tile + j)),
            whole(factor.shape),
            whole(spread.shape),
        ],
        out_specs=[pl.BlockSpec((sources // 2, tokens, tile), lambda j: (0, 0, j))] * 2,
        out_shape=[jax.ShapeDtypeStruct((sources // 2, tokens, width), jnp.bfloat16)] * 2,
        compiler_params=pltpu.CompilerParams(vmem_limit_bytes=VMEM_LIMIT),
        cost_estimate=cost(
            2 * rows * width * (hidden + tokens), 2 * width * (hidden + sources * tokens)
        ),
        name="down",
    )(hidden_q, w_down, factor, spread)


def natural_kernel(columns, *refs):
    *parts, out_ref = refs
    for j in range(parts[0].shape[1] // columns):
        for c, part in enumerate(parts):
            place = (j * len(parts) + c) * columns
            out_ref[:, place : place + columns] = part[:, j * columns : (j + 1) * columns]


def natural(parts, columns):
    rows, step = parts[0].shape
    return pl.pallas_call(
        functools.partial(natural_kernel, columns),
        out_shape=jax.ShapeDtypeStruct((rows, step * len(parts)), parts[0].dtype),
        compiler_params=pltpu.CompilerParams(vmem_limit_bytes=VMEM_LIMIT),
        name="natural",
    )(*parts)


def add(*terms):
    return sum(t.astype(jnp.float32) for t in terms).astype(jnp.bfloat16)


def gather_plan(
    attn_out,
    out_weight,
    residual,
    norm_gain,
    expert_ids,
    route_weight,
    w_gate,
    w_up,
    w_down,
    top_x,
    top_h,
    capacity,
):
    owners, layers = lax.axis_size("dp"), lax.axis_size("tensor")
    experts = owners * layers
    local_rows, width = residual.shape
    half, step = layers // 2, width // CHUNKS
    columns = step // owners

    split = lambda value: value.reshape(-1, owners, CHUNKS, columns)
    parts = lambda value, c: split(value)[:, :, c].reshape(-1, step)
    place = lax.axis_index("dp")[None]

    def summed_over_tensor(terms, c):
        total = lax.psum_scatter(terms, "tensor", scatter_dimension=0, tiled=True)
        part = parts(residual, c).astype(jnp.float32) + total.astype(jnp.float32)
        return part, part.astype(jnp.bfloat16)

    weight_rows = list(out_weight.T.reshape(CHUNKS, columns, -1))
    near = neighbours(weight_rows[0])
    table = chip_table(expert_ids, route_weight, experts)
    near, table = tie(near, table)
    groups = [[weight_rows[0]], [near[0]], [near[1]], diagonal(*near)]
    terms = project_part(place, attn_out, [both_cores(group) for group in groups])
    terms, weight_rows[1] = tie(terms, weight_rows[1])
    near = neighbours(weight_rows[1])
    groups = [[weight_rows[1]], [near[0]], [near[1]], diagonal(*near)]
    groups = [both_cores(group) for group in groups]
    first, sent = summed_over_tensor(terms, 0)

    beside = {}

    def at_hop(hop, arrived):
        if hop == 1:
            arrived, tied, routes = tie(arrived, groups, table)
            beside["terms"] = project_part(place, attn_out, tied)
            beside["weight"] = expert_weights(routes)
        if hop == layers - 1:
            arrived, terms, weight = tie(arrived, beside["terms"], beside["weight"])
            beside["sum"], beside["weight"] = summed_over_tensor(terms, 1), weight
        return arrived

    own = along_tensor(sent, at_hop)
    along_x, along_y = neighbours(own)
    own = both_cores([own])
    weight = beside["weight"]
    second, sent = beside["sum"]
    stream = [first, second]

    named = weight > 0.0
    earlier = jnp.triu(jnp.ones((local_rows, local_rows), jnp.bfloat16), 1)
    slot = lax.dot_general(
        named.astype(jnp.bfloat16),
        earlier,
        (((2,), (0,)), ((), ())),
        preferred_element_type=jnp.float32,
    ).astype(jnp.int32)
    chosen = (
        slot[:, :, None, :] == jnp.arange(capacity, dtype=jnp.int32)[:, None]
    ) & named[:, :, None, :]
    factor = jnp.sum(jnp.where(chosen, weight[:, :, None, :], 0.0), axis=3)
    factor = list(factor.reshape(4, 2 * layers * capacity, 1) * (top_h / FP8_LIMIT))
    choice = chosen.astype(jnp.bfloat16).reshape(4, 2 * layers, capacity, local_rows)
    spread = list(choice.transpose(0, 1, 3, 2))
    choice = list(choice)
    scales = jnp.stack([top_x / FP8_LIMIT, FP8_LIMIT / top_h])

    squares = sum(jnp.sum(part * part, axis=1) for part in stream)
    root = lax.rsqrt(squares / width + 1e-06)
    gains = [parts(norm_gain, c) for c in range(CHUNKS)]
    peak_x = jnp.max(
        jnp.stack([jnp.max(jnp.abs(s * root[:, None] * g)) for s, g in zip(stream, gains)])
    )
    gains = jnp.stack(gains) * (FP8_LIMIT / top_x)

    gate_rows = w_gate.reshape(1, owners, CHUNKS, columns, -1)
    up_rows = w_up.reshape(1, owners, CHUNKS, columns, -1)

    def hidden_of(r, choice):
        rows, pieces = groups[r]
        return gate_up(scales, gains, choice[r], rows, pieces, gate_rows, up_rows)

    own, sent = tie(own, sent)

    def at_middle_hop(hop, arrived):
        nonlocal along_x, along_y, across
        if hop == 1:
            arrived, along_x, along_y = tie(arrived, along_x, along_y)
            across = diagonal(along_x, along_y)
        if hop == layers - 1:
            arrived, across = tie(arrived, across)
        return arrived

    across = []
    later = along_tensor(sent, at_middle_hop)
    first = [own, both_cores([along_x]), both_cores([along_y])]
    own = later
    first = [rows_of(choice[r], p) for r, p in enumerate(first + [both_cores(across)])]
    along_x, along_y = neighbours(own)
    groups = [(first[0], both_cores([own]))]
    hidden = [hidden_of(0, choice)]
    stream = natural(stream, columns)
    along_x, along_y, hidden[0], stream, first, choice, spread, factor = tie(
        along_x, along_y, hidden[0], stream, first, choice, spread, factor
    )
    across = diagonal(along_x, along_y)
    groups += [(first[1], both_cores([along_x])), (first[2], both_cores([along_y]))]
    hidden += [hidden_of(1, choice), hidden_of(2, choice)]
    across, hidden = tie(across, hidden)
    groups.append((first[3], both_cores(across)))

    unit = 512 if width % 512 == 0 else 128
    cut = (width // unit + 1) // 2 * unit
    spans = [(0, cut), (cut, width - cut)]

    def outputs(r, c):
        return down(hidden[r][0], w_down, factor[r], spread[r], *spans[c])

    def halves(kept, given):
        taken = swap(given, 1)
        return [(kept[:half], taken[:half]), (kept[half:], taken[half:])]

    summed = lambda r, c: [add(*terms) for terms in halves(*outputs(r, c))]
    to_x, to_y = summed(1, 0), summed(2, 0)
    groups[3], to_x, to_y = tie(groups[3], to_x, to_y)
    hidden.append(hidden_of(3, choice))
    peak_h = jnp.max(jnp.stack([peaks for _, peaks in hidden]))
    mixture = []
    for c in range(CHUNKS):
        early_x, early_y = swap(to_x[0], 2), swap(to_y[1], 4)
        kept, given = outputs(3, c) if c == 0 else coming[2]
        if c == 0:
            given, early_x, early_y = tie(given, early_x, early_y)
        beyond = [add(*terms) for terms in halves(kept, given)]
        if c > 0:
            beyond, early_x, early_y, mixed = tie(beyond, early_x, early_y, mixed)
            mixture.append(lax.psum_scatter(mixed, "tensor", scatter_dimension=0, tiled=True))
        over_x, over_y = swap(beyond[0], 2), swap(beyond[1], 4)
        to_own = outputs(0, c)
        if c + 1 < CHUNKS:
            coming = [outputs(r, c + 1) for r in (1, 2, 3)]
            over_x, over_y, to_own, coming = tie(over_x, over_y, to_own, coming)
        late_x, late_y = add(to_x[1], over_y), add(to_y[0], over_x)
        if c + 1 < CHUNKS:
            late_x, late_y, hidden = tie(late_x, late_y, hidden)
            to_x, to_y = ([add(*terms) for terms in halves(*pair)] for pair in coming[:2])
        to_own = halves(*to_own)
        low = add(*to_own[0], early_x, swap(late_y, 4))
        high = add(*to_own[1], swap(late_x, 2), early_y)
        mixed = jnp.concatenate([low, high]).reshape(layers * local_rows, -1)
    mixed, mixture = tie(mixed, mixture)
    mixture.append(lax.psum_scatter(mixed, "tensor", scatter_dimension=0, tiled=True))
    layer_out = stream + jnp.concatenate(mixture, axis=1).astype(jnp.float32)
    return layer_out.astype(jnp.bfloat16), peak_x, peak_h


def body(
    attn_out,
    out_weight,
    residual,
    norm_gain,
    expert_ids,
    route_weight,
    w_gate,
    w_up,
    w_down,
    history_x,
    history_h,
):
    experts = lax.axis_size("dp") * lax.axis_size("tensor")
    local_rows, top_count = expert_ids.shape
    capacity = max(2, 3 * local_rows * top_count // (2 * experts))
    top_x, top_h = jnp.max(history_x), jnp.max(history_h)
    gathers = lax.axis_size("dp") == 8 and local_rows < 4 * capacity
    plan = gather_plan if gathers else exchange_plan
    layer_out, peak_x, peak_h = plan(
        attn_out,
        out_weight,
        residual,
        norm_gain,
        expert_ids,
        route_weight,
        w_gate,
        w_up,
        w_down,
        top_x,
        top_h,
        capacity,
    )
    peaks = peaks_over_all(jnp.stack([peak_x, peak_h]))
    new_history_x = jnp.concatenate([peaks[:1], history_x[:-1]])
    new_history_h = jnp.concatenate([peaks[1:], history_h[:-1]])
    return (layer_out, new_history_x, new_history_h)


def solution(mesh):
    in_specs = (
        P("dp", "tensor"),
        P("tensor", "dp"),
        P(AXES, None),
        P(),
        P(AXES, None),
        P(AXES, None),
        P(AXES, None, None),
        P(AXES, None, None),
        P(AXES, None, None),
        P(),
        P(),
    )
    out_specs = (P(AXES, None), P(), P())
    return jax.shard_map(body, mesh=mesh, in_specs=in_specs, out_specs=out_specs, check_vma=False)
```
